128 devices in a mesh: seq: 8 (over z, x_hi), fsdp: 16 (over y, x_lo, core).
Axes of the slice: x: 4 (x_hi: 2, x_lo: 2; x = x_hi * 2 + x_lo), y: 4, z: 4, core: 2. Of those that a mesh axis runs over, the one named last changes fastest.
Arguments:
- tokens: bfloat16 [16, 1024, 1024], P('fsdp', 'seq'), may hold values from -6 to 6
- segments: int32 [16, 1024], P('fsdp'), may hold values from 0 to 3, as said below
- norm_input: bfloat16 [1024], P('fsdp'), may hold values from 0.25 to 1.75
- w_query: bfloat16 [1024, 2048], P('fsdp'), may hold values from -0.1875 to 0.1875
- w_key: bfloat16 [1024, 1024], P('fsdp'), may hold values from -0.1875 to 0.1875
- w_value: bfloat16 [1024, 1024], P('fsdp'), may hold values from -0.1875 to 0.1875
- norm_query: bfloat16 [128], P('fsdp'), may hold values from 0.25 to 1.75
- norm_key: bfloat16 [128], P('fsdp'), may hold values from 0.25 to 1.75
- w_output: bfloat16 [2048, 1024], P(None, 'fsdp'), may hold values from -1 to 1
- norm_post: bfloat16 [1024], P('fsdp'), may hold values from 0.25 to 1.75
- w_gate: bfloat16 [1024, 3072], P('fsdp'), may hold values from -0.1875 to 0.1875
- w_up: bfloat16 [1024, 3072], P('fsdp'), may hold values from -0.1875 to 0.1875
- w_down: bfloat16 [3072, 1024], P(None, 'fsdp'), may hold values from -0.109375 to 0.109375
- cotangent: bfloat16 [16, 1024, 1024], P('fsdp', 'seq'), may hold values from -6 to 6
Outputs:
- output: bfloat16 [16, 1024, 1024], P('fsdp', 'seq')
- grad_tokens: float32 [16, 1024, 1024], P('fsdp', 'seq')
- grad_norm_input: float32 [1024], P('fsdp')
- grad_query: float32 [1024, 2048], P('fsdp')
- grad_key: float32 [1024, 1024], P('fsdp')
- grad_value: float32 [1024, 1024], P('fsdp')
- grad_norm_query: float32 [128], P('fsdp')
- grad_norm_key: float32 [128], P('fsdp')
- grad_output: float32 [2048, 1024], P(None, 'fsdp')
- grad_norm_post: float32 [1024], P('fsdp')
- grad_gate: float32 [1024, 3072], P('fsdp')
- grad_up: float32 [1024, 3072], P('fsdp')
- grad_down: float32 [3072, 1024], P(None, 'fsdp')
The draws below stay inside these ranges and needn't reach their ends.
Inputs may be any that keep to these rules, and one draw needn't show every extreme that they name: `segments`: ids never fall along a sequence; tokens of one sequence with equal ids belong to one document.
All inputs are finite; a program needn't handle non-finite values.
Results may differ from the reference program's by a relative error of at most 0.025.
Values may be sent and summed in bfloat16 or wider, within the bound.
No kernel may reach another device: no remote copies, remote signals or barrier semaphores. Data moves between devices by JAX's collectives and lax.ppermute only.
A program may use at most 192 MiB of HBM per device.

```python
import math
import jax
import jax.numpy as jnp
from jax import lax

D = 1024
HEADS = 16
KV_HEADS = 8
HEAD = 128
FF = 3072
SEQ_LEN = 1024
QBLOCK = 512
Q_WIDTH = 2048
KV_WIDTH = 1024
SEQS = 16
N_SEQ = 8


def draw_segments(key, part):
    key = jax.random.fold_in(key, 11)
    local_rows = SEQ_LEN // N_SEQ
    reach = max(local_rows // 2, 1)
    keys = jax.random.split(key, 3)
    begin = jax.random.randint(keys[0], (SEQS, 1), 1, reach + 1)
    finish = SEQ_LEN - jax.random.randint(keys[1], (SEQS, 1), 1, reach + 1)
    early = jax.random.randint(keys[2], (SEQS, 1), 0, begin)
    places = jnp.arange(SEQ_LEN, dtype=jnp.int32)[None, :]
    ids = (places >= early).astype(jnp.int32) + (places >= begin).astype(jnp.int32) + (places >= finish).astype(jnp.int32)
    return ids.astype(jnp.int32)


def steps_of(key, extent, pieces, low, high):
    def one(dim, parts):
        heights = jax.random.uniform(jax.random.fold_in(jax.random.fold_in(key, 6), dim), (parts,), jnp.float32, low / len(pieces), high / len(pieces))
        return jnp.repeat(jnp.exp(heights), extent[dim] // parts).reshape((-1,) + (1,) * (len(extent) - dim - 1))

    loudness = one(*pieces[0])
    for cut in pieces[1:]:
        loudness = loudness * one(*cut)
    return loudness


def noise(rng, dims, spread, bound, shards=(), held_as=jnp.bfloat16):
    factor_of = steps_of(rng, dims, shards, -0.22, 0.18) if shards else 1.0
    array = jax.random.normal(rng, dims, jnp.float32) * spread * factor_of
    return jnp.minimum(jnp.maximum(array, -bound), bound).astype(held_as)


def setup_inputs(seed: int = 0) -> dict:
    key_list = jax.random.split(jax.random.key(seed), 15)
    tokens = noise(key_list[0], (SEQS, SEQ_LEN, D), 1.0, 6.0, ((0, 16), (1, 8)))
    segments = draw_segments(jax.random.fold_in(key_list[14], 71), 0)
    norm_input = jnp.clip(1.0 + 0.15 * jax.random.normal(key_list[2], (D,), jnp.float32), 0.25, 1.75).astype(jnp.bfloat16)
    w_query = noise(key_list[3], (D, Q_WIDTH), D ** -0.5, 0.1875, ((0, 16),))
    w_key = noise(key_list[4], (D, KV_WIDTH), D ** -0.5, 0.1875, ((0, 16),))
    w_value = noise(key_list[5], (D, KV_WIDTH), D ** -0.5, 0.1875, ((0, 16),))
    norm_query = jnp.clip(1.0 + 0.15 * jax.random.normal(key_list[6], (HEAD,), jnp.float32), 0.25, 1.75).astype(jnp.bfloat16)
    norm_key = jnp.clip(1.0 + 0.15 * jax.random.normal(key_list[7], (HEAD,), jnp.float32), 0.25, 1.75).astype(jnp.bfloat16)
    w_output = noise(key_list[8], (Q_WIDTH, D), (Q_WIDTH // 64) ** -0.5, 1.0, ((1, 16),))
    norm_post = jnp.clip(1.0 + 0.15 * jax.random.normal(key_list[9], (D,), jnp.float32), 0.25, 1.75).astype(jnp.bfloat16)
    w_gate = noise(key_list[10], (D, FF), D ** -0.5, 0.1875, ((0, 16),))
    w_up = noise(key_list[11], (D, FF), D ** -0.5, 0.1875, ((0, 16),))
    w_down = noise(key_list[12], (FF, D), FF ** -0.5, 0.109375, ((1, 16),))
    cotangent = noise(key_list[13], (SEQS, SEQ_LEN, D), 1.0, 6.0, ((0, 16), (1, 8)))
    return {"tokens": tokens, "segments": segments, "norm_input": norm_input, "w_query": w_query, "w_key": w_key, "w_value": w_value, "norm_query": norm_query, "norm_key": norm_key, "w_output": w_output, "norm_post": norm_post, "w_gate": w_gate, "w_up": w_up, "w_down": w_down, "cotangent": cotangent}


EPSILON = 1e-06
THETA = 1000000.0
NEGATIVE = -1e+30
HIGHEST_PRECISION = lax.Precision.HIGHEST

@jax.custom_vjp
def low(v):
    return lax.optimization_barrier(v.astype(jnp.bfloat16)).astype(jnp.float32)

@jax.custom_vjp
def low_back(v):
    return v

def low_keep(v):
    return (low(v), None)

def low_pass(kept, grad):
    return (grad,)

def back_keep(v):
    return (v, None)

def back_low(kept, grad):
    return (low(grad),)
low.defvjp(low_keep, low_pass)
low_back.defvjp(back_keep, back_low)

def normalize(values, gain):
    return values * lax.rsqrt(lax.optimization_barrier(jnp.mean(values * values, axis=-1, keepdims=True)) + EPSILON) * gain

def rotation(positions):
    exponent = jnp.arange(0, HEAD, 2, dtype=jnp.float32) / HEAD
    frequency = jnp.power(jnp.float32(THETA), -exponent)
    angles = positions.astype(jnp.float32)[:, None] * frequency[None, :]
    angles = jnp.concatenate([angles, angles], axis=-1)
    return (jnp.cos(angles)[:, None, :], jnp.sin(angles)[:, None, :])

def rotate(values, cosine, sine):
    half = values.shape[-1] // 2
    turned = jnp.concatenate([-values[..., half:], values[..., :half]], axis=-1)
    return values * cosine + turned * sine

def attend(query, key_rot, values_low, doc_ids):
    length = query.shape[0]
    grouped = HEADS // KV_HEADS
    scale = 1.0 / math.sqrt(HEAD)
    query_grouped = query.reshape(length, KV_HEADS, grouped, HEAD)
    columns = jnp.arange(length, dtype=jnp.int32)

    def block(begin):
        rows_query = lax.dynamic_slice_in_dim(query_grouped, begin, QBLOCK, 0)
        rows_ids = lax.dynamic_slice_in_dim(doc_ids, begin, QBLOCK, 0)
        positions = begin + jnp.arange(QBLOCK, dtype=jnp.int32)
        allowed = (positions[:, None] >= columns[None, :]) & (rows_ids[:, None] == doc_ids[None, :])
        raw = jnp.einsum('qhgd,khd->hgqk', rows_query, key_rot, precision=HIGHEST_PRECISION) * scale
        score = jnp.where(allowed, low_back(raw), NEGATIVE)
        highest = lax.optimization_barrier(jnp.max(score, axis=-1, keepdims=True))
        expo_term = jnp.exp(score - highest)
        prob = expo_term / lax.optimization_barrier(jnp.sum(expo_term, axis=-1, keepdims=True))
        return jnp.einsum('hgqk,khd->qhgd', low(prob), values_low, precision=HIGHEST_PRECISION)
    starts = jnp.arange(length // QBLOCK, dtype=jnp.int32) * QBLOCK
    blocks = lax.map(jax.checkpoint(block), starts)
    return blocks.reshape(length, HEADS * HEAD)

def layer(widened, norm_input, w_query, w_key, w_value, norm_query, norm_key, w_output, norm_post, w_gate, w_up, w_down, doc_ids):
    length = widened.shape[0]
    cosine, sine = rotation(jnp.arange(length, dtype=jnp.int32))
    normed = low(normalize(widened, norm_input))
    query_raw = low_back(jnp.dot(normed, w_query, precision=HIGHEST_PRECISION)).reshape(length, HEADS, HEAD)
    key_raw = low_back(jnp.dot(normed, w_key, precision=HIGHEST_PRECISION)).reshape(length, KV_HEADS, HEAD)
    values_low = low_back(low(jnp.dot(normed, w_value, precision=HIGHEST_PRECISION))).reshape(length, KV_HEADS, HEAD)
    query = low_back(low(rotate(normalize(query_raw, norm_query), cosine, sine)))
    key_rot = low_back(low(rotate(normalize(key_raw, norm_key), cosine, sine)))
    mixed = low_back(low(attend(query, key_rot, values_low, doc_ids)))
    hidden = widened + low_back(jnp.dot(mixed, w_output, precision=HIGHEST_PRECISION))
    normed_post = low(normalize(hidden, norm_post))
    gate = low_back(jnp.dot(normed_post, w_gate, precision=HIGHEST_PRECISION))
    up_part = low_back(jnp.dot(normed_post, w_up, precision=HIGHEST_PRECISION))
    inner = low(gate * jax.nn.sigmoid(gate) * up_part)
    return hidden + low_back(jnp.dot(inner, w_down, precision=HIGHEST_PRECISION))

def reference(tokens, segments, norm_input, w_query, w_key, w_value, norm_query, norm_key, w_output, norm_post, w_gate, w_up, w_down, cotangent):
    params = tuple((p.astype(jnp.float32) for p in (norm_input, w_query, w_key, w_value, norm_query, norm_key, w_output, norm_post, w_gate, w_up, w_down)))

    def one_sequence(totals, item):
        sequence, doc_ids, incoming = item

        def forward(widened, *weights):
            return layer(widened, *weights, doc_ids)
        result, pull = jax.vjp(forward, sequence.astype(jnp.float32), *params)
        grads = pull(incoming.astype(jnp.float32))
        totals = tuple((a + b for a, b in zip(totals, grads[1:])))
        return (totals, (result.astype(jnp.bfloat16), grads[0]))
    zeros = tuple((jnp.zeros_like(p) for p in params))
    totals, (outputs, input_grads) = lax.scan(one_sequence, zeros, (tokens, segments, cotangent))
    return (outputs, input_grads, totals[0], totals[1], totals[2], totals[3], totals[4], totals[5], totals[6], totals[7], totals[8], totals[9], totals[10])
```

```python
import functools
import math

import jax
import jax.numpy as jnp
import numpy as np
from jax import lax
from jax.experimental import pallas as pl
from jax.experimental.pallas import tpu as pltpu
from jax.sharding import PartitionSpec as P

HEAD = 128
D = 1024
FF = 3072
LENGTH = 1024
ROWS = 128
N_SEQ = 8
N_FSDP = 16
Z = 4
OWN = D // N_FSDP
FF_Z = FF // Z
UNIT = 512
BLOCK = 256
EXTRA = 16
SHARE = 2 * UNIT + HEAD
MEGA = 1 << 20
GRANT = 60

EPSILON = 1e-06
THETA = 1000000.0
NEGATIVE = -1e30
SCALE = 1.0 / math.sqrt(HEAD)

PIECES = (
    (0, 0, 0, 0),
    (1, 0, 1, 0),
    (2, 0, 3, 0),
    (2, 1, 2, 0),
    (3, 0, 0, 1),
    (4, 0, 3, 1),
    (5, 0, 1, 1),
    (5, 1, 2, 1),
)
KEPT = ((0, 0), (1, 0), (0, 1), (3, 1))


def exchange(values, axis, bits):
    size = N_SEQ if axis == "seq" else N_FSDP
    return lax.ppermute(values, axis, [(i, i ^ bits) for i in range(size)])


swap_x_hi = functools.partial(exchange, axis="seq", bits=1)
swap_z_a = functools.partial(exchange, axis="seq", bits=2)
swap_z_b = functools.partial(exchange, axis="seq", bits=6)
swap_core = functools.partial(exchange, axis="fsdp", bits=1)
swap_x_lo = functools.partial(exchange, axis="fsdp", bits=2)
swap_chip = functools.partial(exchange, axis="fsdp", bits=3)
swap_y_a = functools.partial(exchange, axis="fsdp", bits=4)
swap_y_b = functools.partial(exchange, axis="fsdp", bits=12)


def after(values, *others):
    return lax.optimization_barrier((values, *others))[0]


def gather4(zero, one, swap_a, swap_b):
    zero_1 = swap_a(zero)
    one_1 = swap_b(one)
    zero_2 = swap_b(jnp.concatenate([zero, zero_1], axis=0))
    one_2 = swap_a(jnp.concatenate([one, one_1], axis=0))
    return zero, zero_1, zero_2, one, one_1, one_2


def halves(rows):
    middle = rows.shape[0] // 2
    return rows[:middle], rows[middle:]


def scatter4(first_0, first_1, block, swap_a, swap_b, between=None):
    got_0, got_1 = swap_b(first_0), swap_a(first_1)
    if between is not None:
        got_0, got_1 = after((got_0, got_1), between)
    n = got_0.shape[0] // 2
    last_0 = swap_a((block(1, 0) + got_0[n:].astype(jnp.float32)).astype(jnp.bfloat16))
    last_1 = swap_b((block(3, 1) + got_1[n:].astype(jnp.float32)).astype(jnp.bfloat16))
    return got_0, got_1, last_0, last_1


def total4(block, got_0, got_1, last_0, last_1):
    n = got_0.shape[0] // 2
    mine_0 = block(0, 0) + got_0[:n].astype(jnp.float32) + last_0.astype(jnp.float32)
    mine_1 = block(0, 1) + got_1[:n].astype(jnp.float32) + last_1.astype(jnp.float32)
    return mine_0, mine_1


def rotation():
    frequency = THETA ** -(np.arange(0, HEAD, 2, dtype=np.float64) / HEAD)
    angles = np.arange(LENGTH, dtype=np.float64)[:, None] * frequency[None, :]
    return jnp.asarray(np.concatenate([np.cos(angles), np.sin(angles)], axis=1).astype(np.float32))


def turns(table):
    turned = pltpu.roll(table, HEAD // 2, 1)
    low = lax.broadcasted_iota(jnp.int32, table.shape, 1) < HEAD // 2
    return jnp.where(low, table, turned), jnp.where(low, -turned, table)


def contract(left, right):
    return lax.dot_general(
        left, right, (((1,), (1,)), ((), ())), preferred_element_type=jnp.float32
    )


def outer_rows(left, right):
    return lax.dot_general(
        left, right, (((0,), (0,)), ((), ())), preferred_element_type=jnp.float32
    )


def product(left, right):
    return jnp.dot(left, right, preferred_element_type=jnp.float32)


def inverse_norm(values):
    return lax.rsqrt(jnp.mean(values * values, axis=-1, keepdims=True) + EPSILON)


def allowed_scores(scores, first_key, begin):
    first = first_key[:, begin : begin + BLOCK]
    place = (BLOCK, BLOCK)
    key, query = lax.broadcasted_iota(jnp.int32, place, 0), lax.broadcasted_iota(jnp.int32, place, 1)
    diagonal = jnp.where((key <= query) & (key + begin >= first), scores[begin:], NEGATIVE)
    if begin == 0:
        return [(0, diagonal)]
    key = lax.broadcasted_iota(jnp.int32, (begin, BLOCK), 0)
    return [(0, jnp.where(key >= first, scores[:begin], NEGATIVE)), (begin, diagonal)]


def front_kernel(
    at, x0, x1, x2, x3, x4, x5, w0, w1, w2, w3, w4, w5, first_key, table,
    normed, raw, heads, mixed, turned, log_total, gains, weight, value_t,
):
    z, x_hi, y, x_lo, core = at[0], at[1], at[2], at[3], at[4]
    weights, tokens = (w0, w1, w2, w3, w4, w5), (x0, x1, x2, x3, x4, x5)
    extra = jnp.zeros((EXTRA, UNIT), jnp.float32)
    for array, step, relative, color in PIECES:
        for other in range(2):
            first = (2 * step + other) * (OWN + EXTRA)
            owner = 4 * (y ^ relative) + 2 * (x_lo ^ color) + (core ^ other)
            weight[pl.ds(pl.multiple_of(owner * OWN, OWN), OWN), :] = weights[array][
                first : first + OWN, :
            ]
            extra += weights[array][first + OWN : first + OWN + EXTRA, :].astype(jnp.float32)
    gain = jnp.concatenate([extra[0:1], extra[1:2]], axis=1)
    gains[...] = jnp.zeros(gains.shape, jnp.float32)
    gains[0:1, :] = gain
    gains[1:2, :] = jnp.concatenate([extra[2:3], extra[3:4]], axis=1)
    gains[2:3, 0:UNIT] = extra[4:5]
    for array, step, relative, color in PIECES:
        values = tokens[array][step * ROWS : (step + 1) * ROWS, :].astype(jnp.float32)
        place = (2 * (z ^ relative) + (x_hi ^ color)) * ROWS
        normed[pl.ds(pl.multiple_of(place, ROWS), ROWS), :] = (
            values * inverse_norm(values) * gain
        ).astype(jnp.bfloat16)
    normed.send()
    weight.send()
    gain_query, gain_key = extra[4:5, :HEAD], extra[4:5, HEAD : 2 * HEAD]
    for begin in range(0, LENGTH, BLOCK):
        rows = slice(begin, begin + BLOCK)
        projected = product(normed[rows, :], weight[...])
        cosine, sine = turns(table[rows, :])
        raw[rows, :] = projected[:, : 3 * HEAD]
        for head, head_gain in enumerate((gain_query, gain_query, gain_key)):
            part = projected[:, head * HEAD : (head + 1) * HEAD]
            part = part * inverse_norm(part) * head_gain
            part = part * cosine + pltpu.roll(part, HEAD // 2, 1) * sine
            heads[rows, head * HEAD : (head + 1) * HEAD] = part.astype(jnp.bfloat16)
        value = projected[:, 3 * HEAD :]
        heads[rows, 3 * HEAD :] = value.astype(jnp.bfloat16)
        value_t[:, rows] = value.T.astype(jnp.bfloat16)
    raw.send()
    heads.send()
    key = slice(2 * HEAD, 3 * HEAD)
    for begin in range(0, LENGTH, BLOCK):
        rows, end = slice(begin, begin + BLOCK), begin + BLOCK
        for head in range(2):
            columns = slice(head * HEAD, (head + 1) * HEAD)
            scores = contract(heads[:end, key], heads[rows, columns]) * SCALE
            parts = allowed_scores(scores, first_key, begin)
            highest = functools.reduce(
                jnp.maximum, [jnp.max(s, axis=0, keepdims=True) for _, s in parts]
            )
            total, result = 0.0, 0.0
            for first, s in parts:
                weights_now = jnp.exp(s - highest)
                total += jnp.sum(weights_now, axis=0, keepdims=True)
                result += product(
                    value_t[:, first : first + s.shape[0]], weights_now.astype(jnp.bfloat16)
                )
            log_total[head : head + 1, rows] = highest + jnp.log(total)
            result = (result / total).T.astype(jnp.bfloat16)
            mixed[rows, columns] = result
            for part in range(2):
                turned[part ^ x_hi, (begin // BLOCK) ^ z, :, columns] = result[
                    part * ROWS : (part + 1) * ROWS
                ]


def back_kernel(
    at, raw, heads, log_total, grad, first_key, table, gains, weight,
    back, gain_grads, first_0, first_1, keep, key_t, key_sum, value_sum, query_sum, turned,
):
    key, value = slice(2 * HEAD, 3 * HEAD), slice(3 * HEAD, 4 * HEAD)
    key_t[...] = heads[:, key].astype(jnp.float32).T.astype(jnp.bfloat16)
    key_sum[...] = jnp.zeros_like(key_sum)
    value_sum[...] = jnp.zeros_like(value_sum)
    for begin in range(0, LENGTH, BLOCK):
        rows, end = slice(begin, begin + BLOCK), begin + BLOCK
        for head in range(2):
            columns = slice(head * HEAD, (head + 1) * HEAD)
            query, rows_grad = heads[rows, columns], grad[rows, columns]
            scores = contract(heads[:end, key], query) * SCALE
            prob_grad = contract(heads[:end, value], rows_grad)
            log_now = log_total[head : head + 1, rows]
            parts, mean = [], 0.0
            for first, s in allowed_scores(scores, first_key, begin):
                prob = jnp.exp(s - log_now)
                pulled = prob_grad[first : first + s.shape[0]]
                mean += jnp.sum(prob * pulled, axis=0, keepdims=True)
                parts.append((first, prob, pulled))
            query_part = 0.0
            for first, prob, pulled in parts:
                keys = slice(first, first + prob.shape[0])
                score_grad = (prob * (pulled - mean)).astype(jnp.bfloat16)
                value_sum[keys, :] += product(prob.astype(jnp.bfloat16), rows_grad)
                key_sum[keys, :] += product(score_grad, query)
                query_part += product(key_t[:, keys], score_grad)
            query_sum[rows, columns] = query_part.T
    back[:, value] = value_sum[...].astype(jnp.bfloat16)
    gain_grads[...] = jnp.zeros(gain_grads.shape, jnp.float32)
    for head in range(3):
        columns = slice(head * HEAD, (head + 1) * HEAD)
        which = 0 if head < 2 else 1
        gain = gains[2:3, which * HEAD : (which + 1) * HEAD]
        for begin in range(0, LENGTH, BLOCK):
            rows = slice(begin, begin + BLOCK)
            cosine, sine = turns(table[rows, :])
            pulled = (query_sum[rows, columns] if head < 2 else key_sum[rows, :]) * SCALE
            pulled = pulled.astype(jnp.bfloat16).astype(jnp.float32)
            pulled = pulled * cosine - pltpu.roll(pulled, HEAD // 2, 1) * sine
            part = raw[rows, columns]
            inverse = inverse_norm(part)
            unit = part * inverse
            gain_grads[which : which + 1, :] += jnp.sum(pulled * unit, axis=0, keepdims=True)
            pulled = pulled * gain
            mean = jnp.mean(unit * pulled, axis=-1, keepdims=True)
            back[rows, columns] = (inverse * (pulled - unit * mean)).astype(jnp.bfloat16)

    back.send()
    z, x_hi = at[0], at[1]
    for relative in range(Z):
        for color in range(2):
            place = (2 * (z ^ relative) + (x_hi ^ color)) * ROWS
            begin = (2 * relative + color) * ROWS
            turned[begin : begin + ROWS, :] = back[pl.ds(pl.multiple_of(place, ROWS), ROWS), :]
    send_order(contract(turned[...], weight[...]), first_0, first_1, keep)


def grad_kernel(
    at, normed, back, gain_grads, p0, p1, p2, p3, p4, p5, mixed_mine, mixed_other,
    mine, theirs, share, proj, mixed, done,
):
    y, x_lo, core = at[2], at[3], at[4]
    ordered((p0, p1, p2, p3, p4, p5), proj)
    mixed[:, : 2 * HEAD] = mixed_mine[...]
    mixed[:, 2 * HEAD :] = mixed_other[...]
    lane = lax.broadcasted_iota(jnp.int32, (OWN, HEAD), 1)
    line = lax.broadcasted_iota(jnp.int32, (OWN, HEAD), 0)
    each = HEAD // N_FSDP
    for begin in range(0, D, BLOCK):
        goal = slice(begin, begin + BLOCK)
        attn = outer_rows(normed[:, goal], back[...]).astype(jnp.bfloat16)
        output = outer_rows(proj[:, goal], mixed[...]).astype(jnp.bfloat16)
        for part in range(BLOCK // OWN):
            owner = begin // OWN + part
            query_gain = pltpu.roll(gain_grads[0:1, :], (HEAD - each * owner) % HEAD, 1)
            key_gain = pltpu.roll(gain_grads[1:2, :], (HEAD + each - each * owner) % HEAD, 1)
            head_gains = jnp.where(lane < each, query_gain, key_gain)
            head_gains = jnp.where((line == 0) & (lane < 2 * each), head_gains, 0.0)
            rows = slice(part * OWN, (part + 1) * OWN)
            place = ((owner % 2) ^ core, (owner // 4) ^ y, ((owner // 2) % 2) ^ x_lo)
            share[(*place, slice(None), slice(0, UNIT))] = attn[rows]
            share[(*place, slice(None), slice(UNIT, 2 * UNIT))] = output[rows]
            share[(*place, slice(None), slice(2 * UNIT, SHARE))] = head_gains.astype(jnp.bfloat16)
    copies = [
        pltpu.make_async_copy(share.at[i], goal, done.at[i]) for i, goal in ((1, theirs), (0, mine))
    ]
    for copy in copies:
        copy.start()
    for copy in copies:
        copy.wait()


def out_kernel(mixed, tokens, gains, later, hidden, upper, lower, rows, weights, arrived):
    whole = fetch(later, weights, arrived, [(0, 2 * D)])
    for head in range(N_SEQ):
        rows[:, head * 2 * HEAD : (head + 1) * 2 * HEAD] = mixed[head]
    values = tokens[...].astype(jnp.float32) + contract(rows[...], whole[0]()[...])
    hidden[...] = values
    values = (values * inverse_norm(values) * gains[1:2, :]).astype(jnp.bfloat16)
    upper[...] = values[: ROWS // 2]
    lower[...] = values[ROWS // 2 :]


def mid_kernel(
    keep, got_0, got_1, last_0, last_1, hidden, incoming, gains, later,
    hidden_grad, upper, lower, mixed_grad, weights, arrived,
):
    parts = fetch(later, weights, arrived, [(i * 2 * HEAD, 2 * HEAD) for i in range(N_SEQ)])
    half = ROWS // 2
    total_0 = keep[:half, :] + got_0[:half, :].astype(jnp.float32) + last_0[...].astype(jnp.float32)
    total_1 = keep[2 * half : 3 * half, :] + got_1[:half, :].astype(jnp.float32)
    total_1 = total_1 + last_1[...].astype(jnp.float32)
    pulled = jnp.concatenate([total_0, total_1], axis=0) * gains[1:2, :]
    inverse = inverse_norm(hidden[...])
    unit = hidden[...] * inverse
    mean = jnp.mean(unit * pulled, axis=-1, keepdims=True)
    grad = incoming[...].astype(jnp.float32) + inverse * (pulled - unit * mean)
    hidden_grad[...] = grad
    grad = grad.astype(jnp.bfloat16)
    upper[...] = grad[:half]
    lower[...] = grad[half:]
    for head in range(N_SEQ):
        mixed_grad[head] = product(grad, parts[head]()[...]).astype(jnp.bfloat16)


def ordered(pieces, place):
    half = pieces[0].shape[0]
    for array, step, relative, color in PIECES:
        begin = (2 * relative + color) * half
        place[begin : begin + half, :] = pieces[array][step * half : (step + 1) * half, :]


def send_order(values, first_0, first_1, keep):
    half = values.shape[0] // 8

    def block(relative, color):
        begin = (2 * relative + color) * half
        return values[begin : begin + half]

    first_0[:half, :] = block(3, 0).astype(jnp.bfloat16)
    first_0[half:, :] = block(2, 0).astype(jnp.bfloat16)
    first_1[:half, :] = block(1, 1).astype(jnp.bfloat16)
    first_1[half:, :] = block(2, 1).astype(jnp.bfloat16)
    for i, (relative, color) in enumerate(KEPT):
        keep[i * half : (i + 1) * half, :] = block(relative, color)


def kept(values):
    half = values.shape[0] // 4

    def block(relative, color):
        i = KEPT.index((relative, color))
        return values[i * half : (i + 1) * half]

    return block


def mlp_kernel(
    n0, n1, n2, n3, n4, n5, c0, c1, c2, c3, c4, c5, later,
    rows, incoming, both_grad, inner, first_0, first_1, keep, weights, arrived,
):
    steps = range(0, FF_Z, BLOCK)
    parts = fetch(
        later, weights, arrived,
        [(i * FF_Z + begin, BLOCK) for begin in steps for i in range(3)], 2 * D,
    )
    ordered((n0, n1, n2, n3, n4, n5), rows)
    ordered((c0, c1, c2, c3, c4, c5), incoming)
    rows.send()
    incoming.send()
    for i, begin in enumerate(steps):
        columns, second = slice(begin, begin + BLOCK), slice(FF_Z + begin, FF_Z + begin + BLOCK)
        gate = product(rows[...], parts[3 * i]()[...])
        up = product(rows[...], parts[3 * i + 1]()[...])
        inner_grad = product(incoming[...], parts[3 * i + 2]()[...])
        sigmoid = jax.nn.sigmoid(gate)
        swish = gate * sigmoid
        inner[:, columns] = (swish * up).astype(jnp.bfloat16)
        both_grad[:, columns] = (
            inner_grad * up * sigmoid * (1.0 + gate * (1.0 - sigmoid))
        ).astype(jnp.bfloat16)
        both_grad[:, second] = (inner_grad * swish).astype(jnp.bfloat16)
    send_order(contract(both_grad[...], weights[:, : 2 * FF_Z]), first_0, first_1, keep)


def mlp_grad_kernel(
    rows, incoming, both_grad, inner, later,
    share, first_0, first_1, keep, weights, arrived,
):
    whole = fetch(later, weights, arrived, [(0, FF_Z)], 2 * D + 2 * FF_Z)
    for begin in range(0, D, BLOCK):
        goal = slice(begin, begin + BLOCK)
        share[goal, : 2 * FF_Z] = outer_rows(rows[:, goal], both_grad[...]).astype(jnp.bfloat16)
        share[goal, 2 * FF_Z :] = outer_rows(incoming[:, goal], inner[...]).astype(jnp.bfloat16)
        share.send(goal)
    send_order(contract(inner[...], whole[0]()[...]), first_0, first_1, keep)


def last_kernel(
    at, p0, p1, p2, p3, p4, p5, w_gate, w_up, w_query, w_key, w_value, norm_post, norm_input,
    gate, up, down_t, query, key, value, output_t, post_grad, input_grad, gain_grads,
):
    z, x_hi = at[0], at[1]
    pieces = (p0, p1, p2, p3, p4, p5)
    half, middle = OWN // 2, SHARE - FF_Z
    gain_total = jnp.zeros((8, HEAD), jnp.float32)
    for array, step, relative, color in PIECES:
        begin = 2 * step * OWN
        part = pieces[array][begin : begin + OWN, :].astype(jnp.float32)
        place, theirs = z ^ relative, x_hi ^ color
        head = 2 * place + theirs
        one = pl.ds(pl.multiple_of(head * HEAD, HEAD), HEAD)
        two = pl.ds(pl.multiple_of(head * 2 * HEAD, 2 * HEAD), 2 * HEAD)
        query[:, two] = part[:, : 2 * HEAD]
        key[:, one] = part[:, 2 * HEAD : 3 * HEAD]
        value[:, one] = part[:, 3 * HEAD : 4 * HEAD]
        for other in range(2):
            goal = (2 * place + (theirs ^ other)) * 2 * HEAD
            goal = pl.ds(pl.multiple_of(goal, 2 * HEAD), 2 * HEAD)
            first = UNIT + other * 2 * HEAD
            share = part[:, first : first + 2 * HEAD]
            output_t[:, goal] = share if color == 0 else output_t[:, goal] + share
        gain_total += part[0:8, 2 * UNIT :]
        left = pieces[array][begin + OWN : begin + OWN + half, :].astype(jnp.float32)
        right = pieces[array][begin + OWN + half : begin + 2 * OWN, :].astype(jnp.float32)
        rows = slice(color * half, (color + 1) * half)
        start = place * FF_Z
        columns = pl.ds(pl.multiple_of(start, FF_Z), FF_Z)
        gate[rows, columns] = left[:, :FF_Z]
        up[rows, pl.ds(pl.multiple_of(start, FF_Z), middle)] = left[:, FF_Z:]
        up[rows, pl.ds(pl.multiple_of(start + middle, middle), middle)] = right[:, :middle]
        down_t[rows, columns] = right[:, middle:]
    for result in (gate, up, down_t, query, key, value, output_t):
        result.send()
    gain_grads[...] = gain_total

    def paired(*pairs):
        return functools.reduce(
            jnp.add,
            [
                jnp.sum(grad[...] * weight[...].astype(jnp.float32), axis=1, keepdims=True)
                for grad, weight in pairs
            ],
        )

    post_grad[...] = paired((gate, w_gate), (up, w_up)) / norm_post[...]
    input_grad[...] = paired((query, w_query), (key, w_key), (value, w_value)) / norm_input[...]


class Reading:
    def __init__(self, copy, place):
        self.copy, self.place, self.shape = copy, place, place.shape
        copy.start()

    def __getitem__(self, index):
        return self()[index]

    def __call__(self):
        if self.copy is not None:
            self.copy.wait()
            self.copy = None
        return self.place


class Writing:
    def __init__(self, place, goal, semaphores):
        self.place, self.goal, self.semaphores, self.copies = place, goal, semaphores, []
        self.shape = place.shape

    def __getitem__(self, index):
        return self.place[index]

    def __setitem__(self, index, values):
        self.place[index] = values

    def send(self, rows=slice(None)):
        copy = pltpu.make_async_copy(self.place.at[rows], self.goal.at[rows], next(self.semaphores))
        copy.start()
        self.copies.append(copy)


def fetch(source, place, arrived, parts, begin=0):
    result = []
    for i, (first, size) in enumerate(parts):
        part = place.at[:, pl.ds(first, size)]
        copy = pltpu.make_async_copy(source.at[:, pl.ds(begin + first, size)], part, arrived.at[i])
        result.append(Reading(copy, part))
    return result


def kernel_call(kernel, inputs, outs, limit, scratch=(), flops=0, raw=(), raw_outs=0):
    modes = ["scalar" if x.ndim == 1 else "raw" if i in raw else "copy" for i, x in enumerate(inputs)]
    n_in, n_out = len(inputs), len(outs)
    buffers = [pltpu.VMEM(x.shape, x.dtype) for x, m in zip(inputs, modes) if m == "copy"]
    out_buffers = [pltpu.VMEM(shape, dtype) for shape, dtype in outs[raw_outs:]]
    n_sent = 24

    def body(*refs):
        ins, results, rest = refs[:n_in], refs[n_in : n_in + n_out], refs[n_in + n_out :]
        places, rest = iter(rest[: len(buffers)]), rest[len(buffers) :]
        out_places, rest = rest[: len(out_buffers)], rest[len(out_buffers) :]
        (arrived, sent), rest = rest[:2], rest[2:]
        semaphores = iter([sent.at[i] for i in range(n_sent)])
        args = []
        for i, (ref, mode) in enumerate(zip(ins, modes)):
            if mode == "copy":
                place = next(places)
                ref = Reading(pltpu.make_async_copy(ref, place, arrived.at[i]), place)
            args.append(ref)
        writes = [Writing(p, g, semaphores) for p, g in zip(out_places, results[raw_outs:])]
        kernel(*args, *results[:raw_outs], *writes, *rest)
        for read in args:
            if isinstance(read, Reading):
                read()
        for write in writes:
            if not write.copies:
                write.send()
        for write in writes:
            for copy in write.copies:
                copy.wait()

    anywhere, scalars = pl.BlockSpec(memory_space=pltpu.HBM), pl.BlockSpec(memory_space=pltpu.SMEM)
    return pl.pallas_call(
        body,
        out_shape=[jax.ShapeDtypeStruct(shape, dtype) for shape, dtype in outs],
        in_specs=[scalars if m == "scalar" else anywhere for m in modes],
        out_specs=[anywhere] * n_out,
        scratch_shapes=[
            *buffers,
            *out_buffers,
            pltpu.SemaphoreType.DMA((n_in,)),
            pltpu.SemaphoreType.DMA((n_sent,)),
            *(x if not isinstance(x, tuple) else pltpu.VMEM(*x) for x in scratch),
        ],
        compiler_params=pltpu.CompilerParams(vmem_limit_bytes=GRANT * MEGA),
        cost_estimate=pl.CostEstimate(flops=flops, bytes_accessed=8 * MEGA, transcendentals=0),
    )(*inputs)


def per_device(
    tokens,
    segments,
    norm_input,
    w_query,
    w_key,
    w_value,
    norm_query,
    norm_key,
    w_output,
    norm_post,
    w_gate,
    w_up,
    w_down,
    cotangent,
):
    bf16, f32 = jnp.bfloat16, jnp.float32
    s, f = lax.axis_index("seq"), lax.axis_index("fsdp")
    z, x_hi = s // 2, s % 2
    at = jnp.stack([z, x_hi, f // 4, (f // 2) % 2, f % 2]).astype(jnp.int32)
    sequence = tokens[0]
    table = rotation()
    ids = segments[0]
    first_key = jnp.sum((ids[None, :] < ids[:, None]).astype(jnp.int32), axis=1).reshape(1, LENGTH)

    token_pieces = gather4(sequence, swap_x_hi(sequence), swap_z_a, swap_z_b)

    def spread(values):
        wide = jnp.tile(values, N_FSDP)
        owner = jnp.arange(wide.shape[0], dtype=jnp.int32) // values.shape[0]
        return jnp.where(owner == f, wide, jnp.zeros_like(wide))

    def my_columns(values, width):
        return lax.dynamic_slice_in_dim(values, s * width, width, 1)

    rest = jnp.zeros((UNIT - 2 * HEAD,), bf16)
    extra = jnp.concatenate(
        [spread(norm_input), spread(norm_post), spread(norm_query), spread(norm_key), rest]
    ).reshape(5, UNIT)
    extra = jnp.pad(extra, ((0, EXTRA - 5), (0, 0)))
    my_unit = jnp.concatenate(
        [my_columns(w_query, 2 * HEAD), my_columns(w_key, HEAD), my_columns(w_value, HEAD)], axis=1
    )
    piece = lax.optimization_barrier(jnp.concatenate([my_unit, extra], axis=0))
    pair = jnp.concatenate([piece, swap_core(piece)], axis=0)
    other_pair = jnp.concatenate([swap_x_lo(piece), swap_chip(piece)], axis=0)
    pair, other_pair = lax.optimization_barrier((pair, other_pair))
    unit_pieces = gather4(pair, other_pair, swap_y_a, swap_y_b)

    def slice_z(values):
        return lax.dynamic_slice_in_dim(values, z * FF_Z, FF_Z, 1)

    later = jnp.concatenate(
        [w_output.T, slice_z(w_gate), slice_z(w_up), slice_z(w_down.T)], axis=1
    )
    later = lax.all_gather(later, "fsdp", axis=0, tiled=True)

    incoming = after(cotangent[0], (token_pieces[1], token_pieces[4]))
    cotangent_z = gather4(*halves(incoming), swap_z_a, swap_z_b)
    token_pieces = after(token_pieces, cotangent_z)

    normed, raw, heads, mixed, turned, log_total, gains, weight = kernel_call(
        front_kernel,
        (at, *token_pieces, *unit_pieces, first_key, table),
        (
            ((LENGTH, D), bf16),
            ((LENGTH, 3 * HEAD), f32),
            ((LENGTH, UNIT), bf16),
            ((LENGTH, 2 * HEAD), bf16),
            ((2, Z, ROWS, 2 * HEAD), bf16),
            ((8, LENGTH), f32),
            ((8, D), f32),
            ((D, UNIT), bf16),
        ),
        28,
        scratch=(((HEAD, LENGTH), bf16),),
        flops=4 * 10**9,
    )

    mixed_tokens = lax.all_to_all(
        mixed.reshape(N_SEQ, ROWS, 2 * HEAD), "seq", split_axis=0, concat_axis=0, tiled=True
    )
    half_rows = ((ROWS // 2, D), bf16)
    hidden, upper, lower = kernel_call(
        out_kernel,
        (mixed_tokens, sequence, gains, later),
        (((ROWS, D), f32), half_rows, half_rows),
        16,
        scratch=(((ROWS, 2 * D), bf16), ((D, 2 * D), bf16), pltpu.SemaphoreType.DMA((1,))),
        flops=10**9,
        raw=(3,),
    )
    turned = after(turned, upper).reshape(2, Z * ROWS, 2 * HEAD)
    mixed_mine, mixed_other = turned[0], swap_x_hi(turned[1])
    normed_post_z = gather4(upper, lower, swap_z_a, swap_z_b)
    sent = (((ROWS, D), bf16), ((ROWS, D), bf16), ((2 * ROWS, D), f32))
    rows_z, incoming_z, both_grad, inner, first_0, first_1, keep = kernel_call(
        mlp_kernel,
        (*normed_post_z, *cotangent_z, later),
        (
            ((Z * ROWS, D), bf16),
            ((Z * ROWS, D), bf16),
            ((Z * ROWS, 2 * FF_Z), bf16),
            ((Z * ROWS, FF_Z), bf16),
            *sent,
        ),
        28,
        scratch=(((D, 3 * FF_Z), bf16), pltpu.SemaphoreType.DMA((9,))),
        flops=4 * 10**9,
        raw=(12,),
    )
    mlp_share, down_0, down_1, down_keep = kernel_call(
        mlp_grad_kernel,
        (rows_z, incoming_z, both_grad, inner, later),
        (((D, 3 * FF_Z), bf16), *sent),
        24,
        scratch=(((D, FF_Z), bf16), pltpu.SemaphoreType.DMA((1,))),
        flops=4 * 10**9,
        raw=(4,),
    )
    got_0, got_1, last_0, last_1 = scatter4(
        first_0, first_1, kept(keep), swap_z_a, swap_z_b, mlp_share
    )
    mlp_share = lax.psum_scatter(mlp_share, "fsdp", scatter_dimension=0, tiled=True)
    hidden_grad, upper, lower, mixed_grad = kernel_call(
        mid_kernel,
        (keep, got_0, got_1, last_0, last_1, hidden, cotangent[0], gains, later),
        (((ROWS, D), f32), half_rows, half_rows, ((N_SEQ, ROWS, 2 * HEAD), bf16)),
        16,
        scratch=(((D, 2 * D), bf16), pltpu.SemaphoreType.DMA((8,))),
        flops=10**9,
        raw=(8,),
    )
    mixed_grad = lax.all_to_all(mixed_grad, "seq", split_axis=0, concat_axis=0, tiled=True)
    proj_grad_z = gather4(upper, lower, swap_z_a, swap_z_b)
    down_0, down_1 = after((down_0, down_1), upper)
    down_got_0, down_got_1, down_last_0, down_last_1 = scatter4(
        down_0, down_1, kept(down_keep), swap_z_a, swap_z_b
    )
    mixed_grad = after(mixed_grad, (down_got_0, down_got_1))

    back, gain_grads, dx_0, dx_1, dx_keep = kernel_call(
        back_kernel,
        (at, raw, heads, log_total, mixed_grad.reshape(LENGTH, 2 * HEAD), first_key, table, gains, weight),
        (
            ((LENGTH, UNIT), bf16),
            ((8, HEAD), f32),
            ((2 * ROWS, D), bf16),
            ((2 * ROWS, D), bf16),
            ((4 * ROWS, D), f32),
        ),
        30,
        scratch=(
            ((HEAD, LENGTH), bf16),
            ((LENGTH, HEAD), f32),
            ((LENGTH, HEAD), f32),
            ((LENGTH, 2 * HEAD), f32),
            ((LENGTH, UNIT), bf16),
        ),
        flops=4 * 10**9,
    )
    share, share_sent = kernel_call(
        grad_kernel,
        (at, normed, back, gain_grads, *proj_grad_z, mixed_mine, mixed_other),
        (((Z, 2, OWN, SHARE), bf16), ((Z, 2, OWN, SHARE), bf16)),
        20,
        scratch=(
            ((2, Z, 2, OWN, SHARE), bf16),
            ((Z * ROWS, D), bf16),
            ((Z * ROWS, UNIT), bf16),
            pltpu.SemaphoreType.DMA((2,)),
        ),
        flops=4 * 10**9,
        raw_outs=2,
    )
    share = share.reshape(D // 2, SHARE)
    other_share = swap_core(share_sent.reshape(D // 2, SHARE))

    def share_block(relative, color):
        begin = (2 * relative + color) * OWN
        mine, other = share[begin : begin + OWN], other_share[begin : begin + OWN]
        return mine.astype(f32) + other.astype(f32)

    def share_pair(one, two):
        return jnp.concatenate([share_block(*one), share_block(*two)], axis=0).astype(bf16)

    share_0, share_1 = total4(
        share_block,
        *scatter4(
            share_pair((3, 0), (2, 0)), share_pair((1, 1), (2, 1)), share_block, swap_y_a, swap_y_b
        ),
    )
    attn_share = (share_0 + swap_x_lo(share_1.astype(bf16)).astype(f32)).astype(bf16)

    mine = jnp.concatenate([attn_share, mlp_share[:, :SHARE], mlp_share[:, SHARE:]], axis=0)
    mine = lax.optimization_barrier(mine)
    other = swap_x_hi(mine)
    mlp_sum = (mine[OWN:].astype(f32) + other[OWN:].astype(f32)).astype(bf16)
    half = OWN // 2
    zero = jnp.concatenate([mine[:OWN], mlp_sum[:half], mlp_sum[OWN : OWN + half]], axis=0)
    one = jnp.concatenate([other[:OWN], mlp_sum[half:OWN], mlp_sum[OWN + half :]], axis=0)
    zero, one = lax.optimization_barrier((zero, one))
    last_pieces = gather4(zero, one, swap_z_a, swap_z_b)

    normed_grad, other_grad = total4(
        kept(dx_keep), *scatter4(dx_0, dx_1, kept(dx_keep), swap_z_a, swap_z_b)
    )
    normed_grad = normed_grad + swap_x_hi(other_grad.astype(bf16)).astype(f32)
    normed_grad = normed_grad * gains[0:1]
    widened = sequence.astype(f32)
    inverse = inverse_norm(widened)
    unit_input = widened * inverse
    tokens_grad = hidden_grad + inverse * (
        normed_grad - unit_input * jnp.mean(unit_input * normed_grad, axis=-1, keepdims=True)
    )

    down_last = after((down_last_0, down_last_1), last_pieces)
    down = total4(kept(down_keep), down_got_0, down_got_1, *down_last)
    result = (hidden + jnp.concatenate(down, axis=0)).astype(bf16)

    (
        gate_total,
        up_total,
        down_total,
        query_total,
        key_total,
        value_total,
        output_total,
        post_gain_total,
        input_gain_total,
        head_gain_total,
    ) = kernel_call(
        last_kernel,
        (
            at, *last_pieces, w_gate, w_up, w_query, w_key, w_value,
            norm_post.astype(f32).reshape(OWN, 1), norm_input.astype(f32).reshape(OWN, 1),
        ),
        (
            ((OWN, FF), f32),
            ((OWN, FF), f32),
            ((OWN, FF), f32),
            ((OWN, 2 * D), f32),
            ((OWN, D), f32),
            ((OWN, D), f32),
            ((OWN, 2 * D), f32),
            ((OWN, 1), f32),
            ((OWN, 1), f32),
            ((8, HEAD), f32),
        ),
        16,
    )
    return (
        result[None],
        tokens_grad[None],
        input_gain_total.reshape(OWN),
        query_total,
        key_total,
        value_total,
        head_gain_total[0, :8],
        head_gain_total[0, 8:16],
        output_total.T,
        post_gain_total.reshape(OWN),
        gate_total,
        up_total,
        down_total.T,
    )


def solution(mesh):
    rows, columns, tokens = P("fsdp", None), P(None, "fsdp"), P("fsdp", "seq", None)
    in_specs = (
        tokens, rows, P("fsdp"), rows, rows, rows, P("fsdp"), P("fsdp"), columns, P("fsdp"),
        rows, rows, columns, tokens,
    )
    out_specs = (
        tokens, tokens, P("fsdp"), rows, rows, rows, P("fsdp"), P("fsdp"), columns, P("fsdp"),
        rows, rows, columns,
    )
    return jax.shard_map(
        per_device, mesh=mesh, in_specs=in_specs, out_specs=out_specs, check_vma=False
    )
```

```python
import functools
import math

import jax
import jax.numpy as jnp
import numpy as np
from jax import lax
from jax.experimental import pallas as pl
from jax.experimental.pallas import tpu as pltpu
from jax.sharding import PartitionSpec as P

HEAD = 128
D = 1024
FF = 3072
LENGTH = 1024
ROWS = 128
N_SEQ = 8
N_FSDP = 16
Z = 4
OWN = D // N_FSDP
FF_Z = FF // Z
UNIT = 512
BLOCK = 256
EXTRA = 16
SHARE = 2 * UNIT + HEAD
MEGA = 1 << 20
GRANT = 60

TOKEN_PIECES = (
    (0, 0, 0, 0),
    (3, 0, 0, 1),
    (1, 0, 1, 0),
    (2, 0, 3, 0),
    (2, 1, 2, 0),
    (4, 0, 1, 1),
    (5, 0, 3, 1),
    (6, 0, 2, 1),
)

EPSILON = 1e-06
THETA = 1000000.0
NEGATIVE = -1e30
SCALE = 1.0 / math.sqrt(HEAD)

PIECES = (
    (0, 0, 0, 0),
    (1, 0, 1, 0),
    (2, 0, 3, 0),
    (2, 1, 2, 0),
    (3, 0, 0, 1),
    (4, 0, 3, 1),
    (5, 0, 1, 1),
    (5, 1, 2, 1),
)


def exchange(values, axis, bits):
    size = N_SEQ if axis == "seq" else N_FSDP
    return lax.ppermute(values, axis, [(i, i ^ bits) for i in range(size)])


swap_x_hi = functools.partial(exchange, axis="seq", bits=1)
swap_z_a = functools.partial(exchange, axis="seq", bits=2)
swap_z_b = functools.partial(exchange, axis="seq", bits=6)
swap_z_both = functools.partial(exchange, axis="seq", bits=4)
swap_core = functools.partial(exchange, axis="fsdp", bits=1)
swap_x_lo = functools.partial(exchange, axis="fsdp", bits=2)
swap_chip = functools.partial(exchange, axis="fsdp", bits=3)


def swap_x_both(values):
    places = [(i, j) for i in range(N_SEQ) for j in range(N_FSDP)]
    pairs = [(i * N_FSDP + j, (i ^ 1) * N_FSDP + (j ^ 2)) for i, j in places]
    return lax.ppermute(values, ("seq", "fsdp"), pairs)


swap_y_a = functools.partial(exchange, axis="fsdp", bits=4)
swap_y_b = functools.partial(exchange, axis="fsdp", bits=12)


def after(values, *others):
    return lax.optimization_barrier((values, *others))[0]


def gather4(zero, one, swap_a, swap_b):
    zero_1 = swap_a(zero)
    one_1 = swap_b(one)
    zero_2 = swap_b(jnp.concatenate([zero, zero_1], axis=0))
    one_2 = swap_a(jnp.concatenate([one, one_1], axis=0))
    return zero, zero_1, zero_2, one, one_1, one_2


def halves(rows):
    middle = rows.shape[0] // 2
    return rows[:middle], rows[middle:]


def scatter4(first_0, first_1, passed_0, passed_1, swap_a, swap_b, tie=None):
    got_0, got_1 = swap_b(first_0), swap_a(first_1)
    if tie is not None:
        got_0, got_1 = tie(got_0, got_1)
    n = got_0.shape[0] // 2
    last_0 = swap_a((passed_0 + got_0[n:].astype(jnp.float32)).astype(jnp.bfloat16))
    last_1 = swap_b((passed_1 + got_1[n:].astype(jnp.float32)).astype(jnp.bfloat16))
    return got_0[:n], got_1[:n], last_0, last_1


def total4(own_0, own_1, got_0, got_1, last_0, last_1):
    mine_0 = own_0 + got_0.astype(jnp.float32) + last_0.astype(jnp.float32)
    mine_1 = own_1 + got_1.astype(jnp.float32) + last_1.astype(jnp.float32)
    return mine_0, mine_1


def rotation():
    frequency = THETA ** -(np.arange(0, HEAD, 2, dtype=np.float64) / HEAD)
    angles = np.arange(LENGTH, dtype=np.float64)[:, None] * frequency[None, :]
    return jnp.asarray(np.concatenate([np.cos(angles), np.sin(angles)], axis=1).astype(np.float32))


def turns(table):
    turned = pltpu.roll(table, HEAD // 2, 1)
    low = lax.broadcasted_iota(jnp.int32, table.shape, 1) < HEAD // 2
    return jnp.where(low, table, turned), jnp.where(low, -turned, table)


def contract(left, right):
    return lax.dot_general(
        left, right, (((1,), (1,)), ((), ())), preferred_element_type=jnp.float32
    )


def outer_rows(left, right):
    return lax.dot_general(
        left, right, (((0,), (0,)), ((), ())), preferred_element_type=jnp.float32
    )


def product(left, right):
    return jnp.dot(left, right, preferred_element_type=jnp.float32)


def inverse_norm(values):
    return lax.rsqrt(jnp.mean(values * values, axis=-1, keepdims=True) + EPSILON)


def allowed_scores(scores, first_key, begin):
    first = first_key[:, begin : begin + BLOCK]
    place = (BLOCK, BLOCK)
    key, query = lax.broadcasted_iota(jnp.int32, place, 0), lax.broadcasted_iota(jnp.int32, place, 1)
    diagonal = jnp.where((key <= query) & (key + begin >= first), scores[begin:], NEGATIVE)
    if begin == 0:
        return [(0, diagonal)]
    key = lax.broadcasted_iota(jnp.int32, (begin, BLOCK), 0)
    return [(0, jnp.where(key >= first, scores[:begin], NEGATIVE)), (begin, diagonal)]


def front_kernel(
    at, w0, w1, w2, w3, w4, w5, x0, x1, x2, x3, x4, x5, x6, table, first_key,
    turned, normed, raw, heads, mixed, log_total, gains, weight, value_t, arrived,
):
    z, x_hi, y, x_lo, core = at[0], at[1], at[2], at[3], at[4]
    weights, tokens = (w0, w1, w2, w3, w4, w5), (x0, x1, x2, x3, x4, x5, x6)
    extra = jnp.zeros((EXTRA, UNIT), jnp.float32)
    for array, step, relative, color in PIECES:
        for other in range(2):
            first = (2 * step + other) * (OWN + EXTRA)
            owner = 4 * (y ^ relative) + 2 * (x_lo ^ color) + (core ^ other)
            weight[pl.ds(pl.multiple_of(owner * OWN, OWN), OWN), :] = weights[array][
                first : first + OWN, :
            ]
            extra += weights[array][first + OWN : first + OWN + EXTRA, :].astype(jnp.float32)
    gain = jnp.concatenate([extra[0:1], extra[1:2]], axis=1)
    gains[...] = jnp.zeros(gains.shape, jnp.float32)
    gains[0:1, :] = gain
    gains[1:2, :] = jnp.concatenate([extra[2:3], extra[3:4]], axis=1)
    gains[2:3, 0:UNIT] = extra[4:5]
    for array, step, relative, color in TOKEN_PIECES:
        values = tokens[array][step * ROWS : (step + 1) * ROWS, :].astype(jnp.float32)
        place = (2 * (z ^ relative) + (x_hi ^ color)) * ROWS
        normed[pl.ds(pl.multiple_of(place, ROWS), ROWS), :] = (
            values * inverse_norm(values) * gain
        ).astype(jnp.bfloat16)
    normed.send()
    weight.send()
    gain_query, gain_key = extra[4:5, :HEAD], extra[4:5, HEAD : 2 * HEAD]
    for begin in range(0, LENGTH, BLOCK):
        rows = slice(begin, begin + BLOCK)
        projected = product(normed[rows, :], weight[...])
        cosine, sine = turns(table[rows, :])
        raw[rows, :] = projected[:, : 3 * HEAD]
        for head, head_gain in enumerate((gain_query, gain_query, gain_key)):
            part = projected[:, head * HEAD : (head + 1) * HEAD]
            part = part * inverse_norm(part) * head_gain
            part = part * cosine + pltpu.roll(part, HEAD // 2, 1) * sine
            heads[rows, head * HEAD : (head + 1) * HEAD] = part.astype(jnp.bfloat16)
        value = projected[:, 3 * HEAD :]
        heads[rows, 3 * HEAD :] = value.astype(jnp.bfloat16)
        value_t[:, rows] = value.T.astype(jnp.bfloat16)
    raw.send()
    heads.send()
    key = slice(2 * HEAD, 3 * HEAD)
    for begin in range(0, LENGTH, BLOCK):
        rows, end = slice(begin, begin + BLOCK), begin + BLOCK
        for head in range(2):
            columns = slice(head * HEAD, (head + 1) * HEAD)
            scores = contract(heads[:end, key], heads[rows, columns]) * SCALE
            parts = allowed_scores(scores, first_key, begin)
            highest = functools.reduce(
                jnp.maximum, [jnp.max(s, axis=0, keepdims=True) for _, s in parts]
            )
            total, result = 0.0, 0.0
            for first, s in parts:
                weights_now = jnp.exp(s - highest)
                total += jnp.sum(weights_now, axis=0, keepdims=True)
                result += product(
                    value_t[:, first : first + s.shape[0]], weights_now.astype(jnp.bfloat16)
                )
            log_total[head : head + 1, rows] = highest + jnp.log(total)
            mixed[rows, columns] = (result / total).T.astype(jnp.bfloat16)
        mixed.send(rows)
        for part in range(2):
            i = begin // ROWS + part
            goal = turned.at[part ^ x_hi, (begin // BLOCK) ^ z]
            copy = pltpu.make_async_copy(
                mixed.place.at[i * ROWS : (i + 1) * ROWS], goal, arrived.at[i]
            )
            copy.start()
            mixed.copies.append(copy)


def back_kernel(
    at, heads, grad, first_key, log_total, raw, table, gains, weight,
    normed, mixed_mine, mixed_other, p0, p1, p2, p3, p4, p5,
    mine, theirs, first_0, first_1, passed, own, back, key_t, key_sum, value_sum, query_sum,
    gain_grads, proj, mixed, share, turned, done,
):
    key, value = slice(2 * HEAD, 3 * HEAD), slice(3 * HEAD, 4 * HEAD)
    key_t[...] = heads[:, key].astype(jnp.float32).T.astype(jnp.bfloat16)
    key_sum[...] = jnp.zeros_like(key_sum)
    value_sum[...] = jnp.zeros_like(value_sum)
    for begin in range(0, LENGTH, BLOCK):
        rows, end = slice(begin, begin + BLOCK), begin + BLOCK
        for head in range(2):
            columns = slice(head * HEAD, (head + 1) * HEAD)
            query, rows_grad = heads[rows, columns], grad[rows, columns]
            scores = contract(heads[:end, key], query) * SCALE
            prob_grad = contract(heads[:end, value], rows_grad)
            log_now = log_total[head : head + 1, rows]
            parts, mean = [], 0.0
            for first, s in allowed_scores(scores, first_key, begin):
                prob = jnp.exp(s - log_now)
                pulled = prob_grad[first : first + s.shape[0]]
                mean += jnp.sum(prob * pulled, axis=0, keepdims=True)
                parts.append((first, prob, pulled))
            query_part = 0.0
            for first, prob, pulled in parts:
                keys = slice(first, first + prob.shape[0])
                score_grad = (prob * (pulled - mean)).astype(jnp.bfloat16)
                value_sum[keys, :] += product(prob.astype(jnp.bfloat16), rows_grad)
                key_sum[keys, :] += product(score_grad, query)
                query_part += product(key_t[:, keys], score_grad)
            query_sum[rows, columns] = query_part.T
    back[:, value] = value_sum[...].astype(jnp.bfloat16)
    gain_grads[...] = jnp.zeros(gain_grads.shape, jnp.float32)
    for head in range(3):
        columns = slice(head * HEAD, (head + 1) * HEAD)
        which = 0 if head < 2 else 1
        gain = gains[2:3, which * HEAD : (which + 1) * HEAD]
        for begin in range(0, LENGTH, BLOCK):
            rows = slice(begin, begin + BLOCK)
            cosine, sine = turns(table[rows, :])
            pulled = (query_sum[rows, columns] if head < 2 else key_sum[rows, :]) * SCALE
            pulled = pulled.astype(jnp.bfloat16).astype(jnp.float32)
            pulled = pulled * cosine - pltpu.roll(pulled, HEAD // 2, 1) * sine
            part = raw[rows, columns]
            inverse = inverse_norm(part)
            unit = part * inverse
            gain_grads[which : which + 1, :] += jnp.sum(pulled * unit, axis=0, keepdims=True)
            pulled = pulled * gain
            mean = jnp.mean(unit * pulled, axis=-1, keepdims=True)
            back[rows, columns] = (inverse * (pulled - unit * mean)).astype(jnp.bfloat16)

    z, x_hi = at[0], at[1]
    for relative in range(Z):
        for color in range(2):
            place = (2 * (z ^ relative) + (x_hi ^ color)) * ROWS
            begin = (2 * relative + color) * ROWS
            turned[begin : begin + ROWS, :] = back[pl.ds(pl.multiple_of(place, ROWS), ROWS), :]
    send_order(contract(turned[...], weight[...]), first_0, first_1, passed, own)
    for values in (first_0, first_1, passed, own):
        values.send()
    y, x_lo, core = at[2], at[3], at[4]
    ordered((p0, p1, p2, p3, p4, p5), proj)
    mixed[:, : 2 * HEAD] = mixed_mine[...]
    mixed[:, 2 * HEAD :] = mixed_other[...]
    lane = lax.broadcasted_iota(jnp.int32, (OWN, HEAD), 1)
    line = lax.broadcasted_iota(jnp.int32, (OWN, HEAD), 0)
    each = HEAD // N_FSDP
    for begin in range(0, D, BLOCK):
        goal = slice(begin, begin + BLOCK)
        attn = outer_rows(normed[:, goal], back[...]).astype(jnp.bfloat16)
        output = outer_rows(proj[:, goal], mixed[...]).astype(jnp.bfloat16)
        for part in range(BLOCK // OWN):
            owner = begin // OWN + part
            query_gain = pltpu.roll(gain_grads[0:1, :], (HEAD - each * owner) % HEAD, 1)
            key_gain = pltpu.roll(gain_grads[1:2, :], (HEAD + each - each * owner) % HEAD, 1)
            head_gains = jnp.where(lane < each, query_gain, key_gain)
            head_gains = jnp.where((line == 0) & (lane < 2 * each), head_gains, 0.0)
            rows = slice(part * OWN, (part + 1) * OWN)
            place = ((owner % 2) ^ core, (owner // 4) ^ y, ((owner // 2) % 2) ^ x_lo)
            share[(*place, slice(None), slice(0, UNIT))] = attn[rows]
            share[(*place, slice(None), slice(UNIT, 2 * UNIT))] = output[rows]
            share[(*place, slice(None), slice(2 * UNIT, SHARE))] = head_gains.astype(jnp.bfloat16)
    copies = [
        pltpu.make_async_copy(share.at[i], goal, done.at[i]) for i, goal in ((1, theirs), (0, mine))
    ]
    for copy in copies:
        copy.start()
    for copy in copies:
        copy.wait()


def out_kernel(mixed, tokens, gains, later, hidden, upper, lower, rows, weights, arrived):
    whole = fetch(later, weights, arrived, [(0, 2 * D)])
    for head in range(N_SEQ):
        rows[:, head * 2 * HEAD : (head + 1) * 2 * HEAD] = mixed[head]
    values = tokens[...].astype(jnp.float32) + contract(rows[...], whole[0]()[...])
    hidden[...] = values
    values = (values * inverse_norm(values) * gains[1:2, :]).astype(jnp.bfloat16)
    upper[...] = values[: ROWS // 2]
    lower[...] = values[ROWS // 2 :]


def mid_kernel(
    own, got_0, got_1, last_0, last_1, hidden, incoming, gains, later,
    hidden_grad, upper, lower, mixed_grad, weights, arrived,
):
    parts = fetch(later, weights, arrived, [(i * 2 * HEAD, 2 * HEAD) for i in range(N_SEQ)])
    half = ROWS // 2
    total_0 = own[:half, :] + got_0[...].astype(jnp.float32) + last_0[...].astype(jnp.float32)
    total_1 = own[half:, :] + got_1[...].astype(jnp.float32) + last_1[...].astype(jnp.float32)
    pulled = jnp.concatenate([total_0, total_1], axis=0) * gains[1:2, :]
    inverse = inverse_norm(hidden[...])
    unit = hidden[...] * inverse
    mean = jnp.mean(unit * pulled, axis=-1, keepdims=True)
    grad = incoming[...].astype(jnp.float32) + inverse * (pulled - unit * mean)
    hidden_grad[...] = grad
    grad = grad.astype(jnp.bfloat16)
    upper[...] = grad[:half]
    lower[...] = grad[half:]
    for head in range(N_SEQ):
        mixed_grad[head] = product(grad, parts[head]()[...]).astype(jnp.bfloat16)


def ordered(pieces, place):
    half = pieces[0].shape[0]
    for array, step, relative, color in PIECES:
        begin = (2 * relative + color) * half
        place[begin : begin + half, :] = pieces[array][step * half : (step + 1) * half, :]


def send_order(values, first_0, first_1, passed, own):
    half = values.shape[0] // 8

    def block(relative, color):
        begin = (2 * relative + color) * half
        return values[begin : begin + half]

    first_0[:half, :] = block(3, 0).astype(jnp.bfloat16)
    first_0[half:, :] = block(2, 0).astype(jnp.bfloat16)
    first_1[:half, :] = block(1, 1).astype(jnp.bfloat16)
    first_1[half:, :] = block(2, 1).astype(jnp.bfloat16)
    passed[:half, :] = block(1, 0)
    passed[half:, :] = block(3, 1)
    own[:half, :] = block(0, 0)
    own[half:, :] = block(0, 1)


def mlp_kernel(
    n0, n1, n2, n3, n4, n5, c0, c1, c2, c3, c4, c5, later,
    first_0, first_1, passed, own, share, down_0, down_1, down_passed, down_own,
    weights, arrived, rows, incoming, both_grad, inner,
):
    steps = range(0, FF_Z, BLOCK)
    parts = fetch(
        later, weights, arrived,
        [(i * FF_Z + begin, BLOCK) for begin in steps for i in range(3)], 2 * D,
    )
    ordered((n0, n1, n2, n3, n4, n5), rows)
    ordered((c0, c1, c2, c3, c4, c5), incoming)
    for i, begin in enumerate(steps):
        columns, second = slice(begin, begin + BLOCK), slice(FF_Z + begin, FF_Z + begin + BLOCK)
        gate = product(rows[...], parts[3 * i]()[...])
        up = product(rows[...], parts[3 * i + 1]()[...])
        inner_grad = product(incoming[...], parts[3 * i + 2]()[...])
        sigmoid = jax.nn.sigmoid(gate)
        swish = gate * sigmoid
        inner[:, columns] = (swish * up).astype(jnp.bfloat16)
        both_grad[:, columns] = (
            inner_grad * up * sigmoid * (1.0 + gate * (1.0 - sigmoid))
        ).astype(jnp.bfloat16)
        both_grad[:, second] = (inner_grad * swish).astype(jnp.bfloat16)
    send_order(contract(both_grad[...], weights[:, : 2 * FF_Z]), first_0, first_1, passed, own)
    for values in (first_0, first_1, passed, own):
        values.send()
    for begin in range(0, D, BLOCK):
        goal = slice(begin, begin + BLOCK)
        share[goal, : 2 * FF_Z] = outer_rows(rows[:, goal], both_grad[...]).astype(jnp.bfloat16)
        share[goal, 2 * FF_Z :] = outer_rows(incoming[:, goal], inner[...]).astype(jnp.bfloat16)
        share.send(goal)
    send_order(
        contract(inner[...], weights[:, 2 * FF_Z :]), down_0, down_1, down_passed, down_own
    )


def weighed(*pairs):
    return functools.reduce(
        jnp.add,
        [
            jnp.sum(grad[...] * weight[...].astype(jnp.float32), axis=1, keepdims=True)
            for grad, weight in pairs
        ],
    )


def as_row(column):
    return jnp.broadcast_to(column, (OWN, HEAD)).T[0:1, :]


def last_mlp_kernel(mlp, w_gate, w_up, norm, gate, up, down_t, norm_grad):
    for place in range(Z):
        part = mlp[2 * place].astype(jnp.float32) + mlp[2 * place + 1].astype(jnp.float32)
        columns = slice(place * FF_Z, (place + 1) * FF_Z)
        gate[:, columns] = part[:, :FF_Z]
        up[:, columns] = part[:, FF_Z : 2 * FF_Z]
        down_t[:, columns] = part[:, 2 * FF_Z :]
    for result in (gate, up, down_t):
        result.send()
    norm_grad[...] = as_row(weighed((gate, w_gate), (up, w_up)) / norm[...])


def last_attn_kernel(
    at, p0, p1, p2, p3, p4, p5, w_query, w_key, w_value, norm,
    query, key, value, output_t, norm_grad, query_gain, key_gain,
):
    z, x_hi = at[0], at[1]
    pieces = (p0, p1, p2, p3, p4, p5)
    each = HEAD // N_FSDP
    gain_total = jnp.zeros((8, HEAD), jnp.float32)
    for array, step, relative, color in PIECES:
        begin = step * OWN
        part = pieces[array][begin : begin + OWN, :].astype(jnp.float32)
        place, theirs = z ^ relative, x_hi ^ color
        head = 2 * place + theirs
        one = pl.ds(pl.multiple_of(head * HEAD, HEAD), HEAD)
        two = pl.ds(pl.multiple_of(head * 2 * HEAD, 2 * HEAD), 2 * HEAD)
        query[:, two] = part[:, : 2 * HEAD]
        key[:, one] = part[:, 2 * HEAD : 3 * HEAD]
        value[:, one] = part[:, 3 * HEAD : 4 * HEAD]
        for other in range(2):
            goal = (2 * place + (theirs ^ other)) * 2 * HEAD
            goal = pl.ds(pl.multiple_of(goal, 2 * HEAD), 2 * HEAD)
            first = UNIT + other * 2 * HEAD
            share = part[:, first : first + 2 * HEAD]
            output_t[:, goal] = share if color == 0 else output_t[:, goal] + share
        gain_total += part[0:8, 2 * UNIT :]
    for result in (query, key, value, output_t):
        result.send()
    query_gain[...] = gain_total[0:1, :each]
    key_gain[...] = gain_total[0:1, each : 2 * each]
    norm_grad[...] = as_row(weighed((query, w_query), (key, w_key), (value, w_value)) / norm[...])


class Reading:
    def __init__(self, copy, place):
        self.copy, self.place, self.shape = copy, place, place.shape
        copy.start()

    def __getitem__(self, index):
        return self()[index]

    def __call__(self):
        if self.copy is not None:
            self.copy.wait()
            self.copy = None
        return self.place


class Writing:
    def __init__(self, place, goal, semaphores):
        self.place, self.goal, self.semaphores, self.copies = place, goal, semaphores, []
        self.shape = place.shape

    def __getitem__(self, index):
        return self.place[index]

    def __setitem__(self, index, values):
        self.place[index] = values

    def send(self, rows=slice(None)):
        copy = pltpu.make_async_copy(self.place.at[rows], self.goal.at[rows], next(self.semaphores))
        copy.start()
        self.copies.append(copy)


def fetch(source, place, arrived, parts, begin=0):
    result = []
    for i, (first, size) in enumerate(parts):
        part = place.at[:, pl.ds(first, size)]
        copy = pltpu.make_async_copy(source.at[:, pl.ds(begin + first, size)], part, arrived.at[i])
        result.append(Reading(copy, part))
    return result


def kernel_call(kernel, inputs, outs, scratch=(), flops=0, raw=(), raw_outs=0):
    modes = ["scalar" if x.ndim == 1 else "raw" if i in raw else "copy" for i, x in enumerate(inputs)]
    n_in, n_out = len(inputs), len(outs)
    buffers = [pltpu.VMEM(x.shape, x.dtype) for x, m in zip(inputs, modes) if m == "copy"]
    out_buffers = [pltpu.VMEM(shape, dtype) for shape, dtype in outs[raw_outs:]]
    n_sent = 24

    def body(*refs):
        ins, results, rest = refs[:n_in], refs[n_in : n_in + n_out], refs[n_in + n_out :]
        places, rest = iter(rest[: len(buffers)]), rest[len(buffers) :]
        out_places, rest = rest[: len(out_buffers)], rest[len(out_buffers) :]
        (arrived, sent), rest = rest[:2], rest[2:]
        semaphores = iter([sent.at[i] for i in range(n_sent)])
        args = []
        for i, (ref, mode) in enumerate(zip(ins, modes)):
            if mode == "copy":
                place = next(places)
                ref = Reading(pltpu.make_async_copy(ref, place, arrived.at[i]), place)
            args.append(ref)
        writes = [Writing(p, g, semaphores) for p, g in zip(out_places, results[raw_outs:])]
        kernel(*args, *results[:raw_outs], *writes, *rest)
        for read in args:
            if isinstance(read, Reading):
                read()
        for write in writes:
            if not write.copies:
                write.send()
        for write in writes:
            for copy in write.copies:
                copy.wait()

    anywhere, scalars = pl.BlockSpec(memory_space=pltpu.HBM), pl.BlockSpec(memory_space=pltpu.SMEM)
    return pl.pallas_call(
        body,
        out_shape=[jax.ShapeDtypeStruct(shape, dtype) for shape, dtype in outs],
        in_specs=[scalars if m == "scalar" else anywhere for m in modes],
        out_specs=[anywhere] * n_out,
        scratch_shapes=[
            *buffers,
            *out_buffers,
            pltpu.SemaphoreType.DMA((n_in,)),
            pltpu.SemaphoreType.DMA((n_sent,)),
            *(x if not isinstance(x, tuple) else pltpu.VMEM(*x) for x in scratch),
        ],
        compiler_params=pltpu.CompilerParams(vmem_limit_bytes=GRANT * MEGA),
        cost_estimate=pl.CostEstimate(flops=flops, bytes_accessed=8 * MEGA, transcendentals=0),
    )(*inputs)


def per_device(
    tokens,
    segments,
    norm_input,
    w_query,
    w_key,
    w_value,
    norm_query,
    norm_key,
    w_output,
    norm_post,
    w_gate,
    w_up,
    w_down,
    cotangent,
):
    bf16, f32 = jnp.bfloat16, jnp.float32
    s, f = lax.axis_index("seq"), lax.axis_index("fsdp")
    z, x_hi = s // 2, s % 2
    at = jnp.stack([z, x_hi, f // 4, (f // 2) % 2, f % 2]).astype(jnp.int32)
    sequence = tokens[0]
    table = rotation()
    ids = segments[0]
    first_key = jnp.sum((ids[None, :] < ids[:, None]).astype(jnp.int32), axis=1).reshape(1, LENGTH)

    other_rows = swap_x_hi(sequence)

    def spread(values):
        wide = jnp.tile(values, N_FSDP)
        owner = jnp.arange(wide.shape[0], dtype=jnp.int32) // values.shape[0]
        return jnp.where(owner == f, wide, jnp.zeros_like(wide))

    def my_columns(values, width):
        return lax.dynamic_slice_in_dim(values, s * width, width, 1)

    rest = jnp.zeros((UNIT - 2 * HEAD,), bf16)
    extra = jnp.concatenate(
        [spread(norm_input), spread(norm_post), spread(norm_query), spread(norm_key), rest]
    ).reshape(5, UNIT)
    extra = jnp.pad(extra, ((0, EXTRA - 5), (0, 0)))
    my_unit = jnp.concatenate(
        [my_columns(w_query, 2 * HEAD), my_columns(w_key, HEAD), my_columns(w_value, HEAD)], axis=1
    )
    piece = lax.optimization_barrier(jnp.concatenate([my_unit, extra], axis=0))
    pair = jnp.concatenate([piece, swap_core(piece)], axis=0)
    other_pair = jnp.concatenate([swap_x_lo(piece), swap_chip(piece)], axis=0)
    pair, other_pair = lax.optimization_barrier((pair, other_pair))
    pair_1, other_pair_1 = swap_y_a(pair), swap_y_b(other_pair)

    pair_2 = swap_y_b(jnp.concatenate([pair, pair_1], axis=0))
    other_pair_2 = swap_y_a(jnp.concatenate([other_pair, other_pair_1], axis=0))
    unit_pieces = (pair, pair_1, pair_2, other_pair, other_pair_1, other_pair_2)
    rows_1 = swap_z_a(sequence)
    rows_2 = swap_z_b(jnp.concatenate([sequence, rows_1], axis=0))
    token_pieces = (
        sequence,
        rows_1,
        rows_2,
        other_rows,
        swap_z_a(other_rows),
        swap_z_b(other_rows),
        swap_z_both(other_rows),
    )

    def slice_z(values):
        return lax.dynamic_slice_in_dim(values, z * FF_Z, FF_Z, 1)

    later = jnp.concatenate(
        [w_output.T, slice_z(w_gate), slice_z(w_up), slice_z(w_down.T)], axis=1
    )
    later = lax.all_gather(later, "fsdp", axis=0, tiled=True)

    turned, normed, raw, heads, mixed, log_total, gains, weight = kernel_call(
        front_kernel,
        (at, *unit_pieces, *token_pieces, table, first_key),
        (
            ((2, Z, ROWS, 2 * HEAD), bf16),
            ((LENGTH, D), bf16),
            ((LENGTH, 3 * HEAD), f32),
            ((LENGTH, UNIT), bf16),
            ((LENGTH, 2 * HEAD), bf16),
            ((8, LENGTH), f32),
            ((8, D), f32),
            ((D, UNIT), bf16),
        ),
        scratch=(((HEAD, LENGTH), bf16), pltpu.SemaphoreType.DMA((8,))),
        flops=4 * 10**9,
        raw_outs=1,
    )

    mixed_tokens = lax.all_to_all(
        mixed.reshape(N_SEQ, ROWS, 2 * HEAD), "seq", split_axis=0, concat_axis=0, tiled=True
    )
    turned = turned.reshape(2, Z * ROWS, 2 * HEAD)
    mixed_mine, mixed_other = turned[0], swap_x_hi(turned[1])
    mixed_tokens, mixed_other = lax.optimization_barrier((mixed_tokens, mixed_other))
    incoming = after(cotangent[0], mixed)
    cotangent_z = gather4(*halves(incoming), swap_z_a, swap_z_b)
    half_rows = ((ROWS // 2, D), bf16)
    hidden, upper, lower = kernel_call(
        out_kernel,
        (mixed_tokens, sequence, gains, later),
        (((ROWS, D), f32), half_rows, half_rows),
        scratch=(((ROWS, 2 * D), bf16), ((D, 2 * D), bf16), pltpu.SemaphoreType.DMA((1,))),
        flops=10**9,
        raw=(3,),
    )
    upper, lower = after((upper, lower), cotangent_z)
    normed_post_z = gather4(upper, lower, swap_z_a, swap_z_b)
    sent = (((ROWS, D), bf16), ((ROWS, D), bf16), ((ROWS, D), f32), ((ROWS, D), f32))
    first_0, first_1, passed, own, mlp_share, down_0, down_1, down_passed, down_own = kernel_call(
        mlp_kernel,
        (*normed_post_z, *cotangent_z, later),
        (*sent, ((D, 3 * FF_Z), bf16), *sent),
        scratch=(
            ((D, 3 * FF_Z), bf16),
            pltpu.SemaphoreType.DMA((9,)),
            ((Z * ROWS, D), bf16),
            ((Z * ROWS, D), bf16),
            ((Z * ROWS, 2 * FF_Z), bf16),
            ((Z * ROWS, FF_Z), bf16),
        ),
        flops=8 * 10**9,
        raw=(12,),
    )
    got_0, got_1, last_0, last_1 = scatter4(
        first_0, first_1, *halves(passed), swap_z_a, swap_z_b
    )
    mlp_share = lax.psum_scatter(mlp_share, "fsdp", scatter_dimension=0, tiled=True)
    hidden_grad, upper, lower, mixed_grad = kernel_call(
        mid_kernel,
        (own, got_0, got_1, last_0, last_1, hidden, cotangent[0], gains, later),
        (((ROWS, D), f32), half_rows, half_rows, ((N_SEQ, ROWS, 2 * HEAD), bf16)),
        scratch=(((D, 2 * D), bf16), pltpu.SemaphoreType.DMA((8,))),
        flops=10**9,
        raw=(8,),
    )
    mixed_grad = lax.all_to_all(mixed_grad, "seq", split_axis=0, concat_axis=0, tiled=True)
    down_got = []

    def tie_down(*got):
        down_got.extend(after(got, upper))
        return down_got

    down_parts = scatter4(down_0, down_1, *halves(down_passed), swap_z_a, swap_z_b, tie_down)
    upper, lower = after((upper, lower), tuple(down_got))
    proj_grad_z = gather4(upper, lower, swap_z_a, swap_z_b)
    result = hidden + jnp.concatenate(total4(*halves(down_own), *down_parts), axis=0)
    result = result.astype(bf16)

    share, share_sent, dx_0, dx_1, dx_passed, dx_own = kernel_call(
        back_kernel,
        (
            at, heads, mixed_grad.reshape(LENGTH, 2 * HEAD), first_key, log_total, raw, table, gains,
            weight, normed, mixed_mine, mixed_other, *proj_grad_z,
        ),
        (
            ((Z, 2, OWN, SHARE), bf16),
            ((Z, 2, OWN, SHARE), bf16),
            ((2 * ROWS, D), bf16),
            ((2 * ROWS, D), bf16),
            ((2 * ROWS, D), f32),
            ((2 * ROWS, D), f32),
        ),
        scratch=(
            ((LENGTH, UNIT), bf16),
            ((HEAD, LENGTH), bf16),
            ((LENGTH, HEAD), f32),
            ((LENGTH, HEAD), f32),
            ((LENGTH, 2 * HEAD), f32),
            ((8, HEAD), f32),
            ((Z * ROWS, D), bf16),
            ((Z * ROWS, UNIT), bf16),
            ((2, Z, 2, OWN, SHARE), bf16),
            ((LENGTH, UNIT), bf16),
            pltpu.SemaphoreType.DMA((2,)),
        ),
        flops=8 * 10**9,
        raw_outs=2,
    )
    share = share.reshape(D // 2, SHARE)
    other_share = swap_core(share_sent.reshape(D // 2, SHARE))

    def share_block(relative, color):
        begin = (2 * relative + color) * OWN
        mine, other = share[begin : begin + OWN], other_share[begin : begin + OWN]
        return mine.astype(f32) + other.astype(f32)

    def share_pair(one, two):
        return jnp.concatenate([share_block(*one), share_block(*two)], axis=0).astype(bf16)

    dx_got = swap_z_b(dx_0), swap_z_a(dx_1)
    share_got = (
        swap_y_b(share_pair((3, 0), (2, 0))),
        swap_y_a(share_pair((1, 1), (2, 1))),
    )
    dx_got, share_got = lax.optimization_barrier((dx_got, share_got))

    def second(got, passed_0, passed_1, swap_a, swap_b):
        n = got[0].shape[0] // 2
        last_0 = swap_a((passed_0 + got[0][n:].astype(f32)).astype(bf16))
        last_1 = swap_b((passed_1 + got[1][n:].astype(f32)).astype(bf16))
        return got[0][:n], got[1][:n], last_0, last_1

    share_parts = second(share_got, share_block(1, 0), share_block(3, 1), swap_y_a, swap_y_b)
    dx_parts = second(dx_got, *halves(dx_passed), swap_z_a, swap_z_b)
    share_parts, dx_parts = lax.optimization_barrier((share_parts, dx_parts))
    share_0, share_1 = total4(share_block(0, 0), share_block(0, 1), *share_parts)
    share_0, share_1 = share_0.astype(bf16), share_1.astype(bf16)
    normed_grad, other_grad = total4(*halves(dx_own), *dx_parts)
    other_grad = other_grad.astype(bf16)
    share_0, share_1, other_grad = lax.optimization_barrier((share_0, share_1, other_grad))
    attn_share = (share_0.astype(f32) + swap_x_lo(share_1).astype(f32)).astype(bf16)
    other_attn = swap_x_hi(share_0).astype(f32) + swap_x_both(share_1).astype(f32)
    other_attn = other_attn.astype(bf16)
    other_grad = swap_x_hi(other_grad)
    attn_share, other_attn, other_grad = lax.optimization_barrier(
        (attn_share, other_attn, other_grad)
    )
    normed_grad = (normed_grad + other_grad.astype(f32)) * gains[0:1]
    widened = sequence.astype(f32)
    inverse = inverse_norm(widened)
    unit_input = widened * inverse
    tokens_grad = hidden_grad + inverse * (
        normed_grad - unit_input * jnp.mean(unit_input * normed_grad, axis=-1, keepdims=True)
    )

    last_pieces = gather4(attn_share, other_attn, swap_z_a, swap_z_b)
    mlp_pieces = lax.all_gather(mlp_share, "seq", axis=0, tiled=False)

    query_total, key_total, value_total, output_total, input_gain, query_gain, key_gain = kernel_call(
        last_attn_kernel,
        (
            at, *last_pieces, w_query, w_key, w_value, norm_input.astype(f32).reshape(OWN, 1),
        ),
        (
            ((OWN, 2 * D), f32),
            ((OWN, D), f32),
            ((OWN, D), f32),
            ((OWN, 2 * D), f32),
            ((1, OWN), f32),
            ((1, HEAD // N_FSDP), f32),
            ((1, HEAD // N_FSDP), f32),
        ),
    )
    gate_total, up_total, down_total, post_gain = kernel_call(
        last_mlp_kernel,
        (mlp_pieces, w_gate, w_up, norm_post.astype(f32).reshape(OWN, 1)),
        (((OWN, FF), f32), ((OWN, FF), f32), ((OWN, FF), f32), ((1, OWN), f32)),
    )
    return (
        result[None],
        tokens_grad[None],
        input_gain[0],
        query_total,
        key_total,
        value_total,
        query_gain[0],
        key_gain[0],
        output_total.T,
        post_gain[0],
        gate_total,
        up_total,
        down_total.T,
    )


def solution(mesh):
    rows, columns, tokens = P("fsdp", None), P(None, "fsdp"), P("fsdp", "seq", None)
    in_specs = (
        tokens, rows, P("fsdp"), rows, rows, rows, P("fsdp"), P("fsdp"), columns, P("fsdp"),
        rows, rows, columns, tokens,
    )
    out_specs = (
        tokens, tokens, P("fsdp"), rows, rows, rows, P("fsdp"), P("fsdp"), columns, P("fsdp"),
        rows, rows, columns,
    )
    return jax.shard_map(
        per_device, mesh=mesh, in_specs=in_specs, out_specs=out_specs, check_vma=False
    )
```

```python
import functools
import math

import jax
import jax.numpy as jnp
import numpy as np
from jax import lax
from jax.experimental import pallas as pl
from jax.experimental.pallas import tpu as pltpu
from jax.sharding import PartitionSpec as P

HEAD = 128
D = 1024
FF = 3072
LENGTH = 1024
ROWS = 128
N_SEQ = 8
N_FSDP = 16
Z = 4
OWN = D // N_FSDP
FF_Z = FF // Z
UNIT = 512
BLOCK = 256
EXTRA = 16
SHARE = 2 * UNIT + HEAD
MEGA = 1 << 20
GRANT = 60

TOKEN_PIECES = (
    (0, 0, 0, 0),
    (3, 0, 0, 1),
    (1, 0, 1, 0),
    (2, 0, 3, 0),
    (2, 1, 2, 0),
    (4, 0, 1, 1),
    (5, 0, 3, 1),
    (6, 0, 2, 1),
)

EPSILON = 1e-06
THETA = 1000000.0
NEGATIVE = -1e30
SCALE = 1.0 / math.sqrt(HEAD)

PIECES = (
    (0, 0, 0, 0),
    (1, 0, 1, 0),
    (2, 0, 3, 0),
    (2, 1, 2, 0),
    (3, 0, 0, 1),
    (4, 0, 3, 1),
    (5, 0, 1, 1),
    (5, 1, 2, 1),
)


def exchange(values, axis, bits):
    size = N_SEQ if axis == "seq" else N_FSDP
    return lax.ppermute(values, axis, [(i, i ^ bits) for i in range(size)])


swap_x_hi = functools.partial(exchange, axis="seq", bits=1)
swap_z_a = functools.partial(exchange, axis="seq", bits=2)
swap_z_b = functools.partial(exchange, axis="seq", bits=6)
swap_z_both = functools.partial(exchange, axis="seq", bits=4)
swap_core = functools.partial(exchange, axis="fsdp", bits=1)
swap_x_lo = functools.partial(exchange, axis="fsdp", bits=2)
swap_chip = functools.partial(exchange, axis="fsdp", bits=3)


def swap_x_both(values):
    places = [(i, j) for i in range(N_SEQ) for j in range(N_FSDP)]
    pairs = [(i * N_FSDP + j, (i ^ 1) * N_FSDP + (j ^ 2)) for i, j in places]
    return lax.ppermute(values, ("seq", "fsdp"), pairs)


swap_y_a = functools.partial(exchange, axis="fsdp", bits=4)
swap_y_b = functools.partial(exchange, axis="fsdp", bits=12)


def after(values, *others):
    return lax.optimization_barrier((values, *others))[0]


def gather4(zero, one, swap_a, swap_b):
    zero_1 = swap_a(zero)
    one_1 = swap_b(one)
    zero_2 = swap_b(jnp.concatenate([zero, zero_1], axis=0))
    one_2 = swap_a(jnp.concatenate([one, one_1], axis=0))
    return zero, zero_1, zero_2, one, one_1, one_2


def gather_z(values):
    groups = [[2 * z + x_hi for z in range(Z)] for x_hi in range(2)]
    return lax.all_gather(values, "seq", axis=0, tiled=False, axis_index_groups=groups)


def halves(rows):
    middle = rows.shape[0] // 2
    return rows[:middle], rows[middle:]


def scatter4(first_0, first_1, passed_0, passed_1, swap_a, swap_b, tie=None):
    got_0, got_1 = swap_b(first_0), swap_a(first_1)
    if tie is not None:
        got_0, got_1 = tie(got_0, got_1)
    n = got_0.shape[0] // 2
    last_0 = swap_a((passed_0 + got_0[n:].astype(jnp.float32)).astype(jnp.bfloat16))
    last_1 = swap_b((passed_1 + got_1[n:].astype(jnp.float32)).astype(jnp.bfloat16))
    return got_0[:n], got_1[:n], last_0, last_1


def total4(own_0, own_1, got_0, got_1, last_0, last_1):
    n = own_0.shape[0]
    mine_0 = own_0 + wide(got_0[:n]) + wide(last_0)
    mine_1 = own_1 + wide(got_1[:n]) + wide(last_1)
    return mine_0, mine_1


def wide(values):
    return values.astype(jnp.float32)


def rotation():
    frequency = THETA ** -(np.arange(0, HEAD, 2, dtype=np.float64) / HEAD)
    angles = np.arange(LENGTH, dtype=np.float64)[:, None] * frequency[None, :]
    return jnp.asarray(np.concatenate([np.cos(angles), np.sin(angles)], axis=1).astype(np.float32))


def turns(table):
    turned = pltpu.roll(table, HEAD // 2, 1)
    low = lax.broadcasted_iota(jnp.int32, table.shape, 1) < HEAD // 2
    return jnp.where(low, table, turned), jnp.where(low, -turned, table)


def contract(left, right):
    return lax.dot_general(
        left, right, (((1,), (1,)), ((), ())), preferred_element_type=jnp.float32
    )


def outer_rows(left, right):
    return lax.dot_general(
        left, right, (((0,), (0,)), ((), ())), preferred_element_type=jnp.float32
    )


def product(left, right):
    return jnp.dot(left, right, preferred_element_type=jnp.float32)


def inverse_norm(values):
    return lax.rsqrt(jnp.mean(values * values, axis=-1, keepdims=True) + EPSILON)


def allowed_scores(scores, first_key, begin):
    first = first_key[:, begin : begin + BLOCK]
    place = (BLOCK, BLOCK)
    key, query = lax.broadcasted_iota(jnp.int32, place, 0), lax.broadcasted_iota(jnp.int32, place, 1)
    diagonal = jnp.where((key <= query) & (key + begin >= first), scores[begin:], NEGATIVE)
    if begin == 0:
        return [(0, diagonal)]
    key = lax.broadcasted_iota(jnp.int32, (begin, BLOCK), 0)
    return [(0, jnp.where(key >= first, scores[:begin], NEGATIVE)), (begin, diagonal)]


def front_kernel(
    at, w0, w1, w2, w3, w4, w5, x0, x1, x2, x3, x4, x5, x6, table, first_key,
    turned, normed, raw, heads, mixed, log_total, gains, weight, value_t, arrived,
):
    z, x_hi, y, x_lo, core = at[0], at[1], at[2], at[3], at[4]
    weights, tokens = (w0, w1, w2, w3, w4, w5), (x0, x1, x2, x3, x4, x5, x6)
    extra = jnp.zeros((EXTRA, UNIT), jnp.float32)
    for array, step, relative, color in PIECES:
        for other in range(2):
            first = (2 * step + other) * (OWN + EXTRA)
            owner = 4 * (y ^ relative) + 2 * (x_lo ^ color) + (core ^ other)
            weight[pl.ds(pl.multiple_of(owner * OWN, OWN), OWN), :] = weights[array][
                first : first + OWN, :
            ]
            extra += weights[array][first + OWN : first + OWN + EXTRA, :].astype(jnp.float32)
    gain = jnp.concatenate([extra[0:1], extra[1:2]], axis=1)
    gains[...] = jnp.zeros(gains.shape, jnp.float32)
    gains[0:1, :] = gain
    gains[1:2, :] = jnp.concatenate([extra[2:3], extra[3:4]], axis=1)
    gains[2:3, 0:UNIT] = extra[4:5]
    for array, step, relative, color in TOKEN_PIECES:
        values = tokens[array][step * ROWS : (step + 1) * ROWS, :].astype(jnp.float32)
        place = (2 * (z ^ relative) + (x_hi ^ color)) * ROWS
        normed[pl.ds(pl.multiple_of(place, ROWS), ROWS), :] = (
            values * inverse_norm(values) * gain
        ).astype(jnp.bfloat16)
    normed.send()
    weight.send()
    gain_query, gain_key = extra[4:5, :HEAD], extra[4:5, HEAD : 2 * HEAD]
    for begin in range(0, LENGTH, BLOCK):
        rows = slice(begin, begin + BLOCK)
        projected = product(normed[rows, :], weight[...])
        cosine, sine = turns(table[rows, :])
        raw[rows, :] = projected[:, : 3 * HEAD]
        for head, head_gain in enumerate((gain_query, gain_query, gain_key)):
            part = projected[:, head * HEAD : (head + 1) * HEAD]
            part = part * inverse_norm(part) * head_gain
            part = part * cosine + pltpu.roll(part, HEAD // 2, 1) * sine
            heads[rows, head * HEAD : (head + 1) * HEAD] = part.astype(jnp.bfloat16)
        value = projected[:, 3 * HEAD :]
        heads[rows, 3 * HEAD :] = value.astype(jnp.bfloat16)
        value_t[:, rows] = value.T.astype(jnp.bfloat16)
    raw.send()
    heads.send()
    key = slice(2 * HEAD, 3 * HEAD)
    for begin in range(0, LENGTH, BLOCK):
        rows, end = slice(begin, begin + BLOCK), begin + BLOCK
        for head in range(2):
            columns = slice(head * HEAD, (head + 1) * HEAD)
            scores = contract(heads[:end, key], heads[rows, columns]) * SCALE
            parts = allowed_scores(scores, first_key, begin)
            highest = functools.reduce(
                jnp.maximum, [jnp.max(s, axis=0, keepdims=True) for _, s in parts]
            )
            total, result = 0.0, 0.0
            for first, s in parts:
                weights_now = jnp.exp(s - highest)
                total += jnp.sum(weights_now, axis=0, keepdims=True)
                result += product(
                    value_t[:, first : first + s.shape[0]], weights_now.astype(jnp.bfloat16)
                )
            log_total[head : head + 1, rows] = highest + jnp.log(total)
            mixed[rows, columns] = (result / total).T.astype(jnp.bfloat16)
        mixed.send(rows)
        for part in range(2):
            i = begin // ROWS + part
            goal = turned.at[part ^ x_hi, (begin // BLOCK) ^ z]
            copy = pltpu.make_async_copy(
                mixed.place.at[i * ROWS : (i + 1) * ROWS], goal, arrived.at[i]
            )
            copy.start()
            mixed.copies.append(copy)


def back_kernel(
    at, heads, grad, first_key, log_total, raw, table, gains, weight,
    normed, mixed_mine, mixed_other, p0, p1, p2, p3, p4, p5,
    mine, theirs, first_0, first_1, passed, own, back, key_t, key_sum, value_sum, query_sum,
    gain_grads, proj, mixed, share, turned, done,
):
    key, value = slice(2 * HEAD, 3 * HEAD), slice(3 * HEAD, 4 * HEAD)
    key_t[...] = heads[:, key].astype(jnp.float32).T.astype(jnp.bfloat16)
    key_sum[...] = jnp.zeros_like(key_sum)
    value_sum[...] = jnp.zeros_like(value_sum)
    for start in range(0, LENGTH, BLOCK):
        rows, end = slice(start, start + BLOCK), start + BLOCK
        for head in range(2):
            columns = slice(head * HEAD, (head + 1) * HEAD)
            query, rows_grad = heads[rows, columns], grad[rows, columns]
            scores = contract(heads[:end, key], query) * SCALE
            prob_grad = contract(heads[:end, value], rows_grad)
            log_now = log_total[head : head + 1, rows]
            parts, mean = [], 0.0
            for first, s in allowed_scores(scores, first_key, start):
                prob = jnp.exp(s - log_now)
                pulled = prob_grad[first : first + s.shape[0]]
                mean += jnp.sum(prob * pulled, axis=0, keepdims=True)
                parts.append((first, prob, pulled))
            query_part = 0.0
            for first, prob, pulled in parts:
                keys = slice(first, first + prob.shape[0])
                score_grad = (prob * (pulled - mean)).astype(jnp.bfloat16)
                value_sum[keys, :] += product(prob.astype(jnp.bfloat16), rows_grad)
                key_sum[keys, :] += product(score_grad, query)
                query_part += product(key_t[:, keys], score_grad)
            query_sum[rows, columns] = query_part.T
    back[:, value] = value_sum[...].astype(jnp.bfloat16)
    gain_grads[...] = jnp.zeros(gain_grads.shape, jnp.float32)
    for head in range(3):
        columns = slice(head * HEAD, (head + 1) * HEAD)
        which = 0 if head < 2 else 1
        gain = gains[2:3, which * HEAD : (which + 1) * HEAD]
        for start in range(0, LENGTH, BLOCK):
            rows = slice(start, start + BLOCK)
            cosine, sine = turns(table[rows, :])
            pulled = (query_sum[rows, columns] if head < 2 else key_sum[rows, :]) * SCALE
            pulled = pulled.astype(jnp.bfloat16).astype(jnp.float32)
            pulled = pulled * cosine - pltpu.roll(pulled, HEAD // 2, 1) * sine
            part = raw[rows, columns]
            inverse = inverse_norm(part)
            unit = part * inverse
            gain_grads[which : which + 1, :] += jnp.sum(pulled * unit, axis=0, keepdims=True)
            pulled = pulled * gain
            mean = jnp.mean(unit * pulled, axis=-1, keepdims=True)
            back[rows, columns] = (inverse * (pulled - unit * mean)).astype(jnp.bfloat16)

    z, x_hi = at[0], at[1]
    for relative in range(Z):
        for color in range(2):
            place = (2 * (z ^ relative) + (x_hi ^ color)) * ROWS
            goal = (2 * relative + color) * ROWS
            turned[goal : goal + ROWS, :] = back[pl.ds(pl.multiple_of(place, ROWS), ROWS), :]
    send_order(contract(turned[...], weight[...]), first_0, first_1, passed, own)
    for values in (first_0, first_1, passed, own):
        values.send()
    y, x_lo, core = at[2], at[3], at[4]
    ordered((p0, p1, p2, p3, p4, p5), proj)
    mixed[:, : 2 * HEAD] = mixed_mine[...]
    mixed[:, 2 * HEAD :] = mixed_other[...]
    lane = lax.broadcasted_iota(jnp.int32, (OWN, HEAD), 1)
    line = lax.broadcasted_iota(jnp.int32, (OWN, HEAD), 0)
    each = HEAD // N_FSDP
    for start in range(0, D, BLOCK):
        goal = slice(start, start + BLOCK)
        attn = outer_rows(normed[:, goal], back[...]).astype(jnp.bfloat16)
        output = outer_rows(proj[:, goal], mixed[...]).astype(jnp.bfloat16)
        for part in range(BLOCK // OWN):
            owner = start // OWN + part
            query_gain = pltpu.roll(gain_grads[0:1, :], (HEAD - each * owner) % HEAD, 1)
            key_gain = pltpu.roll(gain_grads[1:2, :], (HEAD + each - each * owner) % HEAD, 1)
            head_gains = jnp.where(lane < each, query_gain, key_gain)
            head_gains = jnp.where((line == 0) & (lane < 2 * each), head_gains, 0.0)
            rows = slice(part * OWN, (part + 1) * OWN)
            place = ((owner % 2) ^ core, (owner // 4) ^ y, ((owner // 2) % 2) ^ x_lo)
            share[(*place, slice(None), slice(0, UNIT))] = attn[rows]
            share[(*place, slice(None), slice(UNIT, 2 * UNIT))] = output[rows]
            share[(*place, slice(None), slice(2 * UNIT, SHARE))] = head_gains.astype(jnp.bfloat16)
    copies = [
        pltpu.make_async_copy(share.at[i], goal, done.at[i]) for i, goal in ((1, theirs), (0, mine))
    ]
    for copy in copies:
        copy.start()
    for copy in copies:
        copy.wait()


def out_kernel(mixed, tokens, gains, weights, hidden, upper, lower, rows):
    for head in range(N_SEQ):
        rows[:, head * 2 * HEAD : (head + 1) * 2 * HEAD] = mixed[head]
    values = tokens[...].astype(jnp.float32) + contract(rows[...], weights[...])
    hidden[...] = values
    values = (values * inverse_norm(values) * gains[1:2, :]).astype(jnp.bfloat16)
    upper[...] = values[: ROWS // 2]
    lower[...] = values[ROWS // 2 :]


def mid_kernel(
    own, got_0, got_1, last_0, last_1, hidden, incoming, gains, weights,
    hidden_grad, upper, lower, mixed_grad,
):
    half = ROWS // 2
    total_0 = own[:half, :] + got_0[...].astype(jnp.float32) + last_0[...].astype(jnp.float32)
    total_1 = own[half:, :] + got_1[...].astype(jnp.float32) + last_1[...].astype(jnp.float32)
    pulled = jnp.concatenate([total_0, total_1], axis=0) * gains[1:2, :]
    inverse = inverse_norm(hidden[...])
    unit = hidden[...] * inverse
    mean = jnp.mean(unit * pulled, axis=-1, keepdims=True)
    grad = incoming[...].astype(jnp.float32) + inverse * (pulled - unit * mean)
    hidden_grad[...] = grad
    grad = grad.astype(jnp.bfloat16)
    upper[...] = grad[:half]
    lower[...] = grad[half:]
    for head in range(N_SEQ):
        mixed_grad[head] = product(grad, weights[:, head * 2 * HEAD : (head + 1) * 2 * HEAD]).astype(jnp.bfloat16)


def ordered(pieces, place):
    half = pieces[0].shape[0]
    for array, step, relative, color in PIECES:
        begin = (2 * relative + color) * half
        place[begin : begin + half, :] = pieces[array][step * half : (step + 1) * half, :]


def send_order(values, first_0, first_1, passed, own):
    half = values.shape[0] // 8

    def block(relative, color):
        begin = (2 * relative + color) * half
        return values[begin : begin + half]

    first_0[:half, :] = block(3, 0).astype(jnp.bfloat16)
    first_0[half:, :] = block(2, 0).astype(jnp.bfloat16)
    first_1[:half, :] = block(1, 1).astype(jnp.bfloat16)
    first_1[half:, :] = block(2, 1).astype(jnp.bfloat16)
    passed[:half, :] = block(1, 0)
    passed[half:, :] = block(3, 1)
    own[:half, :] = block(0, 0)
    own[half:, :] = block(0, 1)


def mlp_kernel(
    n0, n1, n2, n3, n4, n5, c0, c1, c2, c3, c4, c5, weights,
    first_0, first_1, passed, own, share, down_0, down_1, down_passed, down_own,
    rows, incoming, both_grad, inner,
):
    ordered((n0, n1, n2, n3, n4, n5), rows)
    ordered((c0, c1, c2, c3, c4, c5), incoming)
    for first in range(0, FF_Z, BLOCK):
        columns, second = slice(first, first + BLOCK), slice(FF_Z + first, FF_Z + first + BLOCK)
        third = slice(2 * FF_Z + first, 2 * FF_Z + first + BLOCK)
        gate = product(rows[...], weights[:, columns])
        up = product(rows[...], weights[:, second])
        inner_grad = product(incoming[...], weights[:, third])
        sigmoid = jax.nn.sigmoid(gate)
        swish = gate * sigmoid
        inner[:, columns] = (swish * up).astype(jnp.bfloat16)
        both_grad[:, columns] = (
            inner_grad * up * sigmoid * (1.0 + gate * (1.0 - sigmoid))
        ).astype(jnp.bfloat16)
        both_grad[:, second] = (inner_grad * swish).astype(jnp.bfloat16)
    send_order(contract(both_grad[...], weights[:, : 2 * FF_Z]), first_0, first_1, passed, own)
    for values in (first_0, first_1, passed, own):
        values.send()
    send_order(
        contract(inner[...], weights[:, 2 * FF_Z :]), down_0, down_1, down_passed, down_own
    )
    for values in (down_0, down_1, down_passed, down_own):
        values.send()
    for first in range(0, D, BLOCK):
        goal = slice(first, first + BLOCK)
        share[goal, : 2 * FF_Z] = outer_rows(rows[:, goal], both_grad[...]).astype(jnp.bfloat16)
        share[goal, 2 * FF_Z :] = outer_rows(incoming[:, goal], inner[...]).astype(jnp.bfloat16)
        share.send(goal)


def weighed(*pairs):
    return functools.reduce(
        jnp.add,
        [
            jnp.sum(grad[...] * weight[...].astype(jnp.float32), axis=1, keepdims=True)
            for grad, weight in pairs
        ],
    )


def as_row(column):
    return jnp.broadcast_to(column, (OWN, HEAD)).T[0:1, :]


def last_kernel(
    at, p0, p1, p2, p3, p4, p5, mlp, w_query, w_key, w_value, norm, w_gate, w_up, norm_post,
    query, key, value, output_t, norm_grad, query_gain, key_gain, gate, up, down_t, post_grad,
):
    z, x_hi = at[0], at[1]
    pieces = (p0, p1, p2, p3, p4, p5)
    each = HEAD // N_FSDP
    gain_total = jnp.zeros((8, HEAD), jnp.float32)
    for array, step, relative, color in PIECES:
        begin = step * OWN
        part = pieces[array][begin : begin + OWN, :].astype(jnp.float32)
        place, theirs = z ^ relative, x_hi ^ color
        head = 2 * place + theirs
        one = pl.ds(pl.multiple_of(head * HEAD, HEAD), HEAD)
        two = pl.ds(pl.multiple_of(head * 2 * HEAD, 2 * HEAD), 2 * HEAD)
        query[:, two] = part[:, : 2 * HEAD]
        key[:, one] = part[:, 2 * HEAD : 3 * HEAD]
        value[:, one] = part[:, 3 * HEAD : 4 * HEAD]
        for other in range(2):
            goal = (2 * place + (theirs ^ other)) * 2 * HEAD
            goal = pl.ds(pl.multiple_of(goal, 2 * HEAD), 2 * HEAD)
            first = UNIT + other * 2 * HEAD
            share = part[:, first : first + 2 * HEAD]
            output_t[:, goal] = share if color == 0 else output_t[:, goal] + share
        gain_total += part[0:8, 2 * UNIT :]
    for result in (query, key, value, output_t):
        result.send()
    query_gain[...] = gain_total[0:1, :each]
    key_gain[...] = gain_total[0:1, each : 2 * each]
    for place in range(Z):
        part = mlp[place].astype(jnp.float32)
        columns = slice(place * FF_Z, (place + 1) * FF_Z)
        gate[:, columns] = part[:, :FF_Z]
        up[:, columns] = part[:, FF_Z : 2 * FF_Z]
        down_t[:, columns] = part[:, 2 * FF_Z :]
    for result in (gate, up, down_t):
        result.send()
    norm_grad[...] = as_row(weighed((query, w_query), (key, w_key), (value, w_value)) / norm[...])
    post_grad[...] = as_row(weighed((gate, w_gate), (up, w_up)) / norm_post[...])


class Writing:
    def __init__(self, place, goal, semaphores):
        self.place, self.goal, self.semaphores, self.copies = place, goal, semaphores, []
        self.shape = place.shape

    def __getitem__(self, index):
        return self.place[index]

    def __setitem__(self, index, values):
        self.place[index] = values

    def send(self, rows=slice(None)):
        copy = pltpu.make_async_copy(self.place.at[rows], self.goal.at[rows], next(self.semaphores))
        copy.start()
        self.copies.append(copy)


def kernel_call(kernel, inputs, outs, scratch=(), flops=0, cuts=None, raw_outs=0):
    cuts = cuts or {}
    n_in, n_out, n_sent = len(inputs), len(outs), 24

    def shape(i):
        return (inputs[i].shape[0], cuts[i][1]) if i in cuts else inputs[i].shape

    copied = [i for i, x in enumerate(inputs) if x.ndim > 1]
    buffers = [pltpu.VMEM(shape(i), inputs[i].dtype) for i in copied]
    out_buffers = [pltpu.VMEM(size, dtype) for size, dtype in outs[raw_outs:]]

    def body(*refs):
        ins, results, rest = refs[:n_in], refs[n_in : n_in + n_out], refs[n_in + n_out :]
        places, rest = rest[: len(buffers)], rest[len(buffers) :]
        out_places, rest = rest[: len(out_buffers)], rest[len(out_buffers) :]
        (arrived, sent), rest = rest[:2], rest[2:]
        args, copies = list(ins), []
        for i, place in zip(copied, places):
            source = ins[i].at[:, pl.ds(*cuts[i])] if i in cuts else ins[i]
            copies.append(pltpu.make_async_copy(source, place, arrived.at[i]))
            args[i] = place
        for copy in copies:
            copy.start()
        for copy in copies:
            copy.wait()
        semaphores = iter([sent.at[i] for i in range(n_sent)])
        writes = [Writing(p, g, semaphores) for p, g in zip(out_places, results[raw_outs:])]
        kernel(*args, *results[:raw_outs], *writes, *rest)
        for write in writes:
            if not write.copies:
                write.send()
        for write in writes:
            for copy in write.copies:
                copy.wait()

    anywhere, scalars = pl.BlockSpec(memory_space=pltpu.HBM), pl.BlockSpec(memory_space=pltpu.SMEM)
    return pl.pallas_call(
        body,
        out_shape=[jax.ShapeDtypeStruct(shape, dtype) for shape, dtype in outs],
        in_specs=[anywhere if x.ndim > 1 else scalars for x in inputs],
        out_specs=[anywhere] * n_out,
        scratch_shapes=[
            *buffers,
            *out_buffers,
            pltpu.SemaphoreType.DMA((n_in,)),
            pltpu.SemaphoreType.DMA((n_sent,)),
            *(x if not isinstance(x, tuple) else pltpu.VMEM(*x) for x in scratch),
        ],
        compiler_params=pltpu.CompilerParams(vmem_limit_bytes=GRANT * MEGA),
        cost_estimate=pl.CostEstimate(flops=flops, bytes_accessed=8 * MEGA, transcendentals=0),
    )(*inputs)


def per_device(
    tokens,
    segments,
    norm_input,
    w_query,
    w_key,
    w_value,
    norm_query,
    norm_key,
    w_output,
    norm_post,
    w_gate,
    w_up,
    w_down,
    cotangent,
):
    bf16, f32 = jnp.bfloat16, jnp.float32
    s, f = lax.axis_index("seq"), lax.axis_index("fsdp")
    z, x_hi = s // 2, s % 2
    at = jnp.stack([z, x_hi, f // 4, (f // 2) % 2, f % 2]).astype(jnp.int32)
    sequence = tokens[0]
    table = rotation()
    ids = segments[0]
    first_key = jnp.sum((ids[None, :] < ids[:, None]).astype(jnp.int32), axis=1).reshape(1, LENGTH)

    other_rows = swap_x_hi(sequence)

    def spread(values):
        wide = jnp.tile(values, N_FSDP)
        owner = jnp.arange(wide.shape[0], dtype=jnp.int32) // values.shape[0]
        return jnp.where(owner == f, wide, jnp.zeros_like(wide))

    def my_columns(values, width):
        return lax.dynamic_slice_in_dim(values, s * width, width, 1)

    rest = jnp.zeros((UNIT - 2 * HEAD,), bf16)
    extra = jnp.concatenate(
        [spread(norm_input), spread(norm_post), spread(norm_query), spread(norm_key), rest]
    ).reshape(5, UNIT)
    extra = jnp.pad(extra, ((0, EXTRA - 5), (0, 0)))
    my_unit = jnp.concatenate(
        [my_columns(w_query, 2 * HEAD), my_columns(w_key, HEAD), my_columns(w_value, HEAD)], axis=1
    )
    piece = lax.optimization_barrier(jnp.concatenate([my_unit, extra], axis=0))
    pair = jnp.concatenate([piece, swap_core(piece)], axis=0)
    other_pair = jnp.concatenate([swap_x_lo(piece), swap_chip(piece)], axis=0)
    pair, other_pair = lax.optimization_barrier((pair, other_pair))
    pair_1, other_pair_1 = swap_y_a(pair), swap_y_b(other_pair)

    pair_2 = swap_y_b(jnp.concatenate([pair, pair_1], axis=0))
    other_pair_2 = swap_y_a(jnp.concatenate([other_pair, other_pair_1], axis=0))
    unit_pieces = (pair, pair_1, pair_2, other_pair, other_pair_1, other_pair_2)
    rows_1 = swap_z_a(sequence)
    rows_2 = swap_z_b(jnp.concatenate([sequence, rows_1], axis=0))
    token_pieces = (
        sequence,
        rows_1,
        rows_2,
        other_rows,
        swap_z_a(other_rows),
        swap_z_b(other_rows),
        swap_z_both(other_rows),
    )

    def slice_z(values):
        return lax.dynamic_slice_in_dim(values, z * FF_Z, FF_Z, 1)

    later = jnp.concatenate(
        [w_output.T, slice_z(w_gate), slice_z(w_up), slice_z(w_down.T)], axis=1
    )
    later = lax.all_gather(later, "fsdp", axis=0, tiled=True)

    turned, normed, raw, heads, mixed, log_total, gains, weight = kernel_call(
        front_kernel,
        (at, *unit_pieces, *token_pieces, table, first_key),
        (
            ((2, Z, ROWS, 2 * HEAD), bf16),
            ((LENGTH, D), bf16),
            ((LENGTH, 3 * HEAD), f32),
            ((LENGTH, UNIT), bf16),
            ((LENGTH, 2 * HEAD), bf16),
            ((8, LENGTH), f32),
            ((8, D), f32),
            ((D, UNIT), bf16),
        ),
        scratch=(((HEAD, LENGTH), bf16), pltpu.SemaphoreType.DMA((8,))),
        flops=4 * 10**9,
        raw_outs=1,
    )

    mixed_tokens = lax.all_to_all(
        mixed.reshape(N_SEQ, ROWS, 2 * HEAD), "seq", split_axis=0, concat_axis=0, tiled=True
    )
    incoming = after(cotangent[0], mixed)
    cotangent_z = gather4(*halves(incoming), swap_z_a, swap_z_b)
    half_rows = ((ROWS // 2, D), bf16)
    hidden, upper, lower = kernel_call(
        out_kernel,
        (mixed_tokens, sequence, gains, later),
        (((ROWS, D), f32), half_rows, half_rows),
        scratch=(((ROWS, 2 * D), bf16),),
        flops=10**9,
        cuts={3: (0, 2 * D)},
    )
    upper, lower = after((upper, lower), cotangent_z)
    normed_post_z = gather4(upper, lower, swap_z_a, swap_z_b)
    sent = (((ROWS, D), bf16), ((ROWS, D), bf16), ((ROWS, D), f32), ((ROWS, D), f32))
    first_0, first_1, passed, own, mlp_share, down_0, down_1, down_passed, down_own = kernel_call(
        mlp_kernel,
        (*normed_post_z, *cotangent_z, later),
        (*sent, ((D, 3 * FF_Z), bf16), *sent),
        scratch=(
            ((Z * ROWS, D), bf16),
            ((Z * ROWS, D), bf16),
            ((Z * ROWS, 2 * FF_Z), bf16),
            ((Z * ROWS, FF_Z), bf16),
        ),
        flops=8 * 10**9,
        cuts={12: (2 * D, 3 * FF_Z)},
    )
    turned = after(turned, first_0).reshape(2, Z * ROWS, 2 * HEAD)
    mixed_mine, mixed_other = turned[0], swap_x_hi(turned[1])
    sums = scatter4(first_0, first_1, *halves(passed), swap_z_a, swap_z_b)
    (got_0, got_1, last_0, last_1), mixed_other = lax.optimization_barrier((sums, mixed_other))
    mlp_share = lax.psum_scatter(mlp_share, "fsdp", scatter_dimension=0, tiled=True)
    hidden_grad, upper, lower, mixed_grad = kernel_call(
        mid_kernel,
        (own, got_0, got_1, last_0, last_1, hidden, cotangent[0], gains, later),
        (((ROWS, D), f32), half_rows, half_rows, ((N_SEQ, ROWS, 2 * HEAD), bf16)),
        flops=10**9,
        cuts={8: (0, 2 * D)},
    )
    mixed_grad = lax.all_to_all(mixed_grad, "seq", split_axis=0, concat_axis=0, tiled=True)
    proj_grad_z = gather4(upper, lower, swap_z_a, swap_z_b)
    down_0, down_1 = after((down_0, down_1), proj_grad_z)
    down_got = swap_z_b(down_0), swap_z_a(down_1)

    share, share_sent, dx_0, dx_1, dx_passed, dx_own = kernel_call(
        back_kernel,
        (
            at, heads, mixed_grad.reshape(LENGTH, 2 * HEAD), first_key, log_total, raw, table, gains,
            weight, normed, mixed_mine, mixed_other, *proj_grad_z,
        ),
        (
            ((Z, 2, OWN, SHARE), bf16),
            ((Z, 2, OWN, SHARE), bf16),
            ((2 * ROWS, D), bf16),
            ((2 * ROWS, D), bf16),
            ((2 * ROWS, D), f32),
            ((2 * ROWS, D), f32),
        ),
        scratch=(
            ((LENGTH, UNIT), bf16),
            ((HEAD, LENGTH), bf16),
            ((LENGTH, HEAD), f32),
            ((LENGTH, HEAD), f32),
            ((LENGTH, 2 * HEAD), f32),
            ((8, HEAD), f32),
            ((Z * ROWS, D), bf16),
            ((Z * ROWS, UNIT), bf16),
            ((2, Z, 2, OWN, SHARE), bf16),
            ((LENGTH, UNIT), bf16),
            pltpu.SemaphoreType.DMA((2,)),
        ),
        flops=8 * 10**9,
        raw_outs=2,
    )
    share, share_sent, dx_0, dx_1 = after((share, share_sent, dx_0, dx_1), down_got)
    share = share.reshape(D // 2, SHARE)
    other_share = swap_core(share_sent.reshape(D // 2, SHARE))

    def share_block(relative, color):
        begin = (2 * relative + color) * OWN
        mine, other = share[begin : begin + OWN], other_share[begin : begin + OWN]
        return mine.astype(f32) + other.astype(f32)

    def share_pair(one, two):
        return jnp.concatenate([share_block(*one), share_block(*two)], axis=0).astype(bf16)

    dx_got = swap_z_b(dx_0), swap_z_a(dx_1)
    share_got = (
        swap_y_b(share_pair((3, 0), (2, 0))),
        swap_y_a(share_pair((1, 1), (2, 1))),
    )
    dx_got, share_got = lax.optimization_barrier((dx_got, share_got))

    def second(got, passed_0, passed_1, swap_a, swap_b):
        n = got[0].shape[0] // 2
        last_0 = swap_a((passed_0 + wide(got[0][n:])).astype(bf16))
        last_1 = swap_b((passed_1 + wide(got[1][n:])).astype(bf16))
        return *got, last_0, last_1

    share_parts = second(share_got, share_block(1, 0), share_block(3, 1), swap_y_a, swap_y_b)
    dx_parts = second(dx_got, *halves(dx_passed), swap_z_a, swap_z_b)
    mlp_other = swap_x_hi(mlp_share)
    share_parts, dx_parts, mlp_other = lax.optimization_barrier((share_parts, dx_parts, mlp_other))
    mlp_pieces = gather_z((wide(mlp_share) + wide(mlp_other)).astype(bf16))
    share_0, share_1 = total4(share_block(0, 0), share_block(0, 1), *share_parts)
    share_0, share_1 = share_0.astype(bf16), share_1.astype(bf16)
    normed_grad, other_grad = total4(*halves(dx_own), *dx_parts)
    other_grad = other_grad.astype(bf16)
    share_0, share_1 = lax.optimization_barrier((share_0, share_1))
    attn_share = (share_0.astype(f32) + swap_x_lo(share_1).astype(f32)).astype(bf16)
    other_attn = swap_x_hi(share_0).astype(f32) + swap_x_both(share_1).astype(f32)
    other_attn = other_attn.astype(bf16)
    attn_share, other_attn = lax.optimization_barrier((attn_share, other_attn))
    other_grad = swap_x_hi(after(other_grad, attn_share))
    normed_grad = (normed_grad + other_grad.astype(f32)) * gains[0:1]
    widened = sequence.astype(f32)
    inverse = inverse_norm(widened)
    unit_input = widened * inverse
    tokens_grad = hidden_grad + inverse * (
        normed_grad - unit_input * jnp.mean(unit_input * normed_grad, axis=-1, keepdims=True)
    )

    last_pieces = gather4(attn_share, other_attn, swap_z_a, swap_z_b)
    down_got = after(down_got, last_pieces[1])
    down_parts = second(down_got, *halves(down_passed), swap_z_a, swap_z_b)
    result = hidden + jnp.concatenate(total4(*halves(down_own), *down_parts), axis=0)
    result = result.astype(bf16)

    last_pieces = after(last_pieces, mlp_pieces)
    (
        query_total, key_total, value_total, output_total, input_gain, query_gain, key_gain,
        gate_total, up_total, down_total, post_gain,
    ) = kernel_call(
        last_kernel,
        (
            at, *last_pieces, mlp_pieces,
            w_query, w_key, w_value, norm_input.astype(f32).reshape(OWN, 1),
            w_gate, w_up, norm_post.astype(f32).reshape(OWN, 1),
        ),
        (
            ((OWN, 2 * D), f32),
            ((OWN, D), f32),
            ((OWN, D), f32),
            ((OWN, 2 * D), f32),
            ((1, OWN), f32),
            ((1, HEAD // N_FSDP), f32),
            ((1, HEAD // N_FSDP), f32),
            ((OWN, FF), f32),
            ((OWN, FF), f32),
            ((OWN, FF), f32),
            ((1, OWN), f32),
        ),
    )
    return (
        result[None],
        tokens_grad[None],
        input_gain[0],
        query_total,
        key_total,
        value_total,
        query_gain[0],
        key_gain[0],
        output_total.T,
        post_gain[0],
        gate_total,
        up_total,
        down_total.T,
    )


def solution(mesh):
    rows, columns, tokens = P("fsdp", None), P(None, "fsdp"), P("fsdp", "seq", None)
    in_specs = (
        tokens, rows, P("fsdp"), rows, rows, rows, P("fsdp"), P("fsdp"), columns, P("fsdp"),
        rows, rows, columns, tokens,
    )
    out_specs = (
        tokens, tokens, P("fsdp"), rows, rows, rows, P("fsdp"), P("fsdp"), columns, P("fsdp"),
        rows, rows, columns,
    )
    return jax.shard_map(
        per_device, mesh=mesh, in_specs=in_specs, out_specs=out_specs, check_vma=False
    )
```

```python
import functools
import math

import jax
import jax.numpy as jnp
import numpy as np
from jax import lax
from jax.experimental import pallas as pl
from jax.experimental.pallas import tpu as pltpu
from jax.sharding import PartitionSpec as P

HEAD = 128
D = 1024
FF = 3072
LENGTH = 1024
ROWS = 128
N_SEQ = 8
N_FSDP = 16
Z = 4
OWN = D // N_FSDP
FF_Z = FF // Z
UNIT = 512
BLOCK = 256
EXTRA = 16
SHARE = 2 * UNIT + HEAD
MEGA = 1 << 20
GRANT = 60

TOKEN_PIECES = (
    (0, 0, 0, 0),
    (3, 0, 0, 1),
    (1, 0, 1, 0),
    (2, 0, 3, 0),
    (2, 1, 2, 0),
    (4, 0, 1, 1),
    (5, 0, 3, 1),
    (6, 0, 2, 1),
)

EPSILON = 1e-06
THETA = 1000000.0
NEGATIVE = -1e30
SCALE = 1.0 / math.sqrt(HEAD)

PIECES = (
    (0, 0, 0, 0),
    (1, 0, 1, 0),
    (2, 0, 3, 0),
    (2, 1, 2, 0),
    (3, 0, 0, 1),
    (4, 0, 3, 1),
    (5, 0, 1, 1),
    (5, 1, 2, 1),
)


def exchange(values, axis, bits):
    size = N_SEQ if axis == "seq" else N_FSDP
    return lax.ppermute(values, axis, [(i, i ^ bits) for i in range(size)])


swap_x_hi = functools.partial(exchange, axis="seq", bits=1)
swap_z_a = functools.partial(exchange, axis="seq", bits=2)
swap_z_b = functools.partial(exchange, axis="seq", bits=6)
swap_z_both = functools.partial(exchange, axis="seq", bits=4)
swap_core = functools.partial(exchange, axis="fsdp", bits=1)
swap_x_lo = functools.partial(exchange, axis="fsdp", bits=2)
swap_chip = functools.partial(exchange, axis="fsdp", bits=3)


def swap_x_both(values):
    places = [(i, j) for i in range(N_SEQ) for j in range(N_FSDP)]
    pairs = [(i * N_FSDP + j, (i ^ 1) * N_FSDP + (j ^ 2)) for i, j in places]
    return lax.ppermute(values, ("seq", "fsdp"), pairs)


swap_y_a = functools.partial(exchange, axis="fsdp", bits=4)
swap_y_b = functools.partial(exchange, axis="fsdp", bits=12)


def after(values, *others):
    return lax.optimization_barrier((values, *others))[0]


def gather4(zero, one, swap_a, swap_b):
    zero_1 = swap_a(zero)
    one_1 = swap_b(one)
    zero_2 = swap_b(jnp.concatenate([zero, zero_1], axis=0))
    one_2 = swap_a(jnp.concatenate([one, one_1], axis=0))
    return zero, zero_1, zero_2, one, one_1, one_2


def gather_z(values):
    groups = [[2 * z + x_hi for z in range(Z)] for x_hi in range(2)]
    return lax.all_gather(values, "seq", axis=0, tiled=False, axis_index_groups=groups)


def halves(rows):
    middle = rows.shape[0] // 2
    return rows[:middle], rows[middle:]


def scatter4(first_0, first_1, passed_0, passed_1, swap_a, swap_b, tie=None):
    got_0, got_1 = swap_b(first_0), swap_a(first_1)
    if tie is not None:
        got_0, got_1 = tie(got_0, got_1)
    n = got_0.shape[0] // 2
    last_0 = swap_a((passed_0 + got_0[n:].astype(jnp.float32)).astype(jnp.bfloat16))
    last_1 = swap_b((passed_1 + got_1[n:].astype(jnp.float32)).astype(jnp.bfloat16))
    return got_0[:n], got_1[:n], last_0, last_1


def total4(own_0, own_1, got_0, got_1, last_0, last_1):
    n = own_0.shape[0]
    mine_0 = own_0 + wide(got_0[:n]) + wide(last_0)
    mine_1 = own_1 + wide(got_1[:n]) + wide(last_1)
    return mine_0, mine_1


def wide(values):
    return values.astype(jnp.float32)


def rotation():
    frequency = THETA ** -(np.arange(0, HEAD, 2, dtype=np.float64) / HEAD)
    angles = np.arange(LENGTH, dtype=np.float64)[:, None] * frequency[None, :]
    return jnp.asarray(np.concatenate([np.cos(angles), np.sin(angles)], axis=1).astype(np.float32))


def turns(table):
    turned = pltpu.roll(table, HEAD // 2, 1)
    low = lax.broadcasted_iota(jnp.int32, table.shape, 1) < HEAD // 2
    return jnp.where(low, table, turned), jnp.where(low, -turned, table)


def contract(left, right):
    return lax.dot_general(
        left, right, (((1,), (1,)), ((), ())), preferred_element_type=jnp.float32
    )


def outer_rows(left, right):
    return lax.dot_general(
        left, right, (((0,), (0,)), ((), ())), preferred_element_type=jnp.float32
    )


def product(left, right):
    return jnp.dot(left, right, preferred_element_type=jnp.float32)


def inverse_norm(values):
    return lax.rsqrt(jnp.mean(values * values, axis=-1, keepdims=True) + EPSILON)


def allowed_scores(scores, first_key, begin):
    first = first_key[:, begin : begin + BLOCK]
    place = (BLOCK, BLOCK)
    key, query = lax.broadcasted_iota(jnp.int32, place, 0), lax.broadcasted_iota(jnp.int32, place, 1)
    diagonal = jnp.where((key <= query) & (key + begin >= first), scores[begin:], NEGATIVE)
    if begin == 0:
        return [(0, diagonal)]
    key = lax.broadcasted_iota(jnp.int32, (begin, BLOCK), 0)
    return [(0, jnp.where(key >= first, scores[:begin], NEGATIVE)), (begin, diagonal)]


def front_kernel(
    at, w0, w1, w2, w3, w4, w5, x0, x1, x2, x3, x4, x5, x6, table, first_key,
    turned, normed, raw, heads, mixed, log_total, gains, weight, value_t, arrived,
):
    z, x_hi, y, x_lo, core = at[0], at[1], at[2], at[3], at[4]
    weights = (w0, w1, w2, w3, w4, w5)
    extra = jnp.zeros((EXTRA, UNIT), jnp.float32)
    for array, step, relative, color in PIECES:
        for other in range(2):
            first = (2 * step + other) * (OWN + EXTRA)
            owner = 4 * (y ^ relative) + 2 * (x_lo ^ color) + (core ^ other)
            weight[pl.ds(pl.multiple_of(owner * OWN, OWN), OWN), :] = weights[array][
                first : first + OWN, :
            ]
            extra += weights[array][first + OWN : first + OWN + EXTRA, :].astype(jnp.float32)
    gain = jnp.concatenate([extra[0:1], extra[1:2]], axis=1)
    gains[...] = jnp.zeros(gains.shape, jnp.float32)
    gains[0:1, :] = gain
    gains[1:2, :] = jnp.concatenate([extra[2:3], extra[3:4]], axis=1)
    gains[2:3, 0:UNIT] = extra[4:5]
    table, *tokens = ready(table, x0, x1, x2, x3, x4, x5, x6)
    for array, step, relative, color in TOKEN_PIECES:
        values = tokens[array][step * ROWS : (step + 1) * ROWS, :].astype(jnp.float32)
        place = (2 * (z ^ relative) + (x_hi ^ color)) * ROWS
        normed[pl.ds(pl.multiple_of(place, ROWS), ROWS), :] = (
            values * inverse_norm(values) * gain
        ).astype(jnp.bfloat16)
    normed.send()
    weight.send()
    gain_query, gain_key = extra[4:5, :HEAD], extra[4:5, HEAD : 2 * HEAD]
    for begin in range(0, LENGTH, BLOCK):
        rows = slice(begin, begin + BLOCK)
        projected = product(normed[rows, :], weight[...])
        cosine, sine = turns(table[rows, :])
        raw[rows, :] = projected[:, : 3 * HEAD]
        for head, head_gain in enumerate((gain_query, gain_query, gain_key)):
            part = projected[:, head * HEAD : (head + 1) * HEAD]
            part = part * inverse_norm(part) * head_gain
            part = part * cosine + pltpu.roll(part, HEAD // 2, 1) * sine
            heads[rows, head * HEAD : (head + 1) * HEAD] = part.astype(jnp.bfloat16)
        value = projected[:, 3 * HEAD :]
        heads[rows, 3 * HEAD :] = value.astype(jnp.bfloat16)
        value_t[:, rows] = value.T.astype(jnp.bfloat16)
    raw.send()
    heads.send()
    key = slice(2 * HEAD, 3 * HEAD)
    for begin in range(0, LENGTH, BLOCK):
        rows, end = slice(begin, begin + BLOCK), begin + BLOCK
        for head in range(2):
            columns = slice(head * HEAD, (head + 1) * HEAD)
            scores = contract(heads[:end, key], heads[rows, columns]) * SCALE
            parts = allowed_scores(scores, first_key, begin)
            highest = functools.reduce(
                jnp.maximum, [jnp.max(s, axis=0, keepdims=True) for _, s in parts]
            )
            total, result = 0.0, 0.0
            for first, s in parts:
                weights_now = jnp.exp(s - highest)
                total += jnp.sum(weights_now, axis=0, keepdims=True)
                result += product(
                    value_t[:, first : first + s.shape[0]], weights_now.astype(jnp.bfloat16)
                )
            log_total[head : head + 1, rows] = highest + jnp.log(total)
            mixed[rows, columns] = (result / total).T.astype(jnp.bfloat16)
        mixed.send(rows)
        for part in range(2):
            i = begin // ROWS + part
            goal = turned.at[part ^ x_hi, (begin // BLOCK) ^ z]
            copy = pltpu.make_async_copy(
                mixed.place.at[i * ROWS : (i + 1) * ROWS], goal, arrived.at[i]
            )
            copy.start()
            mixed.copies.append(copy)


def back_kernel(
    at, heads, grad, first_key, log_total, raw, table, gains, weight,
    normed, mixed_mine, mixed_other, p0, p1, p2, p3, p4, p5,
    mine, theirs, first_0, first_1, passed, own, back, key_t, key_sum, value_sum, query_sum,
    gain_grads, proj, mixed, share, turned, done,
):
    key, value = slice(2 * HEAD, 3 * HEAD), slice(3 * HEAD, 4 * HEAD)
    key_t[...] = heads[:, key].astype(jnp.float32).T.astype(jnp.bfloat16)
    key_sum[...] = jnp.zeros_like(key_sum)
    value_sum[...] = jnp.zeros_like(value_sum)
    for start in range(0, LENGTH, BLOCK):
        rows, end = slice(start, start + BLOCK), start + BLOCK
        for head in range(2):
            columns = slice(head * HEAD, (head + 1) * HEAD)
            query, rows_grad = heads[rows, columns], grad[rows, columns]
            scores = contract(heads[:end, key], query) * SCALE
            prob_grad = contract(heads[:end, value], rows_grad)
            log_now = log_total[head : head + 1, rows]
            parts, mean = [], 0.0
            for first, s in allowed_scores(scores, first_key, start):
                prob = jnp.exp(s - log_now)
                pulled = prob_grad[first : first + s.shape[0]]
                mean += jnp.sum(prob * pulled, axis=0, keepdims=True)
                parts.append((first, prob, pulled))
            query_part = 0.0
            for first, prob, pulled in parts:
                keys = slice(first, first + prob.shape[0])
                score_grad = (prob * (pulled - mean)).astype(jnp.bfloat16)
                value_sum[keys, :] += product(prob.astype(jnp.bfloat16), rows_grad)
                key_sum[keys, :] += product(score_grad, query)
                query_part += product(key_t[:, keys], score_grad)
            query_sum[rows, columns] = query_part.T
    back[:, value] = value_sum[...].astype(jnp.bfloat16)
    gain_grads[...] = jnp.zeros(gain_grads.shape, jnp.float32)
    for head in range(3):
        columns = slice(head * HEAD, (head + 1) * HEAD)
        which = 0 if head < 2 else 1
        gain = gains[2:3, which * HEAD : (which + 1) * HEAD]
        for start in range(0, LENGTH, BLOCK):
            rows = slice(start, start + BLOCK)
            cosine, sine = turns(table[rows, :])
            pulled = (query_sum[rows, columns] if head < 2 else key_sum[rows, :]) * SCALE
            pulled = pulled.astype(jnp.bfloat16).astype(jnp.float32)
            pulled = pulled * cosine - pltpu.roll(pulled, HEAD // 2, 1) * sine
            part = raw[rows, columns]
            inverse = inverse_norm(part)
            unit = part * inverse
            gain_grads[which : which + 1, :] += jnp.sum(pulled * unit, axis=0, keepdims=True)
            pulled = pulled * gain
            mean = jnp.mean(unit * pulled, axis=-1, keepdims=True)
            back[rows, columns] = (inverse * (pulled - unit * mean)).astype(jnp.bfloat16)

    z, x_hi = at[0], at[1]
    for relative in range(Z):
        for color in range(2):
            place = (2 * (z ^ relative) + (x_hi ^ color)) * ROWS
            goal = (2 * relative + color) * ROWS
            turned[goal : goal + ROWS, :] = back[pl.ds(pl.multiple_of(place, ROWS), ROWS), :]
    send_order(contract(turned[...], weight[...]), first_0, first_1, passed, own)
    for values in (first_0, first_1, passed, own):
        values.send()
    y, x_lo, core = at[2], at[3], at[4]
    normed, mixed_mine, mixed_other, *pieces = ready(
        normed, mixed_mine, mixed_other, p0, p1, p2, p3, p4, p5
    )
    ordered(pieces, proj)
    mixed[:, : 2 * HEAD] = mixed_mine[...]
    mixed[:, 2 * HEAD :] = mixed_other[...]
    lane = lax.broadcasted_iota(jnp.int32, (OWN, HEAD), 1)
    line = lax.broadcasted_iota(jnp.int32, (OWN, HEAD), 0)
    each = HEAD // N_FSDP
    copies = []
    for start in range(0, D, BLOCK):
        goal = slice(start, start + BLOCK)
        attn = outer_rows(normed[:, goal], back[...]).astype(jnp.bfloat16)
        output = outer_rows(proj[:, goal], mixed[...]).astype(jnp.bfloat16)
        for part in range(BLOCK // OWN):
            owner = start // OWN + part
            query_gain = pltpu.roll(gain_grads[0:1, :], (HEAD - each * owner) % HEAD, 1)
            key_gain = pltpu.roll(gain_grads[1:2, :], (HEAD + each - each * owner) % HEAD, 1)
            head_gains = jnp.where(lane < each, query_gain, key_gain)
            head_gains = jnp.where((line == 0) & (lane < 2 * each), head_gains, 0.0)
            rows = slice(part * OWN, (part + 1) * OWN)
            place = ((owner % 2) ^ core, (owner // 4) ^ y, ((owner // 2) % 2) ^ x_lo)
            share[(*place, slice(None), slice(0, UNIT))] = attn[rows]
            share[(*place, slice(None), slice(UNIT, 2 * UNIT))] = output[rows]
            share[(*place, slice(None), slice(2 * UNIT, SHARE))] = head_gains.astype(jnp.bfloat16)
        which = (start // BLOCK) ^ y
        for i, goal in ((1, theirs), (0, mine)):
            copy = pltpu.make_async_copy(
                share.at[i, which], goal.at[which], done.at[2 * (start // BLOCK) + i]
            )
            copy.start()
            copies.append(copy)
    for copy in copies:
        copy.wait()


def out_kernel(mixed, tokens, gains, weights, hidden, upper, lower, rows):
    for head in range(N_SEQ):
        rows[:, head * 2 * HEAD : (head + 1) * 2 * HEAD] = mixed[head]
    values = tokens[...].astype(jnp.float32) + contract(rows[...], weights[...])
    hidden[...] = values
    values = (values * inverse_norm(values) * gains[1:2, :]).astype(jnp.bfloat16)
    upper[...] = values[: ROWS // 2]
    lower[...] = values[ROWS // 2 :]


def mid_kernel(
    own, got_0, got_1, last_0, last_1, hidden, incoming, gains, weights,
    hidden_grad, upper, lower, mixed_grad,
):
    half = ROWS // 2
    total_0 = own[:half, :] + got_0[...].astype(jnp.float32) + last_0[...].astype(jnp.float32)
    total_1 = own[half:, :] + got_1[...].astype(jnp.float32) + last_1[...].astype(jnp.float32)
    pulled = jnp.concatenate([total_0, total_1], axis=0) * gains[1:2, :]
    inverse = inverse_norm(hidden[...])
    unit = hidden[...] * inverse
    mean = jnp.mean(unit * pulled, axis=-1, keepdims=True)
    grad = incoming[...].astype(jnp.float32) + inverse * (pulled - unit * mean)
    hidden_grad[...] = grad
    grad = grad.astype(jnp.bfloat16)
    upper[...] = grad[:half]
    lower[...] = grad[half:]
    for head in range(N_SEQ):
        mixed_grad[head] = product(grad, weights[:, head * 2 * HEAD : (head + 1) * 2 * HEAD]).astype(jnp.bfloat16)


def ordered(pieces, place):
    half = pieces[0].shape[0]
    for array, step, relative, color in PIECES:
        begin = (2 * relative + color) * half
        place[begin : begin + half, :] = pieces[array][step * half : (step + 1) * half, :]


def send_order(values, first_0, first_1, passed, own):
    half = values.shape[0] // 8

    def block(relative, color):
        begin = (2 * relative + color) * half
        return values[begin : begin + half]

    first_0[:half, :] = block(3, 0).astype(jnp.bfloat16)
    first_0[half:, :] = block(2, 0).astype(jnp.bfloat16)
    first_1[:half, :] = block(1, 1).astype(jnp.bfloat16)
    first_1[half:, :] = block(2, 1).astype(jnp.bfloat16)
    passed[:half, :] = block(1, 0)
    passed[half:, :] = block(3, 1)
    own[:half, :] = block(0, 0)
    own[half:, :] = block(0, 1)


def mlp_kernel(
    n0, n1, n2, n3, n4, n5, c0, c1, c2, c3, c4, c5, weights, down_weights,
    first_0, first_1, passed, own, share, down_0, down_1, down_passed, down_own,
    rows, incoming, both_grad, inner,
):
    ordered((n0, n1, n2, n3, n4, n5), rows)
    for first in range(0, FF_Z, BLOCK):
        columns, second = slice(first, first + BLOCK), slice(FF_Z + first, FF_Z + first + BLOCK)
        gate = product(rows[...], weights[:, columns])
        up = product(rows[...], weights[:, second])
        if first == 0:
            down_weights, *pieces = ready(down_weights, c0, c1, c2, c3, c4, c5)
            ordered(pieces, incoming)
        inner_grad = product(incoming[...], down_weights[:, columns])
        sigmoid = jax.nn.sigmoid(gate)
        swish = gate * sigmoid
        inner[:, columns] = (swish * up).astype(jnp.bfloat16)
        both_grad[:, columns] = (
            inner_grad * up * sigmoid * (1.0 + gate * (1.0 - sigmoid))
        ).astype(jnp.bfloat16)
        both_grad[:, second] = (inner_grad * swish).astype(jnp.bfloat16)
    send_order(contract(both_grad[...], weights[...]), first_0, first_1, passed, own)
    for values in (first_0, first_1, passed, own):
        values.send()
    send_order(
        contract(inner[...], down_weights[...]), down_0, down_1, down_passed, down_own
    )
    for values in (down_0, down_1, down_passed, down_own):
        values.send()
    for first in range(0, D, BLOCK):
        goal = slice(first, first + BLOCK)
        share[goal, : 2 * FF_Z] = outer_rows(rows[:, goal], both_grad[...]).astype(jnp.bfloat16)
        share[goal, 2 * FF_Z :] = outer_rows(incoming[:, goal], inner[...]).astype(jnp.bfloat16)
        share.send(goal)


def weighed(*pairs):
    return functools.reduce(
        jnp.add,
        [
            jnp.sum(grad[...] * weight[...].astype(jnp.float32), axis=1, keepdims=True)
            for grad, weight in pairs
        ],
    )


def as_row(column):
    return jnp.broadcast_to(column, (OWN, HEAD)).T[0:1, :]


def last_mlp_kernel(mlp, w_gate, w_up, norm_post, gate, up, down_t, post_grad):
    for place in range(Z):
        part = mlp[place].astype(jnp.float32)
        columns = slice(place * FF_Z, (place + 1) * FF_Z)
        gate[:, columns] = part[:, :FF_Z]
        up[:, columns] = part[:, FF_Z : 2 * FF_Z]
        down_t[:, columns] = part[:, 2 * FF_Z :]
    for result in (gate, up, down_t):
        result.send()
    post_grad[...] = as_row(weighed((gate, w_gate), (up, w_up)) / norm_post[...])


def last_kernel(
    at, p0, p1, p2, p3, p4, p5, w_query, w_key, w_value, norm,
    query, key, value, output_t, norm_grad, query_gain, key_gain,
):
    z, x_hi = at[0], at[1]
    pieces = (p0, p1, p2, p3, p4, p5)
    each = HEAD // N_FSDP
    gain_total = jnp.zeros((8, HEAD), jnp.float32)
    for array, step, relative, color in PIECES:
        begin = step * OWN
        part = pieces[array][begin : begin + OWN, :].astype(jnp.float32)
        place, theirs = z ^ relative, x_hi ^ color
        head = 2 * place + theirs
        one = pl.ds(pl.multiple_of(head * HEAD, HEAD), HEAD)
        two = pl.ds(pl.multiple_of(head * 2 * HEAD, 2 * HEAD), 2 * HEAD)
        query[:, two] = part[:, : 2 * HEAD]
        key[:, one] = part[:, 2 * HEAD : 3 * HEAD]
        value[:, one] = part[:, 3 * HEAD : 4 * HEAD]
        for other in range(2):
            goal = (2 * place + (theirs ^ other)) * 2 * HEAD
            goal = pl.ds(pl.multiple_of(goal, 2 * HEAD), 2 * HEAD)
            first = UNIT + other * 2 * HEAD
            share = part[:, first : first + 2 * HEAD]
            output_t[:, goal] = share if color == 0 else output_t[:, goal] + share
        gain_total += part[0:8, 2 * UNIT :]
    for result in (query, key, value, output_t):
        result.send()
    query_gain[...] = gain_total[0:1, :each]
    key_gain[...] = gain_total[0:1, each : 2 * each]
    norm_grad[...] = as_row(weighed((query, w_query), (key, w_key), (value, w_value)) / norm[...])


def ready(*inputs):
    for _, copy in inputs:
        copy.wait()
    return [place for place, _ in inputs]


class Writing:
    def __init__(self, place, goal, semaphores):
        self.place, self.goal, self.semaphores, self.copies = place, goal, semaphores, []
        self.shape = place.shape

    def __getitem__(self, index):
        return self.place[index]

    def __setitem__(self, index, values):
        self.place[index] = values

    def send(self, rows=slice(None)):
        copy = pltpu.make_async_copy(self.place.at[rows], self.goal.at[rows], next(self.semaphores))
        copy.start()
        self.copies.append(copy)


def kernel_call(kernel, inputs, outs, scratch=(), flops=0, cuts=None, raw_outs=0, late=()):
    cuts = cuts or {}
    n_in, n_out, n_sent = len(inputs), len(outs), 24

    def shape(i):
        return (inputs[i].shape[0], cuts[i][1]) if i in cuts else inputs[i].shape

    copied = [i for i, x in enumerate(inputs) if x.ndim > 1]
    buffers = [pltpu.VMEM(shape(i), inputs[i].dtype) for i in copied]
    out_buffers = [pltpu.VMEM(size, dtype) for size, dtype in outs[raw_outs:]]

    def body(*refs):
        ins, results, rest = refs[:n_in], refs[n_in : n_in + n_out], refs[n_in + n_out :]
        places, rest = rest[: len(buffers)], rest[len(buffers) :]
        out_places, rest = rest[: len(out_buffers)], rest[len(out_buffers) :]
        (arrived, sent), rest = rest[:2], rest[2:]
        args, copies = list(ins), []
        for i, place in zip(copied, places):
            source = ins[i].at[:, pl.ds(*cuts[i])] if i in cuts else ins[i]
            copy = pltpu.make_async_copy(source, place, arrived.at[i])
            copies.append((i in late, copy))
            args[i] = (place, copy) if i in late else place
        for _, copy in copies:
            copy.start()
        for waits_later, copy in copies:
            if not waits_later:
                copy.wait()
        semaphores = iter([sent.at[i] for i in range(n_sent)])
        writes = [Writing(p, g, semaphores) for p, g in zip(out_places, results[raw_outs:])]
        kernel(*args, *results[:raw_outs], *writes, *rest)
        for write in writes:
            if not write.copies:
                write.send()
        for write in writes:
            for copy in write.copies:
                copy.wait()

    anywhere, scalars = pl.BlockSpec(memory_space=pltpu.HBM), pl.BlockSpec(memory_space=pltpu.SMEM)
    return pl.pallas_call(
        body,
        out_shape=[jax.ShapeDtypeStruct(shape, dtype) for shape, dtype in outs],
        in_specs=[anywhere if x.ndim > 1 else scalars for x in inputs],
        out_specs=[anywhere] * n_out,
        scratch_shapes=[
            *buffers,
            *out_buffers,
            pltpu.SemaphoreType.DMA((n_in,)),
            pltpu.SemaphoreType.DMA((n_sent,)),
            *(x if not isinstance(x, tuple) else pltpu.VMEM(*x) for x in scratch),
        ],
        compiler_params=pltpu.CompilerParams(vmem_limit_bytes=GRANT * MEGA),
        cost_estimate=pl.CostEstimate(flops=flops, bytes_accessed=8 * MEGA, transcendentals=0),
    )(*inputs)


def per_device(
    tokens,
    segments,
    norm_input,
    w_query,
    w_key,
    w_value,
    norm_query,
    norm_key,
    w_output,
    norm_post,
    w_gate,
    w_up,
    w_down,
    cotangent,
):
    bf16, f32 = jnp.bfloat16, jnp.float32
    s, f = lax.axis_index("seq"), lax.axis_index("fsdp")
    z, x_hi = s // 2, s % 2
    at = jnp.stack([z, x_hi, f // 4, (f // 2) % 2, f % 2]).astype(jnp.int32)
    sequence = tokens[0]
    table = rotation()
    ids = segments[0]
    first_key = jnp.sum((ids[None, :] < ids[:, None]).astype(jnp.int32), axis=1).reshape(1, LENGTH)

    other_rows = swap_x_hi(sequence)

    def spread(values):
        wide = jnp.tile(values, N_FSDP)
        owner = jnp.arange(wide.shape[0], dtype=jnp.int32) // values.shape[0]
        return jnp.where(owner == f, wide, jnp.zeros_like(wide))

    def my_columns(values, width):
        return lax.dynamic_slice_in_dim(values, s * width, width, 1)

    rest = jnp.zeros((UNIT - 2 * HEAD,), bf16)
    extra = jnp.concatenate(
        [spread(norm_input), spread(norm_post), spread(norm_query), spread(norm_key), rest]
    ).reshape(5, UNIT)
    extra = jnp.pad(extra, ((0, EXTRA - 5), (0, 0)))
    my_unit = jnp.concatenate(
        [my_columns(w_query, 2 * HEAD), my_columns(w_key, HEAD), my_columns(w_value, HEAD)], axis=1
    )
    piece = lax.optimization_barrier(jnp.concatenate([my_unit, extra], axis=0))
    pair = jnp.concatenate([piece, swap_core(piece)], axis=0)
    other_pair = jnp.concatenate([swap_x_lo(piece), swap_chip(piece)], axis=0)
    pair, other_pair = lax.optimization_barrier((pair, other_pair))
    pair_1, other_pair_1 = swap_y_a(pair), swap_y_b(other_pair)

    pair_2 = swap_y_b(jnp.concatenate([pair, pair_1], axis=0))
    other_pair_2 = swap_y_a(jnp.concatenate([other_pair, other_pair_1], axis=0))
    unit_pieces = (pair, pair_1, pair_2, other_pair, other_pair_1, other_pair_2)
    rows_1 = swap_z_a(sequence)
    rows_2 = swap_z_b(jnp.concatenate([sequence, rows_1], axis=0))
    token_pieces = (
        sequence,
        rows_1,
        rows_2,
        other_rows,
        swap_z_a(other_rows),
        swap_z_b(other_rows),
        swap_z_both(other_rows),
    )

    def slice_z(values):
        return lax.dynamic_slice_in_dim(values, z * FF_Z, FF_Z, 1)

    later = jnp.concatenate(
        [w_output.T, slice_z(w_gate), slice_z(w_up), slice_z(w_down.T)], axis=1
    )
    later = lax.all_gather(later, "fsdp", axis=0, tiled=True)

    turned, normed, raw, heads, mixed, log_total, gains, weight = kernel_call(
        front_kernel,
        (at, *unit_pieces, *token_pieces, table, first_key),
        (
            ((2, Z, ROWS, 2 * HEAD), bf16),
            ((LENGTH, D), bf16),
            ((LENGTH, 3 * HEAD), f32),
            ((LENGTH, UNIT), bf16),
            ((LENGTH, 2 * HEAD), bf16),
            ((8, LENGTH), f32),
            ((8, D), f32),
            ((D, UNIT), bf16),
        ),
        scratch=(((HEAD, LENGTH), bf16), pltpu.SemaphoreType.DMA((8,))),
        flops=4 * 10**9,
        raw_outs=1,
        late=range(7, 15),
    )

    mixed_tokens = lax.all_to_all(
        mixed.reshape(N_SEQ, ROWS, 2 * HEAD), "seq", split_axis=0, concat_axis=0, tiled=True
    )
    incoming = after(cotangent[0], mixed)
    cotangent_z = gather4(*halves(incoming), swap_z_a, swap_z_b)
    half_rows = ((ROWS // 2, D), bf16)
    hidden, upper, lower = kernel_call(
        out_kernel,
        (mixed_tokens, sequence, gains, later),
        (((ROWS, D), f32), half_rows, half_rows),
        scratch=(((ROWS, 2 * D), bf16),),
        flops=10**9,
        cuts={3: (0, 2 * D)},
    )
    upper, lower = after((upper, lower), cotangent_z)
    normed_post_z = gather4(upper, lower, swap_z_a, swap_z_b)
    sent = (((ROWS, D), bf16), ((ROWS, D), bf16), ((ROWS, D), f32), ((ROWS, D), f32))
    first_0, first_1, passed, own, mlp_share, down_0, down_1, down_passed, down_own = kernel_call(
        mlp_kernel,
        (*normed_post_z, *cotangent_z, later, later),
        (*sent, ((D, 3 * FF_Z), bf16), *sent),
        scratch=(
            ((Z * ROWS, D), bf16),
            ((Z * ROWS, D), bf16),
            ((Z * ROWS, 2 * FF_Z), bf16),
            ((Z * ROWS, FF_Z), bf16),
        ),
        flops=8 * 10**9,
        cuts={12: (2 * D, 2 * FF_Z), 13: (2 * D + 2 * FF_Z, FF_Z)},
        late=(6, 7, 8, 9, 10, 11, 13),
    )
    turned = after(turned, first_0).reshape(2, Z * ROWS, 2 * HEAD)
    mixed_mine, mixed_other = turned[0], swap_x_hi(turned[1])
    sums = scatter4(first_0, first_1, *halves(passed), swap_z_a, swap_z_b)
    (got_0, got_1, last_0, last_1), mixed_other = lax.optimization_barrier((sums, mixed_other))
    mlp_share = lax.psum_scatter(mlp_share, "fsdp", scatter_dimension=0, tiled=True)
    hidden_grad, upper, lower, mixed_grad = kernel_call(
        mid_kernel,
        (own, got_0, got_1, last_0, last_1, hidden, cotangent[0], gains, later),
        (((ROWS, D), f32), half_rows, half_rows, ((N_SEQ, ROWS, 2 * HEAD), bf16)),
        flops=10**9,
        cuts={8: (0, 2 * D)},
    )
    mixed_grad = lax.all_to_all(mixed_grad, "seq", split_axis=0, concat_axis=0, tiled=True)
    proj_grad_z = gather4(upper, lower, swap_z_a, swap_z_b)
    down_0, down_1 = after((down_0, down_1), proj_grad_z)
    down_got = swap_z_b(down_0), swap_z_a(down_1)

    share, share_sent, dx_0, dx_1, dx_passed, dx_own = kernel_call(
        back_kernel,
        (
            at, heads, mixed_grad.reshape(LENGTH, 2 * HEAD), first_key, log_total, raw, table, gains,
            weight, normed, mixed_mine, mixed_other, *proj_grad_z,
        ),
        (
            ((Z, 2, OWN, SHARE), bf16),
            ((Z, 2, OWN, SHARE), bf16),
            ((2 * ROWS, D), bf16),
            ((2 * ROWS, D), bf16),
            ((2 * ROWS, D), f32),
            ((2 * ROWS, D), f32),
        ),
        scratch=(
            ((LENGTH, UNIT), bf16),
            ((HEAD, LENGTH), bf16),
            ((LENGTH, HEAD), f32),
            ((LENGTH, HEAD), f32),
            ((LENGTH, 2 * HEAD), f32),
            ((8, HEAD), f32),
            ((Z * ROWS, D), bf16),
            ((Z * ROWS, UNIT), bf16),
            ((2, Z, 2, OWN, SHARE), bf16),
            ((LENGTH, UNIT), bf16),
            pltpu.SemaphoreType.DMA((8,)),
        ),
        flops=8 * 10**9,
        raw_outs=2,
        late=range(9, 18),
    )
    share, share_sent, dx_0, dx_1 = after((share, share_sent, dx_0, dx_1), down_got)
    share = share.reshape(D // 2, SHARE)
    other_share = swap_core(share_sent.reshape(D // 2, SHARE))

    def share_block(relative, color):
        begin = (2 * relative + color) * OWN
        mine, other = share[begin : begin + OWN], other_share[begin : begin + OWN]
        return mine.astype(f32) + other.astype(f32)

    def share_pair(one, two):
        return jnp.concatenate([share_block(*one), share_block(*two)], axis=0).astype(bf16)

    dx_got = swap_z_b(dx_0), swap_z_a(dx_1)
    share_got = (
        swap_y_b(share_pair((3, 0), (2, 0))),
        swap_y_a(share_pair((1, 1), (2, 1))),
    )

    def second(got, passed_0, passed_1, swap_a, swap_b):
        n = got[0].shape[0] // 2
        last_0 = swap_a((passed_0 + wide(got[0][n:])).astype(bf16))
        last_1 = swap_b((passed_1 + wide(got[1][n:])).astype(bf16))
        return *got, last_0, last_1

    share_parts = second(share_got, share_block(1, 0), share_block(3, 1), swap_y_a, swap_y_b)
    mlp_other = swap_x_hi(mlp_share)
    share_parts, dx_got, mlp_other = lax.optimization_barrier((share_parts, dx_got, mlp_other))
    mlp_pieces = gather_z((wide(mlp_share) + wide(mlp_other)).astype(bf16))
    share_0, share_1 = total4(share_block(0, 0), share_block(0, 1), *share_parts)
    share_0, share_1 = share_0.astype(bf16), share_1.astype(bf16)
    share_0, share_1 = lax.optimization_barrier((share_0, share_1))
    attn_share = (share_0.astype(f32) + swap_x_lo(share_1).astype(f32)).astype(bf16)
    other_attn = swap_x_hi(share_0).astype(f32) + swap_x_both(share_1).astype(f32)
    other_attn = other_attn.astype(bf16)
    dx_parts = second(dx_got, *halves(dx_passed), swap_z_a, swap_z_b)
    attn_share, other_attn, dx_parts = lax.optimization_barrier((attn_share, other_attn, dx_parts))
    normed_grad, other_grad = total4(*halves(dx_own), *dx_parts)
    other_grad = swap_x_hi(other_grad.astype(bf16))
    normed_grad = (normed_grad + other_grad.astype(f32)) * gains[0:1]
    widened = sequence.astype(f32)
    inverse = inverse_norm(widened)
    unit_input = widened * inverse
    tokens_grad = hidden_grad + inverse * (
        normed_grad - unit_input * jnp.mean(unit_input * normed_grad, axis=-1, keepdims=True)
    )

    last_pieces = gather4(attn_share, other_attn, swap_z_a, swap_z_b)
    down_got = after(down_got, other_grad)
    down_parts = second(down_got, *halves(down_passed), swap_z_a, swap_z_b)
    result = hidden + jnp.concatenate(total4(*halves(down_own), *down_parts), axis=0)
    result = result.astype(bf16)

    gate_total, up_total, down_total, post_gain = kernel_call(
        last_mlp_kernel,
        (mlp_pieces, w_gate, w_up, norm_post.astype(f32).reshape(OWN, 1)),
        (((OWN, FF), f32), ((OWN, FF), f32), ((OWN, FF), f32), ((1, OWN), f32)),
    )
    last_pieces = after(last_pieces, post_gain)
    query_total, key_total, value_total, output_total, input_gain, query_gain, key_gain = kernel_call(
        last_kernel,
        (
            at, *last_pieces, w_query, w_key, w_value, norm_input.astype(f32).reshape(OWN, 1),
        ),
        (
            ((OWN, 2 * D), f32),
            ((OWN, D), f32),
            ((OWN, D), f32),
            ((OWN, 2 * D), f32),
            ((1, OWN), f32),
            ((1, HEAD // N_FSDP), f32),
            ((1, HEAD // N_FSDP), f32),
        ),
    )
    return (
        result[None],
        tokens_grad[None],
        input_gain[0],
        query_total,
        key_total,
        value_total,
        query_gain[0],
        key_gain[0],
        output_total.T,
        post_gain[0],
        gate_total,
        up_total,
        down_total.T,
    )


def solution(mesh):
    rows, columns, tokens = P("fsdp", None), P(None, "fsdp"), P("fsdp", "seq", None)
    in_specs = (
        tokens, rows, P("fsdp"), rows, rows, rows, P("fsdp"), P("fsdp"), columns, P("fsdp"),
        rows, rows, columns, tokens,
    )
    out_specs = (
        tokens, tokens, P("fsdp"), rows, rows, rows, P("fsdp"), P("fsdp"), columns, P("fsdp"),
        rows, rows, columns,
    )
    return jax.shard_map(
        per_device, mesh=mesh, in_specs=in_specs, out_specs=out_specs, check_vma=False
    )
```

```python
import functools
import math

import jax
import jax.numpy as jnp
import numpy as np
from jax import lax
from jax.experimental import pallas as pl
from jax.experimental.pallas import tpu as pltpu
from jax.sharding import PartitionSpec as P

HEAD = 128
D = 1024
FF = 3072
LENGTH = 1024
ROWS = 128
N_SEQ = 8
N_FSDP = 16
Z = 4
OWN = D // N_FSDP
FF_Z = FF // Z
UNIT = 512
BLOCK = 256
EXTRA = 16
SHARE = 2 * UNIT + HEAD
MEGA = 1 << 20
GRANT = 52
COSTS = {
    "front_kernel": 10.6,
    "out_kernel": 5.0,
    "mlp_kernel": 12.0,
    "mid_kernel": 4.9,
    "back_kernel": 13.7,
    "last_mlp_kernel": 3.3,
    "last_kernel": 3.7,
}

TOKEN_PIECES = (
    (0, 0, 0, 0),
    (3, 0, 0, 1),
    (1, 0, 1, 0),
    (2, 0, 3, 0),
    (2, 1, 2, 0),
    (4, 0, 1, 1),
    (5, 0, 3, 1),
    (6, 0, 2, 1),
)

EPSILON = 1e-06
THETA = 1000000.0
NEGATIVE = -1e30
SCALE = 1.0 / math.sqrt(HEAD)

PIECES = (
    (0, 0, 0, 0),
    (1, 0, 1, 0),
    (2, 0, 3, 0),
    (2, 1, 2, 0),
    (3, 0, 0, 1),
    (4, 0, 3, 1),
    (5, 0, 1, 1),
    (5, 1, 2, 1),
)


def exchange(values, axis, bits):
    size = N_SEQ if axis == "seq" else N_FSDP
    return lax.ppermute(values, axis, [(i, i ^ bits) for i in range(size)])


swap_x_hi = functools.partial(exchange, axis="seq", bits=1)
swap_z_a = functools.partial(exchange, axis="seq", bits=2)
swap_z_b = functools.partial(exchange, axis="seq", bits=6)
swap_z_both = functools.partial(exchange, axis="seq", bits=4)
swap_core = functools.partial(exchange, axis="fsdp", bits=1)
swap_x_lo = functools.partial(exchange, axis="fsdp", bits=2)
swap_chip = functools.partial(exchange, axis="fsdp", bits=3)


def swap_x_both(values):
    places = [(i, j) for i in range(N_SEQ) for j in range(N_FSDP)]
    pairs = [(i * N_FSDP + j, (i ^ 1) * N_FSDP + (j ^ 2)) for i, j in places]
    return lax.ppermute(values, ("seq", "fsdp"), pairs)


swap_y_a = functools.partial(exchange, axis="fsdp", bits=4)
swap_y_b = functools.partial(exchange, axis="fsdp", bits=12)


def after(values, *others):
    return lax.optimization_barrier((values, *others))[0]


def gather4(zero, one, swap_a, swap_b):
    zero_1 = swap_a(zero)
    one_1 = swap_b(one)
    zero_2 = swap_b(jnp.concatenate([zero, zero_1], axis=0))
    one_2 = swap_a(jnp.concatenate([one, one_1], axis=0))
    return zero, zero_1, zero_2, one, one_1, one_2


def gather_z(values):
    groups = [[2 * z + x_hi for z in range(Z)] for x_hi in range(2)]
    return lax.all_gather(values, "seq", axis=0, tiled=False, axis_index_groups=groups)


def halves(rows):
    middle = rows.shape[0] // 2
    return rows[:middle], rows[middle:]


def scatter4(first_0, first_1, passed_0, passed_1, swap_a, swap_b, tie=None):
    got_0, got_1 = swap_b(first_0), swap_a(first_1)
    if tie is not None:
        got_0, got_1 = tie(got_0, got_1)
    n = got_0.shape[0] // 2
    last_0 = swap_a((passed_0 + got_0[n:].astype(jnp.float32)).astype(jnp.bfloat16))
    last_1 = swap_b((passed_1 + got_1[n:].astype(jnp.float32)).astype(jnp.bfloat16))
    return got_0[:n], got_1[:n], last_0, last_1


def total4(own_0, own_1, got_0, got_1, last_0, last_1):
    n = own_0.shape[0]
    mine_0 = own_0 + wide(got_0[:n]) + wide(last_0)
    mine_1 = own_1 + wide(got_1[:n]) + wide(last_1)
    return mine_0, mine_1


def wide(values):
    return values.astype(jnp.float32)


def rotation():
    frequency = THETA ** -(np.arange(0, HEAD, 2, dtype=np.float64) / HEAD)
    angles = np.arange(LENGTH, dtype=np.float64)[:, None] * frequency[None, :]
    return jnp.asarray(np.concatenate([np.cos(angles), np.sin(angles)], axis=1).astype(np.float32))


def turns(table):
    turned = pltpu.roll(table, HEAD // 2, 1)
    low = lax.broadcasted_iota(jnp.int32, table.shape, 1) < HEAD // 2
    return jnp.where(low, table, turned), jnp.where(low, -turned, table)


def contract(left, right):
    return lax.dot_general(
        left, right, (((1,), (1,)), ((), ())), preferred_element_type=jnp.float32
    )


def outer_rows(left, right):
    return lax.dot_general(
        left, right, (((0,), (0,)), ((), ())), preferred_element_type=jnp.float32
    )


def product(left, right):
    return jnp.dot(left, right, preferred_element_type=jnp.float32)


def inverse_norm(values):
    return lax.rsqrt(jnp.mean(values * values, axis=-1, keepdims=True) + EPSILON)


def allowed_scores(scores, first_key, begin):
    first = first_key[:, begin : begin + BLOCK]
    place = (BLOCK, BLOCK)
    key, query = lax.broadcasted_iota(jnp.int32, place, 0), lax.broadcasted_iota(jnp.int32, place, 1)
    diagonal = jnp.where((key <= query) & (key + begin >= first), scores[begin:], NEGATIVE)
    if begin == 0:
        return [(0, diagonal)]
    key = lax.broadcasted_iota(jnp.int32, (begin, BLOCK), 0)
    return [(0, jnp.where(key >= first, scores[:begin], NEGATIVE)), (begin, diagonal)]


def front_kernel(
    at, w0, w1, w2, w3, w4, w5, x0, x1, x2, x3, x4, x5, x6, table, first_key,
    turned, normed, raw, heads, mixed, log_total, gains, weight, value_t, arrived,
):
    z, x_hi, y, x_lo, core = at[0], at[1], at[2], at[3], at[4]
    weights = (w0, w1, w2, w3, w4, w5)
    extra = jnp.zeros((EXTRA, UNIT), jnp.float32)
    for array, step, relative, color in PIECES:
        for other in range(2):
            first = (2 * step + other) * (OWN + EXTRA)
            owner = 4 * (y ^ relative) + 2 * (x_lo ^ color) + (core ^ other)
            weight[pl.ds(pl.multiple_of(owner * OWN, OWN), OWN), :] = weights[array][
                first : first + OWN, :
            ]
            extra += weights[array][first + OWN : first + OWN + EXTRA, :].astype(jnp.float32)
    gain = jnp.concatenate([extra[0:1], extra[1:2]], axis=1)
    gains[...] = jnp.zeros(gains.shape, jnp.float32)
    gains[0:1, :] = gain
    gains[1:2, :] = jnp.concatenate([extra[2:3], extra[3:4]], axis=1)
    gains[2:3, 0:UNIT] = extra[4:5]
    table, *tokens = ready(table, x0, x1, x2, x3, x4, x5, x6)
    for array, step, relative, color in TOKEN_PIECES:
        values = tokens[array][step * ROWS : (step + 1) * ROWS, :].astype(jnp.float32)
        place = (2 * (z ^ relative) + (x_hi ^ color)) * ROWS
        normed[pl.ds(pl.multiple_of(place, ROWS), ROWS), :] = (
            values * inverse_norm(values) * gain
        ).astype(jnp.bfloat16)
    normed.send()
    weight.send()
    gain_query, gain_key = extra[4:5, :HEAD], extra[4:5, HEAD : 2 * HEAD]
    for begin in range(0, LENGTH, BLOCK):
        rows = slice(begin, begin + BLOCK)
        projected = product(normed[rows, :], weight[...])
        cosine, sine = turns(table[rows, :])
        raw[rows, :] = projected[:, : 3 * HEAD]
        for head, head_gain in enumerate((gain_query, gain_query, gain_key)):
            part = projected[:, head * HEAD : (head + 1) * HEAD]
            part = part * inverse_norm(part) * head_gain
            part = part * cosine + pltpu.roll(part, HEAD // 2, 1) * sine
            heads[rows, head * HEAD : (head + 1) * HEAD] = part.astype(jnp.bfloat16)
        value = projected[:, 3 * HEAD :]
        heads[rows, 3 * HEAD :] = value.astype(jnp.bfloat16)
        value_t[:, rows] = value.T.astype(jnp.bfloat16)
    raw.send()
    heads.send()
    key = slice(2 * HEAD, 3 * HEAD)
    for begin in range(0, LENGTH, BLOCK):
        rows, end = slice(begin, begin + BLOCK), begin + BLOCK
        for head in range(2):
            columns = slice(head * HEAD, (head + 1) * HEAD)
            scores = contract(heads[:end, key], heads[rows, columns]) * SCALE
            parts = allowed_scores(scores, first_key, begin)
            highest = functools.reduce(
                jnp.maximum, [jnp.max(s, axis=0, keepdims=True) for _, s in parts]
            )
            total, result = 0.0, 0.0
            for first, s in parts:
                weights_now = jnp.exp(s - highest)
                total += jnp.sum(weights_now, axis=0, keepdims=True)
                result += product(
                    value_t[:, first : first + s.shape[0]], weights_now.astype(jnp.bfloat16)
                )
            log_total[head : head + 1, rows] = highest + jnp.log(total)
            mixed[rows, columns] = (result / total).T.astype(jnp.bfloat16)
        mixed.send(rows)
        for part in range(2):
            i = begin // ROWS + part
            goal = turned.at[part ^ x_hi, (begin // BLOCK) ^ z]
            copy = pltpu.make_async_copy(
                mixed.place.at[i * ROWS : (i + 1) * ROWS], goal, arrived.at[i]
            )
            copy.start()
            mixed.copies.append(copy)


def back_kernel(
    at, heads, grad, first_key, log_total, raw, table, gains, weight,
    normed, mixed_mine, mixed_other, p0, p1, p2, p3, p4, p5,
    mine, theirs, first_0, first_1, passed, own, back, key_t, key_sum, value_sum, query_sum,
    gain_grads, proj, mixed, share, turned, done,
):
    key, value = slice(2 * HEAD, 3 * HEAD), slice(3 * HEAD, 4 * HEAD)
    key_t[...] = heads[:, key].astype(jnp.float32).T.astype(jnp.bfloat16)
    key_sum[...] = jnp.zeros_like(key_sum)
    value_sum[...] = jnp.zeros_like(value_sum)
    for start in range(0, LENGTH, BLOCK):
        rows, end = slice(start, start + BLOCK), start + BLOCK
        for head in range(2):
            columns = slice(head * HEAD, (head + 1) * HEAD)
            query, rows_grad = heads[rows, columns], grad[rows, columns]
            scores = contract(heads[:end, key], query) * SCALE
            prob_grad = contract(heads[:end, value], rows_grad)
            log_now = log_total[head : head + 1, rows]
            parts, mean = [], 0.0
            for first, s in allowed_scores(scores, first_key, start):
                prob = jnp.exp(s - log_now)
                pulled = prob_grad[first : first + s.shape[0]]
                mean += jnp.sum(prob * pulled, axis=0, keepdims=True)
                parts.append((first, prob, pulled))
            query_part = 0.0
            for first, prob, pulled in parts:
                keys = slice(first, first + prob.shape[0])
                score_grad = (prob * (pulled - mean)).astype(jnp.bfloat16)
                value_sum[keys, :] += product(prob.astype(jnp.bfloat16), rows_grad)
                key_sum[keys, :] += product(score_grad, query)
                query_part += product(key_t[:, keys], score_grad)
            query_sum[rows, columns] = query_part.T
    back[:, value] = value_sum[...].astype(jnp.bfloat16)
    gain_grads[...] = jnp.zeros(gain_grads.shape, jnp.float32)
    for head in range(3):
        columns = slice(head * HEAD, (head + 1) * HEAD)
        which = 0 if head < 2 else 1
        gain = gains[2:3, which * HEAD : (which + 1) * HEAD]
        for start in range(0, LENGTH, BLOCK):
            rows = slice(start, start + BLOCK)
            cosine, sine = turns(table[rows, :])
            pulled = (query_sum[rows, columns] if head < 2 else key_sum[rows, :]) * SCALE
            pulled = pulled.astype(jnp.bfloat16).astype(jnp.float32)
            pulled = pulled * cosine - pltpu.roll(pulled, HEAD // 2, 1) * sine
            part = raw[rows, columns]
            inverse = inverse_norm(part)
            unit = part * inverse
            gain_grads[which : which + 1, :] += jnp.sum(pulled * unit, axis=0, keepdims=True)
            pulled = pulled * gain
            mean = jnp.mean(unit * pulled, axis=-1, keepdims=True)
            back[rows, columns] = (inverse * (pulled - unit * mean)).astype(jnp.bfloat16)

    z, x_hi = at[0], at[1]
    for relative in range(Z):
        for color in range(2):
            place = (2 * (z ^ relative) + (x_hi ^ color)) * ROWS
            goal = (2 * relative + color) * ROWS
            turned[goal : goal + ROWS, :] = back[pl.ds(pl.multiple_of(place, ROWS), ROWS), :]
    send_order(contract(turned[...], weight[...]), first_0, first_1, passed, own)
    for values in (first_0, first_1, passed, own):
        values.send()
    y, x_lo, core = at[2], at[3], at[4]
    normed, mixed_mine, mixed_other, *pieces = ready(
        normed, mixed_mine, mixed_other, p0, p1, p2, p3, p4, p5
    )
    ordered(pieces, proj)
    mixed[:, : 2 * HEAD] = mixed_mine[...]
    mixed[:, 2 * HEAD :] = mixed_other[...]
    lane = lax.broadcasted_iota(jnp.int32, (OWN, HEAD), 1)
    line = lax.broadcasted_iota(jnp.int32, (OWN, HEAD), 0)
    each = HEAD // N_FSDP
    copies = []
    for start in range(0, D, BLOCK):
        goal = slice(start, start + BLOCK)
        attn = outer_rows(normed[:, goal], back[...]).astype(jnp.bfloat16)
        output = outer_rows(proj[:, goal], mixed[...]).astype(jnp.bfloat16)
        for part in range(BLOCK // OWN):
            owner = start // OWN + part
            query_gain = pltpu.roll(gain_grads[0:1, :], (HEAD - each * owner) % HEAD, 1)
            key_gain = pltpu.roll(gain_grads[1:2, :], (HEAD + each - each * owner) % HEAD, 1)
            head_gains = jnp.where(lane < each, query_gain, key_gain)
            head_gains = jnp.where((line == 0) & (lane < 2 * each), head_gains, 0.0)
            rows = slice(part * OWN, (part + 1) * OWN)
            place = ((owner % 2) ^ core, (owner // 4) ^ y, ((owner // 2) % 2) ^ x_lo)
            share[(*place, slice(None), slice(0, UNIT))] = attn[rows]
            share[(*place, slice(None), slice(UNIT, 2 * UNIT))] = output[rows]
            share[(*place, slice(None), slice(2 * UNIT, SHARE))] = head_gains.astype(jnp.bfloat16)
        which = (start // BLOCK) ^ y
        for i, goal in ((1, theirs), (0, mine)):
            copy = pltpu.make_async_copy(
                share.at[i, which], goal.at[which], done.at[2 * (start // BLOCK) + i]
            )
            copy.start()
            copies.append(copy)
    for copy in copies:
        copy.wait()


def out_kernel(mixed, tokens, gains, weights, hidden, upper, lower, rows):
    for head in range(N_SEQ):
        rows[:, head * 2 * HEAD : (head + 1) * 2 * HEAD] = mixed[head]
    values = tokens[...].astype(jnp.float32) + contract(rows[...], weights[...])
    hidden[...] = values
    values = (values * inverse_norm(values) * gains[1:2, :]).astype(jnp.bfloat16)
    upper[...] = values[: ROWS // 2]
    lower[...] = values[ROWS // 2 :]


def mid_kernel(
    own, got_0, got_1, last_0, last_1, hidden, incoming, gains, weights,
    hidden_grad, upper, lower, mixed_grad,
):
    half = ROWS // 2
    total_0 = own[:half, :] + got_0[...].astype(jnp.float32) + last_0[...].astype(jnp.float32)
    total_1 = own[half:, :] + got_1[...].astype(jnp.float32) + last_1[...].astype(jnp.float32)
    pulled = jnp.concatenate([total_0, total_1], axis=0) * gains[1:2, :]
    inverse = inverse_norm(hidden[...])
    unit = hidden[...] * inverse
    mean = jnp.mean(unit * pulled, axis=-1, keepdims=True)
    grad = incoming[...].astype(jnp.float32) + inverse * (pulled - unit * mean)
    hidden_grad[...] = grad
    grad = grad.astype(jnp.bfloat16)
    upper[...] = grad[:half]
    lower[...] = grad[half:]
    for head in range(N_SEQ):
        mixed_grad[head] = product(grad, weights[:, head * 2 * HEAD : (head + 1) * 2 * HEAD]).astype(jnp.bfloat16)


def ordered(pieces, place):
    half = pieces[0].shape[0]
    for array, step, relative, color in PIECES:
        begin = (2 * relative + color) * half
        place[begin : begin + half, :] = pieces[array][step * half : (step + 1) * half, :]


def send_order(values, first_0, first_1, passed, own):
    half = values.shape[0] // 8

    def block(relative, color):
        begin = (2 * relative + color) * half
        return values[begin : begin + half]

    first_0[:half, :] = block(3, 0).astype(jnp.bfloat16)
    first_0[half:, :] = block(2, 0).astype(jnp.bfloat16)
    first_1[:half, :] = block(1, 1).astype(jnp.bfloat16)
    first_1[half:, :] = block(2, 1).astype(jnp.bfloat16)
    passed[:half, :] = block(1, 0)
    passed[half:, :] = block(3, 1)
    own[:half, :] = block(0, 0)
    own[half:, :] = block(0, 1)


def mlp_kernel(
    n0, n1, n2, n3, n4, n5, c0, c1, c2, c3, c4, c5, weights, down_weights,
    first_0, first_1, passed, own, share, down_0, down_1, down_passed, down_own,
    rows, incoming, both_grad, inner,
):
    ordered((n0, n1, n2, n3, n4, n5), rows)
    for first in range(0, FF_Z, BLOCK):
        columns, second = slice(first, first + BLOCK), slice(FF_Z + first, FF_Z + first + BLOCK)
        gate = product(rows[...], weights[:, columns])
        up = product(rows[...], weights[:, second])
        if first == 0:
            down_weights, *pieces = ready(down_weights, c0, c1, c2, c3, c4, c5)
            ordered(pieces, incoming)
        inner_grad = product(incoming[...], down_weights[:, columns])
        sigmoid = jax.nn.sigmoid(gate)
        swish = gate * sigmoid
        inner[:, columns] = (swish * up).astype(jnp.bfloat16)
        both_grad[:, columns] = (
            inner_grad * up * sigmoid * (1.0 + gate * (1.0 - sigmoid))
        ).astype(jnp.bfloat16)
        both_grad[:, second] = (inner_grad * swish).astype(jnp.bfloat16)
    send_order(contract(both_grad[...], weights[...]), first_0, first_1, passed, own)
    for values in (first_0, first_1, passed, own):
        values.send()
    send_order(
        contract(inner[...], down_weights[...]), down_0, down_1, down_passed, down_own
    )
    for values in (down_0, down_1, down_passed, down_own):
        values.send()
    for first in range(0, D, BLOCK):
        goal = slice(first, first + BLOCK)
        share[goal, : 2 * FF_Z] = outer_rows(rows[:, goal], both_grad[...]).astype(jnp.bfloat16)
        share[goal, 2 * FF_Z :] = outer_rows(incoming[:, goal], inner[...]).astype(jnp.bfloat16)
        share.send(goal)


def weighed(*pairs):
    return functools.reduce(
        jnp.add,
        [
            jnp.sum(grad[...] * weight[...].astype(jnp.float32), axis=1, keepdims=True)
            for grad, weight in pairs
        ],
    )


def as_row(column):
    return jnp.broadcast_to(column, (OWN, HEAD)).T[0:1, :]


def last_mlp_kernel(mlp, w_gate, w_up, norm_post, gate, up, down_t, post_grad):
    for place in range(Z):
        part = mlp[place].astype(jnp.float32)
        columns = slice(place * FF_Z, (place + 1) * FF_Z)
        gate[:, columns] = part[:, :FF_Z]
        up[:, columns] = part[:, FF_Z : 2 * FF_Z]
        down_t[:, columns] = part[:, 2 * FF_Z :]
    for result in (gate, up, down_t):
        result.send()
    post_grad[...] = as_row(weighed((gate, w_gate), (up, w_up)) / norm_post[...])


def last_kernel(
    at, p0, p1, p2, p3, p4, p5, w_query, w_key, w_value, norm,
    query, key, value, output_t, norm_grad, query_gain, key_gain,
):
    z, x_hi = at[0], at[1]
    pieces = (p0, p1, p2, p3, p4, p5)
    each = HEAD // N_FSDP
    gain_total = jnp.zeros((8, HEAD), jnp.float32)
    for array, step, relative, color in PIECES:
        begin = step * OWN
        part = pieces[array][begin : begin + OWN, :].astype(jnp.float32)
        place, theirs = z ^ relative, x_hi ^ color
        head = 2 * place + theirs
        one = pl.ds(pl.multiple_of(head * HEAD, HEAD), HEAD)
        two = pl.ds(pl.multiple_of(head * 2 * HEAD, 2 * HEAD), 2 * HEAD)
        query[:, two] = part[:, : 2 * HEAD]
        key[:, one] = part[:, 2 * HEAD : 3 * HEAD]
        value[:, one] = part[:, 3 * HEAD : 4 * HEAD]
        for other in range(2):
            goal = (2 * place + (theirs ^ other)) * 2 * HEAD
            goal = pl.ds(pl.multiple_of(goal, 2 * HEAD), 2 * HEAD)
            first = UNIT + other * 2 * HEAD
            share = part[:, first : first + 2 * HEAD]
            output_t[:, goal] = share if color == 0 else output_t[:, goal] + share
        gain_total += part[0:8, 2 * UNIT :]
    for result in (query, key, value, output_t):
        result.send()
    query_gain[...] = gain_total[0:1, :each]
    key_gain[...] = gain_total[0:1, each : 2 * each]
    norm_grad[...] = as_row(weighed((query, w_query), (key, w_key), (value, w_value)) / norm[...])


def ready(*inputs):
    for _, copy in inputs:
        copy.wait()
    return [place for place, _ in inputs]


class Writing:
    def __init__(self, place, goal, semaphores):
        self.place, self.goal, self.semaphores, self.copies = place, goal, semaphores, []
        self.shape = place.shape

    def __getitem__(self, index):
        return self.place[index]

    def __setitem__(self, index, values):
        self.place[index] = values

    def send(self, rows=slice(None)):
        copy = pltpu.make_async_copy(self.place.at[rows], self.goal.at[rows], next(self.semaphores))
        copy.start()
        self.copies.append(copy)


def kernel_call(kernel, inputs, outs, scratch=(), flops=0, cuts=None, raw_outs=0, late=()):
    cuts = cuts or {}
    n_in, n_out, n_sent = len(inputs), len(outs), 24

    def shape(i):
        return (inputs[i].shape[0], cuts[i][1]) if i in cuts else inputs[i].shape

    copied = [i for i, x in enumerate(inputs) if x.ndim > 1]
    buffers = [pltpu.VMEM(shape(i), inputs[i].dtype) for i in copied]
    out_buffers = [pltpu.VMEM(size, dtype) for size, dtype in outs[raw_outs:]]

    def body(*refs):
        ins, results, rest = refs[:n_in], refs[n_in : n_in + n_out], refs[n_in + n_out :]
        places, rest = rest[: len(buffers)], rest[len(buffers) :]
        out_places, rest = rest[: len(out_buffers)], rest[len(out_buffers) :]
        (arrived, sent), rest = rest[:2], rest[2:]
        args, copies = list(ins), []
        for i, place in zip(copied, places):
            source = ins[i].at[:, pl.ds(*cuts[i])] if i in cuts else ins[i]
            copy = pltpu.make_async_copy(source, place, arrived.at[i])
            copies.append((i in late, copy))
            args[i] = (place, copy) if i in late else place
        for _, copy in copies:
            copy.start()
        for waits_later, copy in copies:
            if not waits_later:
                copy.wait()
        semaphores = iter([sent.at[i] for i in range(n_sent)])
        writes = [Writing(p, g, semaphores) for p, g in zip(out_places, results[raw_outs:])]
        kernel(*args, *results[:raw_outs], *writes, *rest)
        for write in writes:
            if not write.copies:
                write.send()
        for write in writes:
            for copy in write.copies:
                copy.wait()

    anywhere, scalars = pl.BlockSpec(memory_space=pltpu.HBM), pl.BlockSpec(memory_space=pltpu.SMEM)
    return pl.pallas_call(
        body,
        out_shape=[jax.ShapeDtypeStruct(shape, dtype) for shape, dtype in outs],
        in_specs=[anywhere if x.ndim > 1 else scalars for x in inputs],
        out_specs=[anywhere] * n_out,
        scratch_shapes=[
            *buffers,
            *out_buffers,
            pltpu.SemaphoreType.DMA((n_in,)),
            pltpu.SemaphoreType.DMA((n_sent,)),
            *(x if not isinstance(x, tuple) else pltpu.VMEM(*x) for x in scratch),
        ],
        compiler_params=pltpu.CompilerParams(vmem_limit_bytes=GRANT * MEGA),
        cost_estimate=pl.CostEstimate(
            flops=int(COSTS[kernel.__name__] * 1.15e9), bytes_accessed=MEGA, transcendentals=0
        ),
    )(*inputs)


def per_device(
    tokens,
    segments,
    norm_input,
    w_query,
    w_key,
    w_value,
    norm_query,
    norm_key,
    w_output,
    norm_post,
    w_gate,
    w_up,
    w_down,
    cotangent,
):
    bf16, f32 = jnp.bfloat16, jnp.float32
    s, f = lax.axis_index("seq"), lax.axis_index("fsdp")
    z, x_hi = s // 2, s % 2
    at = jnp.stack([z, x_hi, f // 4, (f // 2) % 2, f % 2]).astype(jnp.int32)
    sequence = tokens[0]
    table = rotation()
    ids = segments[0]
    first_key = jnp.sum((ids[None, :] < ids[:, None]).astype(jnp.int32), axis=1).reshape(1, LENGTH)

    other_rows = swap_x_hi(sequence)

    def spread(values):
        wide = jnp.tile(values, N_FSDP)
        owner = jnp.arange(wide.shape[0], dtype=jnp.int32) // values.shape[0]
        return jnp.where(owner == f, wide, jnp.zeros_like(wide))

    def my_columns(values, width):
        return lax.dynamic_slice_in_dim(values, s * width, width, 1)

    rest = jnp.zeros((UNIT - 2 * HEAD,), bf16)
    extra = jnp.concatenate(
        [spread(norm_input), spread(norm_post), spread(norm_query), spread(norm_key), rest]
    ).reshape(5, UNIT)
    extra = jnp.pad(extra, ((0, EXTRA - 5), (0, 0)))
    my_unit = jnp.concatenate(
        [my_columns(w_query, 2 * HEAD), my_columns(w_key, HEAD), my_columns(w_value, HEAD)], axis=1
    )
    piece = lax.optimization_barrier(jnp.concatenate([my_unit, extra], axis=0))
    pair = jnp.concatenate([piece, swap_core(piece)], axis=0)
    other_pair = jnp.concatenate([swap_x_lo(piece), swap_chip(piece)], axis=0)
    pair, other_pair = lax.optimization_barrier((pair, other_pair))
    pair_1, other_pair_1 = swap_y_a(pair), swap_y_b(other_pair)

    pair_2 = swap_y_b(jnp.concatenate([pair, pair_1], axis=0))
    other_pair_2 = swap_y_a(jnp.concatenate([other_pair, other_pair_1], axis=0))
    unit_pieces = (pair, pair_1, pair_2, other_pair, other_pair_1, other_pair_2)
    rows_1 = swap_z_a(sequence)
    rows_2 = swap_z_b(jnp.concatenate([sequence, rows_1], axis=0))
    token_pieces = (
        sequence,
        rows_1,
        rows_2,
        other_rows,
        swap_z_a(other_rows),
        swap_z_b(other_rows),
        swap_z_both(other_rows),
    )

    def slice_z(values):
        return lax.dynamic_slice_in_dim(values, z * FF_Z, FF_Z, 1)

    later = jnp.concatenate(
        [w_output.T, slice_z(w_gate), slice_z(w_up), slice_z(w_down.T)], axis=1
    )
    later = lax.all_gather(later, "fsdp", axis=0, tiled=True)

    turned, normed, raw, heads, mixed, log_total, gains, weight = kernel_call(
        front_kernel,
        (at, *unit_pieces, *token_pieces, table, first_key),
        (
            ((2, Z, ROWS, 2 * HEAD), bf16),
            ((LENGTH, D), bf16),
            ((LENGTH, 3 * HEAD), f32),
            ((LENGTH, UNIT), bf16),
            ((LENGTH, 2 * HEAD), bf16),
            ((8, LENGTH), f32),
            ((8, D), f32),
            ((D, UNIT), bf16),
        ),
        scratch=(((HEAD, LENGTH), bf16), pltpu.SemaphoreType.DMA((8,))),
        flops=4 * 10**9,
        raw_outs=1,
        late=range(7, 15),
    )

    mixed_tokens = lax.all_to_all(
        mixed.reshape(N_SEQ, ROWS, 2 * HEAD), "seq", split_axis=0, concat_axis=0, tiled=True
    )
    incoming = after(cotangent[0], mixed)
    cotangent_z = gather4(*halves(incoming), swap_z_a, swap_z_b)
    half_rows = ((ROWS // 2, D), bf16)
    hidden, upper, lower = kernel_call(
        out_kernel,
        (mixed_tokens, sequence, gains, later),
        (((ROWS, D), f32), half_rows, half_rows),
        scratch=(((ROWS, 2 * D), bf16),),
        flops=10**9,
        cuts={3: (0, 2 * D)},
    )
    upper, lower = after((upper, lower), cotangent_z)
    normed_post_z = gather4(upper, lower, swap_z_a, swap_z_b)
    sent = (((ROWS, D), bf16), ((ROWS, D), bf16), ((ROWS, D), f32), ((ROWS, D), f32))
    first_0, first_1, passed, own, mlp_share, down_0, down_1, down_passed, down_own = kernel_call(
        mlp_kernel,
        (*normed_post_z, *cotangent_z, later, later),
        (*sent, ((D, 3 * FF_Z), bf16), *sent),
        scratch=(
            ((Z * ROWS, D), bf16),
            ((Z * ROWS, D), bf16),
            ((Z * ROWS, 2 * FF_Z), bf16),
            ((Z * ROWS, FF_Z), bf16),
        ),
        flops=8 * 10**9,
        cuts={12: (2 * D, 2 * FF_Z), 13: (2 * D + 2 * FF_Z, FF_Z)},
        late=(6, 7, 8, 9, 10, 11, 13),
    )
    turned = after(turned, first_0).reshape(2, Z * ROWS, 2 * HEAD)
    mixed_mine, mixed_other = turned[0], swap_x_hi(turned[1])
    sums = scatter4(first_0, first_1, *halves(passed), swap_z_a, swap_z_b)
    (got_0, got_1, last_0, last_1), mixed_other = lax.optimization_barrier((sums, mixed_other))
    mlp_share = lax.psum_scatter(mlp_share, "fsdp", scatter_dimension=0, tiled=True)
    hidden_grad, upper, lower, mixed_grad = kernel_call(
        mid_kernel,
        (own, got_0, got_1, last_0, last_1, hidden, cotangent[0], gains, later),
        (((ROWS, D), f32), half_rows, half_rows, ((N_SEQ, ROWS, 2 * HEAD), bf16)),
        flops=10**9,
        cuts={8: (0, 2 * D)},
    )
    mixed_grad = lax.all_to_all(mixed_grad, "seq", split_axis=0, concat_axis=0, tiled=True)
    proj_grad_z = gather4(upper, lower, swap_z_a, swap_z_b)
    down_0, down_1 = after((down_0, down_1), proj_grad_z)
    down_got = swap_z_b(down_0), swap_z_a(down_1)

    share, share_sent, dx_0, dx_1, dx_passed, dx_own = kernel_call(
        back_kernel,
        (
            at, heads, mixed_grad.reshape(LENGTH, 2 * HEAD), first_key, log_total, raw, table, gains,
            weight, normed, mixed_mine, mixed_other, *proj_grad_z,
        ),
        (
            ((Z, 2, OWN, SHARE), bf16),
            ((Z, 2, OWN, SHARE), bf16),
            ((2 * ROWS, D), bf16),
            ((2 * ROWS, D), bf16),
            ((2 * ROWS, D), f32),
            ((2 * ROWS, D), f32),
        ),
        scratch=(
            ((LENGTH, UNIT), bf16),
            ((HEAD, LENGTH), bf16),
            ((LENGTH, HEAD), f32),
            ((LENGTH, HEAD), f32),
            ((LENGTH, 2 * HEAD), f32),
            ((8, HEAD), f32),
            ((Z * ROWS, D), bf16),
            ((Z * ROWS, UNIT), bf16),
            ((2, Z, 2, OWN, SHARE), bf16),
            ((LENGTH, UNIT), bf16),
            pltpu.SemaphoreType.DMA((8,)),
        ),
        flops=8 * 10**9,
        raw_outs=2,
        late=range(9, 18),
    )
    share, share_sent, dx_0, dx_1 = after((share, share_sent, dx_0, dx_1), down_got)
    share = share.reshape(D // 2, SHARE)
    other_share = swap_core(share_sent.reshape(D // 2, SHARE))

    def share_block(relative, color):
        begin = (2 * relative + color) * OWN
        mine, other = share[begin : begin + OWN], other_share[begin : begin + OWN]
        return mine.astype(f32) + other.astype(f32)

    def share_pair(one, two):
        return jnp.concatenate([share_block(*one), share_block(*two)], axis=0).astype(bf16)

    dx_got = swap_z_b(dx_0), swap_z_a(dx_1)
    share_got = (
        swap_y_b(share_pair((3, 0), (2, 0))),
        swap_y_a(share_pair((1, 1), (2, 1))),
    )

    def second(got, passed_0, passed_1, swap_a, swap_b):
        n = got[0].shape[0] // 2
        last_0 = swap_a((passed_0 + wide(got[0][n:])).astype(bf16))
        last_1 = swap_b((passed_1 + wide(got[1][n:])).astype(bf16))
        return *got, last_0, last_1

    share_parts = second(share_got, share_block(1, 0), share_block(3, 1), swap_y_a, swap_y_b)
    mlp_other = swap_x_hi(mlp_share)
    share_parts, dx_got, mlp_other = lax.optimization_barrier((share_parts, dx_got, mlp_other))
    mlp_pieces = gather_z((wide(mlp_share) + wide(mlp_other)).astype(bf16))
    share_0, share_1 = total4(share_block(0, 0), share_block(0, 1), *share_parts)
    share_0, share_1 = share_0.astype(bf16), share_1.astype(bf16)
    share_0, share_1 = lax.optimization_barrier((share_0, share_1))
    attn_share = (share_0.astype(f32) + swap_x_lo(share_1).astype(f32)).astype(bf16)
    other_attn = swap_x_hi(share_0).astype(f32) + swap_x_both(share_1).astype(f32)
    other_attn = other_attn.astype(bf16)
    dx_parts = second(dx_got, *halves(dx_passed), swap_z_a, swap_z_b)
    attn_share, other_attn, dx_parts = lax.optimization_barrier((attn_share, other_attn, dx_parts))
    normed_grad, other_grad = total4(*halves(dx_own), *dx_parts)
    other_grad = swap_x_hi(other_grad.astype(bf16))
    normed_grad = (normed_grad + other_grad.astype(f32)) * gains[0:1]
    widened = sequence.astype(f32)
    inverse = inverse_norm(widened)
    unit_input = widened * inverse
    tokens_grad = hidden_grad + inverse * (
        normed_grad - unit_input * jnp.mean(unit_input * normed_grad, axis=-1, keepdims=True)
    )

    last_pieces = gather4(attn_share, other_attn, swap_z_a, swap_z_b)
    down_got = after(down_got, other_grad)
    down_parts = second(down_got, *halves(down_passed), swap_z_a, swap_z_b)
    result = hidden + jnp.concatenate(total4(*halves(down_own), *down_parts), axis=0)
    result = result.astype(bf16)

    gate_total, up_total, down_total, post_gain = kernel_call(
        last_mlp_kernel,
        (mlp_pieces, w_gate, w_up, norm_post.astype(f32).reshape(OWN, 1)),
        (((OWN, FF), f32), ((OWN, FF), f32), ((OWN, FF), f32), ((1, OWN), f32)),
    )
    last_pieces = after(last_pieces, post_gain)
    query_total, key_total, value_total, output_total, input_gain, query_gain, key_gain = kernel_call(
        last_kernel,
        (
            at, *last_pieces, w_query, w_key, w_value, norm_input.astype(f32).reshape(OWN, 1),
        ),
        (
            ((OWN, 2 * D), f32),
            ((OWN, D), f32),
            ((OWN, D), f32),
            ((OWN, 2 * D), f32),
            ((1, OWN), f32),
            ((1, HEAD // N_FSDP), f32),
            ((1, HEAD // N_FSDP), f32),
        ),
    )
    return (
        result[None],
        tokens_grad[None],
        input_gain[0],
        query_total,
        key_total,
        value_total,
        query_gain[0],
        key_gain[0],
        output_total.T,
        post_gain[0],
        gate_total,
        up_total,
        down_total.T,
    )


def solution(mesh):
    rows, columns, tokens = P("fsdp", None), P(None, "fsdp"), P("fsdp", "seq", None)
    in_specs = (
        tokens, rows, P("fsdp"), rows, rows, rows, P("fsdp"), P("fsdp"), columns, P("fsdp"),
        rows, rows, columns, tokens,
    )
    out_specs = (
        tokens, tokens, P("fsdp"), rows, rows, rows, P("fsdp"), P("fsdp"), columns, P("fsdp"),
        rows, rows, columns,
    )
    return jax.shard_map(
        per_device, mesh=mesh, in_specs=in_specs, out_specs=out_specs, check_vma=False
    )
```
